32 devices in a mesh: dp: 8 (over z, x), tensor: 4 (over y, core).
Axes of the slice: x: 2, y: 2, z: 4, core: 2. Of those that a mesh axis runs over, the one named last changes fastest.
Arguments:
- hidden_in: bfloat16 [512, 16, 768], P('tensor', 'dp'), may hold values from -2.5 to 2.5
- cotangent: bfloat16 [512, 16, 768], P('tensor', 'dp'), may hold values from -2.5 to 2.5
- doc_lengths: int32 [16, 5], P('dp'), may hold values from 1 to 385, 512 in all within a row
- pad_count: int32 [16], P('dp'), may hold values from 1 to 32
- input_weight: bfloat16 [2, 3, 768, 768], P(None, None, None, 'tensor'), may hold values from -0.21875 to 0.21875
- input_bias: bfloat16 [2, 2, 768], P(None, None, 'tensor'), may hold values from -1.5 to 1.5
- output_weight: bfloat16 [2, 768, 768], P(None, 'tensor'), may hold values from -0.875 to 0.875
- up_weight: bfloat16 [2, 768, 3072], P(None, None, 'tensor'), may hold values from -0.21875 to 0.21875
- up_bias: bfloat16 [2, 3072], P(None, 'tensor'), may hold values from -1.5 to 1.5
- down_weight: bfloat16 [2, 3072, 768], P(None, 'tensor'), may hold values from -0.109375 to 0.109375
- branch_bias: bfloat16 [2, 2, 768], replicated, may hold values from -1.5 to 1.5
- norm_gain: bfloat16 [2, 2, 768], replicated, may hold values from 0.3984375 to 1.59375
- norm_shift: bfloat16 [2, 2, 768], replicated, may hold values from -1.5 to 1.5
Outputs:
- hidden_out: bfloat16 [512, 16, 768], P('tensor', 'dp')
- grad_hidden: float32 [512, 16, 768], P('tensor', 'dp')
- grad_input_weight: float32 [2, 3, 768, 768], P(None, None, None, 'tensor')
- grad_input_bias: float32 [2, 2, 768], P(None, None, 'tensor')
- grad_output_weight: float32 [2, 768, 768], P(None, 'tensor')
- grad_up_weight: float32 [2, 768, 3072], P(None, None, 'tensor')
- grad_up_bias: float32 [2, 3072], P(None, 'tensor')
- grad_down_weight: float32 [2, 3072, 768], P(None, 'tensor')
- grad_branch_bias: float32 [2, 2, 768], replicated
- grad_norm_gain: float32 [2, 2, 768], replicated
- grad_norm_shift: float32 [2, 2, 768], replicated
The draws below stay inside these ranges and needn't reach their ends.
Inputs may be any that keep to these rules, and one draw needn't show every extreme that they name: `doc_lengths`: each row's 5 lengths add up to 512; in every row the longest text has exactly 385 positions.
All inputs are finite; a program needn't handle non-finite values.
Results may differ from the reference program's by a relative error of at most 0.029.
Values may be sent and summed in bfloat16 or wider, within the bound.
A program may use at most 128 MiB of HBM per device.

```python
import math
import jax
import jax.numpy as jnp
import numpy as np
from jax import lax

D = 768
HEADS = 12
HEAD_DIM = 64
FF = 3072
SEQ = 512
DOCS = 5
LAYERS = 2
ROWS = 16


def with_ends(values, rng, smallest, top_value):
    longest = values.shape.index(max(values.shape))
    spots = []
    for shift in (0, 1):
        where = [jax.random.randint(jax.random.fold_in(rng, axis), (), 0, length) for axis, length in enumerate(values.shape)]
        where[longest] = (where[longest] + shift) % values.shape[longest]
        spots.append(tuple(where))
    return values.at[spots[0]].set(smallest).at[spots[1]].set(top_value)


def steps_of(key, extent, shards, smallest, high):
    def one(axis_at, parts):
        draws = jax.random.uniform(jax.random.fold_in(jax.random.fold_in(key, 6), axis_at), (parts,), jnp.float32, smallest / len(shards), high / len(shards))
        return jnp.repeat(jnp.exp(draws), extent[axis_at] // parts).reshape((-1,) + (1,) * (len(extent) - axis_at - 1))

    level = one(*shards[0])
    for cut in shards[1:]:
        level = level * one(*cut)
    return level


def profile(count, total, bound, skew):
    loads = [(1 << 20) // math.isqrt(standing ** skew) + 1 for standing in range(2, count + 1)]
    surplus, given = total - bound - (count - 1), [1] * (count - 1)
    while surplus > 0:
        movable = [i for i in range(count - 1) if given[i] < bound]
        mass, left = sum([loads[i] for i in movable]), surplus
        for i in movable:
            more = min(bound - given[i], max(1, left * loads[i] // mass), surplus)
            given[i] = given[i] + more
            surplus = surplus - more
    return np.array([bound] + given)


def uneven(key, count, total, bound, slope):
    if count == 2:
        one = jax.random.randint(key, (), max(1, total - bound), min(bound, total - 1) + 1)
        return jnp.stack([one, total - one])
    sizes = jnp.asarray(profile(count, total, bound, slope), jnp.int32)
    twos = (count - 1) // 2
    donor, sink = sizes[1:1 + 2 * twos:2], sizes[2:2 + 2 * twos:2]
    room = jnp.minimum(donor - 1, bound - sink)
    passed = jax.random.randint(jax.random.fold_in(key, 1), (twos,), 0, 1 << 20) % (room + 1)
    sizes = sizes.at[1:1 + 2 * twos:2].set(donor - passed).at[2:2 + 2 * twos:2].set(sink + passed)
    return sizes[jax.random.permutation(jax.random.fold_in(key, 2), count)]


def noise(key, shape, spread, reach, shards=(), kind=jnp.bfloat16):
    array = jax.random.normal(key, shape, jnp.float32) * spread
    if len(shards) > 0:
        array = steps_of(key, shape, shards, -0.22, 0.18) * array
    return jnp.clip(array, min=-reach, max=reach).astype(kind)


def setup_inputs(seed: int = 0) -> dict:
    splits = jax.random.split(jax.random.key(seed), 14)
    return {
        "hidden_in": noise(splits[0], (SEQ, ROWS, D), 1.0, 2.5, ((0, 4), (1, 8))),
        "cotangent": noise(splits[1], (SEQ, ROWS, D), 1.0, 2.5, ((0, 4), (1, 8))),
        "doc_lengths": jax.vmap(lambda own: uneven(own, DOCS, SEQ, 3 * SEQ // 4 + 1, 2))(jax.random.split(splits[2], ROWS)).reshape((ROWS, DOCS)).astype(jnp.int32),
        "pad_count": with_ends(jax.random.randint(splits[3], (ROWS,), 1, SEQ // 16 + 1), jax.random.fold_in(splits[3], 1), 1, (SEQ // 16 + 1) - 1).astype(jnp.int32),
        "input_weight": noise(splits[4], (LAYERS, 3, D, D), D ** -0.5, 0.21875, ((3, 4),)),
        "input_bias": noise(splits[5], (LAYERS, 2, D), 0.5, 1.5, ((2, 4),)),
        "output_weight": noise(splits[6], (LAYERS, D, D), (D // 16) ** -0.5, 0.875, ((1, 4),)),
        "up_weight": noise(splits[7], (LAYERS, D, FF), D ** -0.5, 0.21875, ((2, 4),)),
        "up_bias": noise(splits[8], (LAYERS, FF), 0.5, 1.5, ((1, 4),)),
        "down_weight": noise(splits[9], (LAYERS, FF, D), FF ** -0.5, 0.109375, ((1, 4),)),
        "branch_bias": noise(splits[10], (LAYERS, 2, D), 0.5, 1.5),
        "norm_gain": jnp.clip(1.0 + 0.12 * jax.random.normal(splits[11], (LAYERS, 2, D), jnp.float32), 0.3984375, 1.59375).astype(jnp.bfloat16),
        "norm_shift": noise(splits[12], (LAYERS, 2, D), 0.5, 1.5),
    }


epsilon = 1e-05
masked_value = -1e+30
exact = lax.Precision.HIGHEST

@jax.custom_vjp
def low(v):
    return lax.optimization_barrier(v.astype(jnp.bfloat16)).astype(jnp.float32)

@jax.custom_vjp
def low_back(v):
    return v

def low_keep(v):
    return (low(v), None)

def low_pass(kept, grad):
    return (grad,)

def back_keep(v):
    return (v, None)

def back_low(kept, grad):
    return (low(grad),)
low.defvjp(low_keep, low_pass)
low_back.defvjp(back_keep, back_low)

def normalize(value, gain, shift):
    average = lax.optimization_barrier(jnp.mean(value, axis=-1, keepdims=True))
    centered = value - average
    variance = lax.optimization_barrier(jnp.mean(centered * centered, axis=-1, keepdims=True))
    return centered * lax.rsqrt(variance + epsilon) * gain + shift

def gelu(value):
    return 0.5 * value * (1.0 + lax.erf(value * 0.7071067811865476))

def segment_table(lengths, padding, seq_len):
    ends = jnp.cumsum(lengths, axis=1).astype(jnp.int32)
    position = jnp.arange(seq_len, dtype=jnp.int32)
    index = lax.optimization_barrier(jnp.sum((position[:, None, None] >= ends[None, :, :]).astype(jnp.int32), axis=2)).astype(jnp.int32)
    padded = position[:, None] >= (seq_len - padding)[None, :]
    return jnp.where(padded, lengths.shape[1], index).astype(jnp.int32)

def block(hidden, segments, weights):
    in_weight, in_bias, out_weight, wide_weight, wide_bias, narrow_weight, biases, gains, shifts = weights
    projected = jnp.einsum('sbd,cde->csbe', low(hidden), in_weight, precision=exact)
    query = low_back(low(projected[0] + in_bias[0]))
    keys = low_back(low(projected[1]))
    values = low_back(low(projected[2] + in_bias[1]))
    shape = (hidden.shape[0], hidden.shape[1], HEADS, HEAD_DIM)
    scores = low_back(jnp.einsum('qbhe,kbhe->bhqk', query.reshape(shape), keys.reshape(shape), precision=exact) * HEAD_DIM ** (-0.5))
    allowed = (segments.T[:, :, None] == segments.T[:, None, :])[:, None]
    masked = jnp.where(allowed, scores, masked_value)
    largest = lax.optimization_barrier(jnp.max(masked, axis=-1, keepdims=True))
    powers = jnp.exp(masked - largest)
    probs = powers / lax.optimization_barrier(jnp.sum(powers, axis=-1, keepdims=True))
    context = jnp.einsum('bhqk,kbhe->qbhe', low(probs), values.reshape(shape), precision=exact).reshape(hidden.shape)
    context = low_back(low(context))
    mixed = low_back(jnp.einsum('sbd,de->sbe', context, out_weight, precision=exact))
    first = normalize(hidden + mixed + biases[0], gains[0], shifts[0])
    wide = low_back(jnp.einsum('sbd,df->sbf', low(first), wide_weight, precision=exact) + wide_bias)
    fed = low_back(jnp.einsum('sbf,fd->sbd', low(gelu(wide)), narrow_weight, precision=exact))
    return normalize(first + fed + biases[1], gains[1], shifts[1])

def network(hidden, segments, weights):
    for layer in range(LAYERS):
        hidden = block(hidden, segments, tuple((item[layer] for item in weights)))
    return hidden

def reference(hidden_in, cotangent, doc_lengths, pad_count, input_weight, input_bias, output_weight, up_weight, up_bias, down_weight, branch_bias, norm_gain, norm_shift):
    params = tuple((item.astype(jnp.float32) for item in (input_weight, input_bias, output_weight, up_weight, up_bias, down_weight, branch_bias, norm_gain, norm_shift)))
    segments = segment_table(doc_lengths, pad_count, SEQ)
    blocks = ROWS // 4

    def split(value):
        return jnp.moveaxis(value.reshape((SEQ, blocks, 4) + value.shape[2:]), 1, 0)

    def join(value):
        return jnp.moveaxis(value, 0, 1).reshape((SEQ, ROWS) + value.shape[3:])

    def step(totals, slices):
        block_in, block_grad, block_seg = slices

        def forward(hidden, weights):
            return network(hidden, block_seg, weights)
        result, pull = jax.vjp(forward, block_in, params)
        grad_in, grad_params = pull(block_grad)
        totals = jax.tree.map(jnp.add, totals, grad_params)
        return (totals, (result, grad_in))
    zeros = jax.tree.map(jnp.zeros_like, params)
    totals, outputs = lax.scan(step, zeros, (split(hidden_in.astype(jnp.float32)), split(cotangent.astype(jnp.float32)), split(segments)))
    results, grad_ins = outputs
    return (join(results).astype(jnp.bfloat16), join(grad_ins), totals[0], totals[1], totals[2], totals[3], totals[4], totals[5], totals[6], totals[7], totals[8])
```

```python
import functools

import jax
import jax.numpy as jnp
from jax import lax
from jax.experimental import pallas as pl
from jax.experimental.pallas import tpu as pltpu
from jax.sharding import PartitionSpec as P

HEAD_DIM = 64
EPSILON = 1e-05
MASKED = -1e30
MESH = pl.DeviceIdType.MESH
BF, F32 = jnp.bfloat16, jnp.float32
NN = (((1,), (0,)), ((), ()))
NT = (((1,), (1,)), ((), ()))
TN = (((0,), (0,)), ((), ()))
UNIT = 384


def dot(a, b, dims):
    return lax.dot_general(a, b, dims, preferred_element_type=F32)


def aligned(value, by=16):
    return pl.multiple_of(value, by)


def segment_table(lengths, padding, seq_len):
    ends = jnp.cumsum(lengths, axis=1)
    position = jnp.arange(seq_len, dtype=jnp.int32)
    index = jnp.sum((position[:, None, None] >= ends[None, :, :]).astype(jnp.int32), axis=2)
    padded = position[:, None] >= (seq_len - padding)[None, :]
    return jnp.where(padded, lengths.shape[1], index)


class Net:
    def __init__(self, n_dp):
        dp, t = lax.axis_index("dp"), lax.axis_index("tensor")
        self.dp, self.t = dp, t
        y, c = t // 2, t % 2
        self.t_core = t + 1 - 2 * c
        self.t_y = t + 2 - 4 * y
        self.t_far = 3 - t
        self.core, self.y = (dp, self.t_core), (dp, self.t_y)
        self.x = dp % 2
        z = (dp // 2) % 4
        self.half = z // 2
        self.inner = (z == 1) | (z == 2)
        self.edge = (z == 0) | (z == 3)
        self.x_dev = (dp + 1 - 2 * self.x, t)
        self.hop_dev = (dp + 2 * (1 - 2 * (z % 2)), t)
        self.mid_dev = (dp + 2 * (3 - 2 * z), t)
        self.z2_dev = (dp + 2 * (2 - 4 * (z // 2)), t)
        self.outer_devs = []
        step = 8
        while step < n_dp:
            self.outer_devs.append((dp + step * (1 - 2 * ((dp // step) % 2)), t))
            step *= 2
        self.vector_devs = [self.x_dev, self.hop_dev, self.z2_dev] + self.outer_devs
        self.partners = [self.core, self.y, self.mid_dev] + self.vector_devs


def remote(src, dst, send, recv, device):
    return pltpu.make_async_remote_copy(
        src_ref=src, dst_ref=dst, send_sem=send, recv_sem=recv, device_id=device, device_id_type=MESH
    )


def kernel(n_dp, layers, *refs):
    (x_in, cot, segc, segr, wt_h, bcol, wo_h, wu_h, wd_h, bup, vec,
     hidden_out, grad_hidden, grads, vectors,
     WT, WO, WU, WD, XG, HG, G, DG, DF, DM, DU, QKVT, PT, CT, DPT, DST, DCT, PART, RB, XRES, HRES, XH, RSTD, GR,
     RX0, RX1, RX2, RZ0, RZ1, RZ2, RXO, RZO, SX0, SX1, SX2, SZ0, SZ1, SZ2, VB, RV,
     wsem, ag_s, ag_r, rs_s, rs_r, arx_s, arx_r, arz_s, arz_r, v_s, v_r, osem) = refs
    DY, DH = XRES, HRES
    net = Net(n_dp)
    rows, block, width = x_in.shape
    seq = PART.shape[1]
    n_qkv = WT.shape[1]
    n_head = n_qkv // 3
    heads = n_head // HEAD_DIM
    ff = WU.shape[2]

    weight_copies = [
        pltpu.make_async_copy(a, b, wsem.at[i])
        for i, (a, b) in enumerate(((wt_h, WT), (wo_h, WO), (wu_h, WU), (wd_h, WD)))
    ]
    for copy in weight_copies:
        copy.start()

    barrier = pltpu.get_barrier_semaphore()
    for device in net.partners:
        pl.semaphore_signal(barrier, inc=1, device_id=device, device_id_type=MESH)
    pl.semaphore_wait(barrier, len(net.partners))

    def rows_at(r, t):
        return pl.ds(aligned(r * seq + t * block), block)

    def mine(r):
        return rows_at(r, net.t)

    ALONG, ACROSS, ONWARD = 0, 1, 2

    def gather_copy(buf, r, k):
        block = buf.at[rows_at(r, net.t_y if k == ONWARD else net.t)]
        return remote(block, block, ag_s.at[r, k], ag_r.at[r, k], net.y if k == ALONG else net.core)

    def gather_start(buf, r):
        gather_copy(buf, r, ALONG).start()
        gather_copy(buf, r, ACROSS).start()

    def gather_pass(buf, r):
        gather_copy(buf, r, ALONG).wait_recv()
        gather_copy(buf, r, ONWARD).start()

    def gather_end(buf, r):
        gather_copy(buf, r, ACROSS).wait_recv()
        gather_copy(buf, r, ONWARD).wait_recv()
        for k in (ALONG, ACROSS, ONWARD):
            gather_copy(buf, r, k).wait_send()

    FAR, NEAR, SUMMED = 0, 1, 2

    def sum_copy(r, k):
        block_of = (net.t_far, net.t_core, net.t_y)[k]
        src = PART.at[r, pl.ds(aligned(block_of * block), block)]
        return remote(src, RB.at[r, k], rs_s.at[r, k], rs_r.at[r, k], net.y if k == SUMMED else net.core)

    def sum_start(r):
        sum_copy(r, FAR).start()
        sum_copy(r, NEAR).start()

    def sum_pass(r):
        sum_copy(r, FAR).wait_recv()
        at = pl.ds(aligned(net.t_y * block), block)
        PART[r, at] = (PART[r, at].astype(F32) + RB[r, FAR].astype(F32)).astype(BF)
        sum_copy(r, SUMMED).start()

    def sum_end(r):
        sum_copy(r, NEAR).wait_recv()
        sum_copy(r, SUMMED).wait_recv()
        for k in (FAR, NEAR, SUMMED):
            sum_copy(r, k).wait_send()
        own = PART[r, pl.ds(aligned(net.t * block), block)]
        return own.astype(F32) + RB[r, NEAR].astype(F32) + RB[r, SUMMED].astype(F32)

    def attention_forward(l, r):
        xg = XG[l, r * seq : (r + 1) * seq]
        for c in range(3):
            at = slice(c * n_head, (c + 1) * n_head)
            QKVT[l, r, at] = (dot(WT[l, at], xg, NT) + bcol[l, at]).astype(BF)

        def head(h, carry):
            o = h * HEAD_DIM
            kt = QKVT[l, r, pl.ds(aligned(n_head + o), HEAD_DIM)] * jnp.asarray(HEAD_DIM**-0.5, BF)
            vt = QKVT[l, r, pl.ds(aligned(2 * n_head + o), HEAD_DIM)]
            qt = QKVT[l, r, pl.ds(aligned(o), HEAD_DIM)]
            scores = jnp.where(segc[r] == segr[r], dot(kt, qt, TN), MASKED)
            powers = jnp.exp(scores - jnp.max(scores, axis=0, keepdims=True))
            probs = (powers * (1.0 / jnp.sum(powers, axis=0, keepdims=True))).astype(BF)
            PT[l, r, h] = probs
            CT[l, r, pl.ds(aligned(o), HEAD_DIM)] = dot(vt, probs, NN).astype(BF)
            return carry

        lax.fori_loop(0, heads, head, 0)
        for q in range(2):
            at = slice(q * seq // 2, (q + 1) * seq // 2)
            PART[r, at] = dot(CT[l, r, :, at], WO[l], TN).astype(BF)

    def norm(l, k, r, value):
        centered = value - jnp.mean(value, axis=-1, keepdims=True)
        rstd = lax.rsqrt(jnp.mean(centered * centered, axis=-1, keepdims=True) + EPSILON)
        normal = centered * rstd
        XH[l, k, r] = normal.astype(BF)
        RSTD[l, k, r] = rstd
        return normal * vec[l, 2 + k : 3 + k] + vec[l, 4 + k : 5 + k]

    def first_norm(l, r):
        out = norm(l, 0, r, XRES[r] + sum_end(r) + vec[l, 0:1])
        HRES[r] = out
        HG[l, mine(r)] = out.astype(BF)
        gather_start(HG.at[l], r)

    def ff_forward(l, r):
        hg = HG[l, r * seq : (r + 1) * seq]
        wide = dot(hg, WU[l], NN) + bup[l]
        cdf = 0.5 * (1.0 + lax.erf(wide * 0.7071067811865476))
        active = (wide * cdf).astype(BF)
        G[l, r * seq : (r + 1) * seq] = active
        DG[l, r * seq : (r + 1) * seq] = (cdf + wide * 0.3989422804014327 * jnp.exp(-0.5 * wide * wide)).astype(BF)
        PART[r] = dot(G[l, r * seq : (r + 1) * seq], WD[l], NN).astype(BF)

    def second_norm(l, r):
        out = norm(l, 1, r, HRES[r] + sum_end(r) + vec[l, 1:2])
        XRES[r] = out

        @pl.when(l < layers - 1)
        def _():
            XG[l + 1, mine(r)] = out.astype(BF)
            gather_start(XG.at[l + 1], r)

        @pl.when(l == layers - 1)
        def _():
            hidden_out[r] = out.astype(BF)

    def norm_backward(l, k, r, upstream):
        normal, rstd = XH[l, k, r].astype(F32), RSTD[l, k, r]
        VB[0, l, 2 + k : 3 + k] += jnp.sum(upstream * normal, axis=0, keepdims=True)
        VB[0, l, 4 + k : 5 + k] += jnp.sum(upstream, axis=0, keepdims=True)
        scaled = upstream * vec[l, 2 + k : 3 + k]
        grad = rstd * (
            scaled
            - jnp.mean(scaled, axis=-1, keepdims=True)
            - normal * jnp.mean(scaled * normal, axis=-1, keepdims=True)
        )
        VB[0, l, k : k + 1] += jnp.sum(grad, axis=0, keepdims=True)
        return grad

    def second_norm_backward(l, r, upstream):
        grad = norm_backward(l, 1, r, upstream)
        DH[r] = grad
        DF[mine(r)] = grad.astype(BF)
        gather_start(DF, r)

    def ff_backward(l, r):
        at = slice(r * seq, (r + 1) * seq)
        grad = (dot(DF[at], WD[l], NT) * DG[l, at].astype(F32)).astype(BF)
        DU[at] = grad
        VB[1, l, 0:1, :ff] += jnp.sum(grad.astype(F32), axis=0, keepdims=True)
        PART[r] = dot(DU[at], WU[l], NT).astype(BF)

    def first_norm_backward(l, r):
        grad = norm_backward(l, 0, r, DH[r] + sum_end(r))
        DY[r] = grad
        DM[mine(r)] = grad.astype(BF)
        gather_start(DM, r)

    def attention_backward(l, r):
        DCT[...] = dot(WO[l], DM[r * seq : (r + 1) * seq], NT).astype(BF)

        def head(h, carry):
            o = h * HEAD_DIM
            q_at, k_at, v_at = (pl.ds(aligned(c * n_head + o), HEAD_DIM) for c in range(3))
            dct = DCT[q_at]
            probs = PT[l, r, h].astype(F32)
            weighted = probs * dot(QKVT[l, r, v_at], dct, TN)
            inner = jnp.sum(weighted, axis=0, keepdims=True)
            DST[...] = (weighted - probs * inner).astype(BF)
            scale = HEAD_DIM**-0.5
            DPT[r, q_at] = (dot(QKVT[l, r, k_at], DST[...], NN) * scale).astype(BF)
            DPT[r, k_at] = (dot(QKVT[l, r, q_at], DST[...], NT) * scale).astype(BF)
            DPT[r, v_at] = dot(dct, PT[l, r, h], NT).astype(BF)
            return carry

        lax.fori_loop(0, heads, head, 0)
        ones = jnp.ones((8, seq), BF)
        VB[1, l, 1:2, :n_qkv] += dot(ones, DPT[r], NT)[0:1]
        for q in range(2):
            at = slice(q * seq // 2, (q + 1) * seq // 2)
            PART[r, at] = dot(DPT[r, :, at], WT[l], TN).astype(BF)

    per_layer = GR.shape[0] // layers

    def tokens_product(left, right, base):
        def strip(i, carry):
            at = pl.ds(aligned(i * 256, 256), 256)
            GR[pl.ds(aligned(base + i * 256), 256)] = dot(left[:, at], right[...], TN).astype(BF)
            return carry

        lax.fori_loop(0, left.shape[1] // 256, strip, 0)

    def attention_gradients(l, base):
        at = pl.ds(aligned(base), n_qkv)
        GR[at] = sum(dot(DPT[r], XG[l, r * seq : (r + 1) * seq], NN) for r in range(rows)).astype(BF)
        at = pl.ds(aligned(base + n_qkv), n_head)
        GR[at] = sum(dot(CT[l, r], DM[r * seq : (r + 1) * seq], NN) for r in range(rows)).astype(BF)

    units = GR.shape[0] // UNIT
    part = UNIT // 2
    half, quarter = part // 2, part // 4
    stages_x, stages_z = [], []
    always = None

    def stage(who_send, who_recv, device, offset, length, landing=None, add=None, staging=None):
        return (who_send, who_recv, device, offset, length, landing, add, staging)

    inner, edge = net.inner, net.edge
    keep, give = net.x * half, (1 - net.x) * half
    keep2, give2 = keep + net.half * quarter, keep + (1 - net.half) * quarter
    stages_x.append(stage(always, always, net.x_dev, give, half, RX0, keep, SX0))
    stages_x.append(stage(edge, inner, net.hop_dev, keep, half, RX1, keep, SX1))
    stages_x.append(stage(inner, inner, net.mid_dev, give2, quarter, RX2, keep2, SX2))
    for i, device in enumerate(net.outer_devs):
        stages_x.append(stage(inner, inner, device, keep2, quarter, RXO.at[i], keep2))
    stages_x.append(stage(inner, inner, net.mid_dev, keep2, quarter))
    stages_x.append(stage(inner, edge, net.hop_dev, keep, half))
    stages_x.append(stage(always, always, net.x_dev, keep, half))
    keep, give = part + net.half * half, part + (1 - net.half) * half
    keep2, give2 = keep + net.x * quarter, keep + (1 - net.x) * quarter
    stages_z.append(stage(edge, inner, net.hop_dev, part, part, RZ0, part, SZ0))
    stages_z.append(stage(inner, inner, net.mid_dev, give, half, RZ1, keep, SZ1))
    stages_z.append(stage(inner, inner, net.x_dev, give2, quarter, RZ2, keep2, SZ2))
    for i, device in enumerate(net.outer_devs):
        stages_z.append(stage(inner, inner, device, keep2, quarter, RZO.at[i], keep2))
    stages_z.append(stage(inner, inner, net.x_dev, keep2, quarter))
    stages_z.append(stage(inner, inner, net.mid_dev, keep, half))
    stages_z.append(stage(inner, edge, net.hop_dev, part, part))
    depth = len(stages_x)

    def when(condition, body):
        if condition is None:
            body()
        else:
            pl.when(condition)(body)

    def stage_copy(which, s, u):
        _, _, device, offset, length, landing, _, staging = which[0][s]
        slot = u % depth
        src = GR.at[pl.ds(aligned(u * UNIT + offset), length)]
        dst = src if landing is None else landing.at[u % landing.shape[0]]
        src = src if staging is None else staging
        return remote(src, dst, which[1].at[slot, s], which[2].at[slot, s], device)

    def stage_send(which, s, u):
        who_send, _, _, offset, length, _, _, staging = which[0][s]

        def send():
            if staging is not None:
                staging[...] = GR[pl.ds(aligned(u * UNIT + offset), length)]
            stage_copy(which, s, u).start()

        when(who_send, send)

    def stage_sent(which, s, u):
        when(which[0][s][0], lambda: stage_copy(which, s, u).wait_send())

    def stage_recv(which, s, u):
        _, who_recv, _, _, length, landing, add, _ = which[0][s]

        def take():
            stage_copy(which, s, u).wait_recv()
            if landing is not None:
                at = pl.ds(aligned(u * UNIT + add), length)
                GR[at] = (GR[at].astype(F32) + landing[u % landing.shape[0]].astype(F32)).astype(BF)

        when(who_recv, take)

    both = ((stages_x, arx_s, arx_r), (stages_z, arz_s, arz_r))

    def out_copy(u):
        at = pl.ds(aligned(u * UNIT), UNIT)
        return pltpu.make_async_copy(GR.at[at], grads.at[at], osem.at[u])

    def tick(t):
        for s in range(depth):
            u = t - 1 - s

            @pl.when((u >= 0) & (u < units))
            def _(s=s, u=u):
                for which in both:
                    stage_sent(which, s, u)

        @pl.when(t < units)
        def _():
            for which in both:
                stage_send(which, 0, t)

        for s in range(depth):
            u = t - 1 - s

            @pl.when((u >= 0) & (u < units))
            def _(s=s, u=u):
                for which in both:
                    stage_recv(which, s, u)
                    if s + 1 < depth:
                        stage_send(which, s + 1, u)
                if s + 1 == depth:
                    out_copy(u).start()

    VB[...] = jnp.zeros(VB.shape, F32)
    for r in range(rows):
        XG[0, mine(r)] = x_in[r]
        XRES[r] = x_in[r].astype(F32)
        gather_start(XG.at[0], r)
    for copy in weight_copies:
        copy.wait()

    def half_layer(buf, compute):
        gather_pass(buf, 0)
        gather_end(buf, 0)
        compute(0)
        sum_start(0)
        gather_pass(buf, 1)
        sum_pass(0)
        gather_end(buf, 1)
        compute(1)
        sum_start(1)
        sum_pass(1)

    def forward(l, carry):
        half_layer(XG.at[l], lambda r: attention_forward(l, r))
        for r in range(rows):
            first_norm(l, r)
        half_layer(HG.at[l], lambda r: ff_forward(l, r))
        for r in range(rows):
            second_norm(l, r)
        return carry

    lax.fori_loop(0, layers, forward, 0)

    per_units = per_layer // UNIT
    for r in range(rows):
        second_norm_backward(layers - 1, r, cot[r].astype(F32))

    def backward(i, carry):
        l = layers - 1 - i
        base, first = i * per_layer, i * per_units
        half_layer(DF, lambda r: ff_backward(l, r))
        tokens_product(G.at[l], DF, base)
        tick(first)
        for r in range(rows):
            first_norm_backward(l, r)
        tokens_product(HG.at[l], DU, base + ff)
        tick(first + 1)
        buf = DM
        gather_pass(buf, 0)
        gather_end(buf, 0)
        attention_backward(l, 0)
        sum_start(0)
        tick(first + 2)
        gather_pass(buf, 1)
        sum_pass(0)
        gather_end(buf, 1)
        attention_backward(l, 1)
        sum_start(1)
        sum_pass(1)
        tick(first + 3)
        attention_gradients(l, base + 2 * ff)
        tick(first + 4)
        for r in range(rows):
            DY[r] = DY[r] + sum_end(r)

            @pl.when(l > 0)
            def _(r=r):
                second_norm_backward(l - 1, r, DY[r])

            @pl.when(l == 0)
            def _(r=r):
                grad_hidden[r] = DY[r]

        tick(first + 5)
        return carry

    lax.fori_loop(0, layers, backward, 0)

    def vector_copy(k):
        if k < 2:
            return remote(VB.at[0], RV.at[k, 0], v_s.at[k], v_r.at[k], (net.core, net.y)[k])
        return remote(VB, RV.at[k], v_s.at[k], v_r.at[k], net.vector_devs[k - 2])

    n_vector = 2 + len(net.vector_devs)
    for k in range(max(depth, n_vector + 1)):
        if 0 < k <= n_vector:
            vector_copy(k - 1).wait()
            if k - 1 < 2:
                VB[0] += RV[k - 1, 0]
            else:
                VB[...] += RV[k - 1]
        if k < n_vector:
            vector_copy(k).start()
        tick(units + k)
    vectors[...] = VB[...]

    def finish(u, carry):
        out_copy(u).wait()
        return carry

    lax.fori_loop(0, units, finish, 0)


def local(
    hidden_in,
    cotangent,
    doc_lengths,
    pad_count,
    input_weight,
    input_bias,
    output_weight,
    up_weight,
    up_bias,
    down_weight,
    branch_bias,
    norm_gain,
    norm_shift,
):
    n_dp = lax.axis_size("dp")
    block, rows, width = hidden_in.shape
    seq = block * lax.axis_size("tensor")
    layers, _, _, n_head = input_weight.shape
    n_qkv, heads, ff = 3 * n_head, n_head // HEAD_DIM, up_weight.shape[2]
    tokens = rows * seq
    segments = segment_table(doc_lengths, pad_count, seq).T
    wt = jnp.swapaxes(input_weight, 2, 3).reshape(layers, n_qkv, width)
    bcol = jnp.stack(
        [input_bias[:, 0], jnp.zeros_like(input_bias[:, 0]), input_bias[:, 1]], axis=1
    ).reshape(layers, n_qkv, 1).astype(F32)
    vec = jnp.concatenate([branch_bias, norm_gain, norm_shift], axis=1).astype(F32)
    per_layer = 2 * ff + n_qkv + n_head
    part = UNIT // 2
    outer = 0
    while 8 << outer < n_dp:
        outer += 1
    depth = 6 + outer
    n_vector = 5 + outer
    vmem = pltpu.VMEM
    dma = pltpu.SemaphoreType.DMA
    scratch = [
        vmem((layers, n_qkv, width), BF),
        vmem((layers, n_head, width), BF),
        vmem((layers, width, ff), BF),
        vmem((layers, ff, width), BF),
        vmem((layers, tokens, width), BF),
        vmem((layers, tokens, width), BF),
        vmem((layers, tokens, ff), BF),
        vmem((layers, tokens, ff), BF),
        vmem((tokens, width), BF),
        vmem((tokens, width), BF),
        vmem((tokens, ff), BF),
        vmem((layers, rows, n_qkv, seq), BF),
        vmem((layers, rows, heads, seq, seq), BF),
        vmem((layers, rows, n_head, seq), BF),
        vmem((rows, n_qkv, seq), BF),
        vmem((seq, seq), BF),
        vmem((n_head, seq), BF),
        vmem((rows, seq, width), BF),
        vmem((rows, 3, block, width), BF),
        vmem((rows, block, width), F32),
        vmem((rows, block, width), F32),
        vmem((layers, 2, rows, block, width), BF),
        vmem((layers, 2, rows, block, 1), F32),
        vmem((layers * per_layer, width), BF),
        vmem((4, part // 2, width), BF),
        vmem((depth, part // 2, width), BF),
        vmem((4, part // 4, width), BF),
        vmem((depth, part, width), BF),
        vmem((4, part // 2, width), BF),
        vmem((4, part // 4, width), BF),
        vmem((max(outer, 1), 4 if outer else 1, part // 4, width), BF),
        vmem((max(outer, 1), 4 if outer else 1, part // 4, width), BF),
        vmem((part // 2, width), BF),
        vmem((part // 2, width), BF),
        vmem((part // 4, width), BF),
        vmem((part, width), BF),
        vmem((part // 2, width), BF),
        vmem((part // 4, width), BF),
        vmem((2, layers, 8, width), F32),
        vmem((n_vector, 2, layers, 8, width), F32),
        dma((4,)),
        dma((rows, 3)),
        dma((rows, 3)),
        dma((rows, 3)),
        dma((rows, 3)),
        dma((depth, depth)),
        dma((depth, depth)),
        dma((depth, depth)),
        dma((depth, depth)),
        dma((n_vector,)),
        dma((n_vector,)),
        dma((layers * per_layer // UNIT,)),
    ]
    whole, anywhere = pl.BlockSpec(memory_space=vmem), pl.BlockSpec(memory_space=pl.ANY)
    hidden_out, grad_hidden, grads, vectors = pl.pallas_call(
        functools.partial(kernel, n_dp, layers),
        out_shape=(
            jax.ShapeDtypeStruct((rows, block, width), BF),
            jax.ShapeDtypeStruct((rows, block, width), F32),
            jax.ShapeDtypeStruct((layers * per_layer, width), BF),
            jax.ShapeDtypeStruct((2, layers, 8, width), F32),
        ),
        in_specs=[whole] * 4 + [anywhere, whole, anywhere, anywhere, anywhere, whole, whole],
        out_specs=(whole, whole, anywhere, whole),
        scratch_shapes=scratch,
        compiler_params=pltpu.CompilerParams(
            collective_id=0, has_side_effects=True, vmem_limit_bytes=63 << 20
        ),
    )(
        jnp.swapaxes(hidden_in, 0, 1),
        jnp.swapaxes(cotangent, 0, 1),
        segments[:, :, None],
        segments[:, None, :],
        wt,
        bcol,
        output_weight,
        up_weight,
        down_weight,
        up_bias.astype(F32)[:, None, :],
        vec,
    )
    grads = grads.reshape(layers, per_layer, width)[::-1]
    grad_in = grads[:, 2 * ff : 2 * ff + n_qkv].reshape(layers, 3, n_head, width)
    shared, split = vectors[0], vectors[1]
    in_bias = split[:, 1, :n_qkv].reshape(layers, 3, n_head)
    return (
        jnp.swapaxes(hidden_out, 0, 1),
        jnp.swapaxes(grad_hidden, 0, 1),
        jnp.swapaxes(grad_in, 2, 3).astype(F32),
        jnp.stack([in_bias[:, 0], in_bias[:, 2]], axis=1),
        grads[:, 2 * ff + n_qkv :].astype(F32),
        grads[:, ff : 2 * ff].astype(F32),
        split[:, 0, :ff],
        grads[:, :ff].astype(F32),
        shared[:, 0:2],
        shared[:, 2:4],
        shared[:, 4:6],
    )


def solution(mesh):
    return jax.shard_map(
        local,
        mesh=mesh,
        in_specs=(
            P("tensor", "dp", None),
            P("tensor", "dp", None),
            P("dp", None),
            P("dp"),
            P(None, None, None, "tensor"),
            P(None, None, "tensor"),
            P(None, "tensor", None),
            P(None, None, "tensor"),
            P(None, "tensor"),
            P(None, "tensor", None),
            P(),
            P(),
            P(),
        ),
        out_specs=(
            P("tensor", "dp", None),
            P("tensor", "dp", None),
            P(None, None, None, "tensor"),
            P(None, None, "tensor"),
            P(None, "tensor", None),
            P(None, None, "tensor"),
            P(None, "tensor"),
            P(None, "tensor", None),
            P(),
            P(),
            P(),
        ),
        check_vma=False,
    )
```

```python
import functools

import jax
import jax.numpy as jnp
from jax import lax
from jax.experimental import pallas as pl
from jax.experimental.pallas import tpu as pltpu
from jax.sharding import PartitionSpec as P

HEAD_DIM = 64
EPSILON = 1e-05
MASKED = -1e30
MESH = pl.DeviceIdType.MESH
BF, F32 = jnp.bfloat16, jnp.float32
NN = (((1,), (0,)), ((), ()))
NT = (((1,), (1,)), ((), ()))
TN = (((0,), (0,)), ((), ()))
UNIT = 128
SPACING, SLOTS = 2, 6


def dot(a, b, dims):
    return lax.dot_general(a, b, dims, preferred_element_type=F32)


def aligned(value, by=16):
    return pl.multiple_of(value, by)


class Net:
    def __init__(self, n_dp):
        dp, t = lax.axis_index("dp"), lax.axis_index("tensor")
        self.dp, self.t = dp, t
        y, c = t // 2, t % 2
        self.t_core = t + 1 - 2 * c
        self.t_y = t + 2 - 4 * y
        self.t_far = 3 - t
        self.core, self.y = (dp, self.t_core), (dp, self.t_y)
        self.x = dp % 2
        z = (dp // 2) % 4
        self.half = z // 2
        self.inner = (z == 1) | (z == 2)
        self.edge = (z == 0) | (z == 3)
        self.x_dev = (dp + 1 - 2 * self.x, t)
        self.hop_dev = (dp + 2 * (1 - 2 * (z % 2)), t)
        self.mid_dev = (dp + 2 * (3 - 2 * z), t)
        self.z2_dev = (dp + 2 * (2 - 4 * (z // 2)), t)
        self.outer_devs = []
        step = 8
        while step < n_dp:
            self.outer_devs.append((dp + step * (1 - 2 * ((dp // step) % 2)), t))
            step *= 2
        self.vector_devs = [self.x_dev, self.hop_dev, self.z2_dev] + self.outer_devs
        self.partners = [self.core, self.y, self.mid_dev] + self.vector_devs


def remote(src, dst, send, recv, device):
    return pltpu.make_async_remote_copy(
        src_ref=src, dst_ref=dst, send_sem=send, recv_sem=recv, device_id=device, device_id_type=MESH
    )


def kernel(n_dp, layers, *refs):
    (x_in, cot, lengths, padding, wt_h, in_bias, wo_h, wu_h, up_bias, wd_h, branch_bias, norm_gain, norm_shift,
     hidden_out, grad_hidden, grad_in, grad_in_bias, grad_out, grad_up, grad_up_bias, grad_down,
     grad_branch, grad_gain, grad_shift,
     WT, WO, WU, WD, XG, HG, G, DG, DF, DU, QKVT, PT, CT, DPT, DST, DCT, PART, RB, XRES, HRES, XH, RSTD, GR,
     RX0, RX1, RX2, RZ0, RZ1, RZ2, RXO, RZO, SX0, SX1, SZ0, SZ1, VB, RV, segc, segr, bcol, bup, vec,
     wsem, ag_s, ag_r, rs_s, rs_r, arx_s, arx_r, arz_s, arz_r, v_s, v_r, osem, credit_x, credit_z) = refs
    DY, DH = XRES, HRES
    net = Net(n_dp)
    block, rows, width = x_in.shape
    seq = PART.shape[1]
    n_qkv = WT.shape[1]
    n_head = n_qkv // 3
    heads = n_head // HEAD_DIM
    ff = WU.shape[2]

    weight_copies = [
        pltpu.make_async_copy(a, b, wsem.at[i])
        for i, (a, b) in enumerate(((wt_h, WT), (wo_h, WO), (wu_h, WU), (wd_h, WD)))
    ]
    for copy in weight_copies:
        copy.start()

    barrier = pltpu.get_barrier_semaphore()
    for device in net.partners:
        pl.semaphore_signal(barrier, inc=1, device_id=device, device_id_type=MESH)
    pl.semaphore_wait(barrier, len(net.partners))

    def rows_at(r, t):
        return pl.ds(aligned(r * seq + t * block), block)

    def mine(r):
        return rows_at(r, net.t)

    ALONG, ACROSS, ONWARD = 0, 1, 2

    def gather_copy(buf, r, k):
        block = buf.at[rows_at(r, net.t_y if k == ONWARD else net.t)]
        return remote(block, block, ag_s.at[r, k], ag_r.at[r, k], net.y if k == ALONG else net.core)

    def gather_start(buf, r):
        gather_copy(buf, r, ALONG).start()
        gather_copy(buf, r, ACROSS).start()

    def gather_pass(buf, r):
        gather_copy(buf, r, ALONG).wait_recv()
        gather_copy(buf, r, ONWARD).start()

    def gather_end(buf, r):
        gather_copy(buf, r, ACROSS).wait_recv()
        gather_copy(buf, r, ONWARD).wait_recv()
        for k in (ALONG, ACROSS, ONWARD):
            gather_copy(buf, r, k).wait_send()

    FAR, NEAR, SUMMED = 0, 1, 2

    def sum_copy(r, k):
        block_of = (net.t_far, net.t_core, net.t_y)[k]
        src = PART.at[r, pl.ds(aligned(block_of * block), block)]
        return remote(src, RB.at[r, k], rs_s.at[r, k], rs_r.at[r, k], net.y if k == SUMMED else net.core)

    def sum_start(r):
        sum_copy(r, FAR).start()
        sum_copy(r, NEAR).start()

    def sum_pass(r):
        sum_copy(r, FAR).wait_recv()
        at = pl.ds(aligned(net.t_y * block), block)
        PART[r, at] = (PART[r, at].astype(F32) + RB[r, FAR].astype(F32)).astype(BF)
        sum_copy(r, SUMMED).start()

    def sum_end(r):
        sum_copy(r, NEAR).wait_recv()
        sum_copy(r, SUMMED).wait_recv()
        for k in (FAR, NEAR, SUMMED):
            sum_copy(r, k).wait_send()
        own = PART[r, pl.ds(aligned(net.t * block), block)]
        return own.astype(F32) + RB[r, NEAR].astype(F32) + RB[r, SUMMED].astype(F32)

    def attention_forward(l, r):
        xg = XG[l, r * seq : (r + 1) * seq]
        for c in range(3):
            at = slice(c * n_head, (c + 1) * n_head)
            QKVT[l, r, at] = (dot(WT[l, at], xg, NT) + bcol[l, at]).astype(BF)

        def head(h, carry):
            o = h * HEAD_DIM
            kt = QKVT[l, r, pl.ds(aligned(n_head + o), HEAD_DIM)] * jnp.asarray(HEAD_DIM**-0.5, BF)
            vt = QKVT[l, r, pl.ds(aligned(2 * n_head + o), HEAD_DIM)]
            qt = QKVT[l, r, pl.ds(aligned(o), HEAD_DIM)]
            scores = jnp.where(segc[r] == segr[r], dot(kt, qt, TN), MASKED)
            powers = jnp.exp(scores - jnp.max(scores, axis=0, keepdims=True))
            probs = (powers * (1.0 / jnp.sum(powers, axis=0, keepdims=True))).astype(BF)
            PT[l, r, h] = probs
            CT[l, r, pl.ds(aligned(o), HEAD_DIM)] = dot(vt, probs, NN).astype(BF)
            return carry

        lax.fori_loop(0, heads, head, 0)
        for q in range(2):
            at = slice(q * seq // 2, (q + 1) * seq // 2)
            PART[r, at] = dot(CT[l, r, :, at], WO[l], TN).astype(BF)

    def norm(l, k, r, value):
        centered = value - jnp.mean(value, axis=-1, keepdims=True)
        rstd = lax.rsqrt(jnp.mean(centered * centered, axis=-1, keepdims=True) + EPSILON)
        normal = centered * rstd
        XH[l, k, r] = normal.astype(BF)
        RSTD[l, k, r] = rstd
        return normal * vec[l, 2 + k : 3 + k] + vec[l, 4 + k : 5 + k]

    def first_norm(l, r):
        out = norm(l, 0, r, XRES[r] + sum_end(r) + vec[l, 0:1])
        HRES[r] = out
        HG[l, mine(r)] = out.astype(BF)
        gather_start(HG.at[l], r)

    def ff_forward(l, r):
        hg = HG[l, r * seq : (r + 1) * seq]
        wide = dot(hg, WU[l], NN) + bup[l, 0:1]
        cdf = 0.5 * (1.0 + lax.erf(wide * 0.7071067811865476))
        active = (wide * cdf).astype(BF)
        G[l, r * seq : (r + 1) * seq] = active
        DG[l, r * seq : (r + 1) * seq] = (cdf + wide * 0.3989422804014327 * jnp.exp(-0.5 * wide * wide)).astype(BF)
        PART[r] = dot(G[l, r * seq : (r + 1) * seq], WD[l], NN).astype(BF)

    def second_norm(l, r):
        out = norm(l, 1, r, HRES[r] + sum_end(r) + vec[l, 1:2])
        XRES[r] = out

        @pl.when(l < layers - 1)
        def _():
            XG[l + 1, mine(r)] = out.astype(BF)
            gather_start(XG.at[l + 1], r)

        @pl.when(l == layers - 1)
        def _():
            hidden_out[:, r, :] = out.astype(BF)

    def norm_backward(l, k, r, upstream):
        normal, rstd = XH[l, k, r].astype(F32), RSTD[l, k, r]
        VB[0, l, 2 + k : 3 + k] += jnp.sum(upstream * normal, axis=0, keepdims=True)
        VB[0, l, 4 + k : 5 + k] += jnp.sum(upstream, axis=0, keepdims=True)
        scaled = upstream * vec[l, 2 + k : 3 + k]
        grad = rstd * (
            scaled
            - jnp.mean(scaled, axis=-1, keepdims=True)
            - normal * jnp.mean(scaled * normal, axis=-1, keepdims=True)
        )
        VB[0, l, k : k + 1] += jnp.sum(grad, axis=0, keepdims=True)
        return grad

    def second_norm_backward(l, r, upstream):
        grad = norm_backward(l, 1, r, upstream)
        DH[r] = grad
        DF[mine(r)] = grad.astype(BF)
        gather_start(DF, r)

    def ff_backward(l, r):
        at = slice(r * seq, (r + 1) * seq)
        grad = (dot(DF[at], WD[l], NT) * DG[l, at].astype(F32)).astype(BF)
        DU[at] = grad
        VB[1, l, 0:1, :ff] += jnp.sum(grad.astype(F32), axis=0, keepdims=True)
        PART[r] = dot(DU[at], WU[l], NT).astype(BF)

    def first_norm_backward(l, r):
        grad = norm_backward(l, 0, r, DH[r] + sum_end(r))
        DY[r] = grad
        DG[l, mine(r)] = grad.astype(BF)
        gather_start(DG.at[l], r)

    def attention_backward(l, r):
        DCT[...] = dot(WO[l], DG[l, r * seq : (r + 1) * seq], NT).astype(BF)

        def head(h, carry):
            o = h * HEAD_DIM
            q_at, k_at, v_at = (pl.ds(aligned(c * n_head + o), HEAD_DIM) for c in range(3))
            dct = DCT[q_at]
            probs = PT[l, r, h].astype(F32)
            weighted = probs * dot(QKVT[l, r, v_at], dct, TN)
            inner = jnp.sum(weighted, axis=0, keepdims=True)
            DST[...] = (weighted - probs * inner).astype(BF)
            scale = HEAD_DIM**-0.5
            DPT[r, q_at] = (dot(QKVT[l, r, k_at], DST[...], NN) * scale).astype(BF)
            DPT[r, k_at] = (dot(QKVT[l, r, q_at], DST[...], NT) * scale).astype(BF)
            DPT[r, v_at] = dot(dct, PT[l, r, h], NT).astype(BF)
            return carry

        lax.fori_loop(0, heads, head, 0)
        ones = jnp.ones((8, seq), BF)
        VB[1, l, 1:2, :n_qkv] += dot(ones, DPT[r], NT)[0:1]
        for q in range(2):
            at = slice(q * seq // 2, (q + 1) * seq // 2)
            PART[r, at] = dot(DPT[r, :, at], WT[l], TN).astype(BF)

    per_layer = GR.shape[0] // layers

    def tokens_product(left, right, base):
        def strip(i, carry):
            at = pl.ds(aligned(i * 256, 256), 256)
            GR[pl.ds(aligned(base + i * 256), 256)] = dot(left[:, at], right[...], TN).astype(BF)
            return carry

        lax.fori_loop(0, left.shape[1] // 256, strip, 0)

    def attention_gradients(l, base):
        at = pl.ds(aligned(base), n_qkv)
        GR[at] = sum(dot(DPT[r], XG[l, r * seq : (r + 1) * seq], NN) for r in range(rows)).astype(BF)
        at = pl.ds(aligned(base + n_qkv), n_head)
        GR[at] = sum(dot(CT[l, r], DG[l, r * seq : (r + 1) * seq], NN) for r in range(rows)).astype(BF)

    units = GR.shape[0] // UNIT
    part = UNIT // 2
    half = part // 2
    stages_x, stages_z = [], []
    always = None

    def stage(who_send, who_recv, device, offset, length, landing=None, add=None, staging=None):
        return (who_send, who_recv, device, offset, length, landing, add, staging)

    inner, edge = net.inner, net.edge
    keep, give = net.x * half, (1 - net.x) * half
    stages_x.append(stage(always, always, net.x_dev, give, half, RX0, keep, SX0))
    stages_x.append(stage(edge, inner, net.hop_dev, keep, half, RX1, keep, SX1))
    stages_x.append(stage(inner, inner, net.mid_dev, keep, half, RX2, keep))
    for i, device in enumerate(net.outer_devs):
        stages_x.append(stage(inner, inner, device, keep, half, RXO.at[i], keep))
    stages_x.append(stage(inner, edge, net.hop_dev, keep, half))
    stages_x.append(stage(always, always, net.x_dev, keep, half))
    keep, give = part + net.half * half, part + (1 - net.half) * half
    stages_z.append(stage(edge, inner, net.hop_dev, part, part, RZ0, part, SZ0))
    stages_z.append(stage(inner, inner, net.mid_dev, give, half, RZ1, keep, SZ1))
    stages_z.append(stage(inner, inner, net.x_dev, keep, half, RZ2, keep))
    for i, device in enumerate(net.outer_devs):
        stages_z.append(stage(inner, inner, device, keep, half, RZO.at[i], keep))
    stages_z.append(stage(inner, inner, net.mid_dev, keep, half))
    stages_z.append(stage(inner, edge, net.hop_dev, part, part))
    depth = len(stages_x)
    hops = {0: (stages_z, credit_z), 1: (stages_x, credit_x)}

    def when(condition, body):
        if condition is None:
            body()
        else:
            pl.when(condition)(body)

    def stage_copy(which, s, u):
        _, _, device, offset, length, landing, _, staging = which[0][s]
        src = GR.at[pl.ds(aligned(u * UNIT + offset), length)]
        dst = src if landing is None else landing.at[u % SLOTS]
        src = src if staging is None else staging.at[u % SPACING]
        return remote(src, dst, which[1].at[u, s], which[2].at[u, s], device)

    def credit_of(which, s):
        return hops[s][1] if s in hops and hops[s][0] is which[0] else None

    def stage_send(which, s, u):
        who_send, _, _, offset, length, _, _, staging = which[0][s]

        def send():
            if credit_of(which, s) is not None:

                @pl.when(u >= SLOTS)
                def _():
                    pl.semaphore_wait(credit_of(which, s), 1)

            if staging is not None:
                staging[u % SPACING] = GR[pl.ds(aligned(u * UNIT + offset), length)]
            stage_copy(which, s, u).start()

        when(who_send, send)

    def stage_sent(which, s, u):
        when(which[0][s][0], lambda: stage_copy(which, s, u).wait_send())

    def stage_recv(which, s, u):
        _, who_recv, device, _, length, landing, add, _ = which[0][s]

        def take():
            stage_copy(which, s, u).wait_recv()
            if landing is not None:
                at = pl.ds(aligned(u * UNIT + add), length)
                GR[at] = (GR[at].astype(F32) + landing[u % SLOTS].astype(F32)).astype(BF)
            if credit_of(which, s) is not None:

                @pl.when(u < units - SLOTS)
                def _():
                    pl.semaphore_signal(credit_of(which, s), inc=1, device_id=device, device_id_type=MESH)

        when(who_recv, take)

    both = ((stages_x, arx_s, arx_r), (stages_z, arz_s, arz_r))
    per_units = per_layer // UNIT
    sections = (
        (ff // UNIT, grad_down, 0),
        (2 * ff // UNIT, grad_up, ff),
        (per_units, grad_in, 2 * ff),
        (per_units, grad_out, 2 * ff + n_qkv),
    )
    at_place = (2, 1, 1, 1, 1, 1, 1, 1, 2, 1, 1, 1, 1, 2, 1)
    before = [sum(at_place[:e]) * per_units // sum(at_place) for e in range(len(at_place) + 1)]
    down_done, up_done, all_done = 4, 6, 13
    lag = before[down_done]
    assert before[up_done] <= lag + ff // UNIT and before[all_done] <= lag + 2 * ff // UNIT

    def out_copy(i, k):
        _, out, base = sections[k]
        out = out.at[layers - 1 - i]
        src = GR.at[pl.ds(aligned(i * per_layer + base), out.shape[0])]
        return pltpu.make_async_copy(src, out, osem.at[i, k])

    def unit_done(u):
        i, own = u // per_units, u % per_units
        for k, (end, _, _) in enumerate(sections):

            @pl.when(own == end - 1)
            def _(k=k):
                out_copy(i, k).start()

    def tick(now, carry=0):
        t = now - lag
        for s in range(depth):
            u = t - SPACING * (s + 1)

            @pl.when((u >= 0) & (u < units))
            def _(s=s, u=u):
                for which in both:
                    stage_sent(which, s, u)

        @pl.when((t >= 0) & (t < units))
        def _():
            for which in both:
                stage_send(which, 0, t)

        for s in range(depth):
            u = t - SPACING * (s + 1)

            @pl.when((u >= 0) & (u < units))
            def _(s=s, u=u):
                for which in both:
                    stage_recv(which, s, u)
                    if s + 1 < depth:
                        stage_send(which, s + 1, u)
                if s + 1 == depth:
                    unit_done(u)

        return carry

    for r in range(rows):
        XG[0, mine(r)] = x_in[:, r, :]
        gather_start(XG.at[0], r)

    VB[...] = jnp.zeros(VB.shape, F32)
    diagonal = lax.broadcasted_iota(jnp.int32, (n_head, n_head), 0) == lax.broadcasted_iota(
        jnp.int32, (n_head, n_head), 1
    )
    for l in range(layers):
        vec[l, 0:2] = branch_bias[l].astype(F32)
        vec[l, 2:4] = norm_gain[l].astype(F32)
        vec[l, 4:6] = norm_shift[l].astype(F32)
        bup[l, 0:1] = up_bias[l : l + 1].astype(F32)
        for c, at in ((0, 0), (1, 2 * n_head)):
            spread = jnp.where(diagonal, in_bias[l, c : c + 1].astype(F32), 0.0)
            bcol[l, at : at + n_head] = jnp.sum(spread, axis=1, keepdims=True)
        bcol[l, n_head : 2 * n_head] = jnp.zeros((n_head, 1), F32)
    for r in range(rows):
        for ref, shape, axis in ((segc, (seq, 1), 0), (segr, (1, seq), 1)):
            position = lax.broadcasted_iota(jnp.int32, shape, axis)
            index, end = jnp.zeros(shape, jnp.int32), 0
            for j in range(lengths.shape[1]):
                end = end + lengths[r, j]
                index = index + jnp.where(position >= end, 1, 0)
            ref[r] = jnp.where(position >= seq - padding[r], lengths.shape[1], index)
    for r in range(rows):
        XRES[r] = XG[0, mine(r)].astype(F32)
    for copy in weight_copies:
        copy.wait()

    def half_layer(buf, compute):
        gather_pass(buf, 0)
        gather_end(buf, 0)
        compute(0)
        sum_start(0)
        gather_pass(buf, 1)
        sum_pass(0)
        gather_end(buf, 1)
        compute(1)
        sum_start(1)
        sum_pass(1)

    def forward(l, carry):
        half_layer(XG.at[l], lambda r: attention_forward(l, r))
        for r in range(rows):
            first_norm(l, r)
        half_layer(HG.at[l], lambda r: ff_forward(l, r))
        for r in range(rows):
            second_norm(l, r)
        return carry

    lax.fori_loop(0, layers, forward, 0)

    for r in range(rows):
        second_norm_backward(layers - 1, r, cot[:, r, :].astype(F32))

    def backward(i, carry):
        l = layers - 1 - i
        base = i * per_layer

        def place(e):
            for k in range(before[e], before[e + 1]):
                tick(i * per_units + k)

        place(0)
        gather_pass(DF, 0)
        place(1)
        gather_end(DF, 0)
        ff_backward(l, 0)
        sum_start(0)
        place(2)
        gather_pass(DF, 1)
        sum_pass(0)
        place(3)
        gather_end(DF, 1)
        tokens_product(G.at[l], DF, base)
        place(4)
        ff_backward(l, 1)
        sum_start(1)
        place(5)
        sum_pass(1)
        tokens_product(HG.at[l], DU, base + ff)
        place(6)
        first_norm_backward(l, 0)
        place(7)
        first_norm_backward(l, 1)
        place(8)
        buf = DG.at[l]
        gather_pass(buf, 0)
        place(9)
        gather_end(buf, 0)
        attention_backward(l, 0)
        sum_start(0)
        place(10)
        gather_pass(buf, 1)
        sum_pass(0)
        place(11)
        gather_end(buf, 1)
        attention_backward(l, 1)
        sum_start(1)
        place(12)
        sum_pass(1)
        attention_gradients(l, base + 2 * ff)
        place(13)
        for r in range(rows):
            DY[r] = DY[r] + sum_end(r)

            @pl.when(l > 0)
            def _(r=r):
                second_norm_backward(l - 1, r, DY[r])

            @pl.when(l == 0)
            def _(r=r):
                grad_hidden[:, r, :] = DY[r]

            if r == 0:
                place(14)

        return carry

    lax.fori_loop(0, layers, backward, 0)

    def vector_copy(k):
        if k < 2:
            return remote(VB.at[0], RV.at[k, 0], v_s.at[k], v_r.at[k], (net.core, net.y)[k])
        return remote(VB, RV.at[k], v_s.at[k], v_r.at[k], net.vector_devs[k - 2])

    n_vector = 2 + len(net.vector_devs)
    now, last = layers * per_units, lag + units + SPACING * depth
    for k in range(n_vector + 1):
        if k > 0:
            vector_copy(k - 1).wait()
            if k - 1 < 2:
                VB[0] += RV[k - 1, 0]
            else:
                VB[...] += RV[k - 1]
        if k < n_vector:
            vector_copy(k).start()
        lax.fori_loop(now, now + 2, tick, 0)
        now += 2
    lax.fori_loop(now, last, tick, 0)
    for l in range(layers):
        grad_branch[l] = VB[0, l, 0:2]
        grad_gain[l] = VB[0, l, 2:4]
        grad_shift[l] = VB[0, l, 4:6]
        grad_up_bias[l : l + 1] = VB[1, l, 0:1, :ff]
        for c, at in ((0, 0), (1, 2 * n_head)):
            grad_in_bias[l, c : c + 1] = VB[1, l, 1:2, at : at + n_head]
    for i in range(layers):
        for k in range(len(sections)):
            out_copy(i, k).wait()


def local(
    hidden_in,
    cotangent,
    doc_lengths,
    pad_count,
    input_weight,
    input_bias,
    output_weight,
    up_weight,
    up_bias,
    down_weight,
    branch_bias,
    norm_gain,
    norm_shift,
):
    n_dp = lax.axis_size("dp")
    block, rows, width = hidden_in.shape
    seq = block * lax.axis_size("tensor")
    layers, _, _, n_head = input_weight.shape
    n_qkv, heads, ff = 3 * n_head, n_head // HEAD_DIM, up_weight.shape[2]
    tokens = rows * seq
    wt = jnp.swapaxes(input_weight, 2, 3).reshape(layers, n_qkv, width)
    per_layer = 2 * ff + n_qkv + n_head
    part = UNIT // 2
    outer = 0
    while 8 << outer < n_dp:
        outer += 1
    depth = 5 + outer
    n_vector = 5 + outer
    vmem = pltpu.VMEM
    dma = pltpu.SemaphoreType.DMA
    scratch = [
        vmem((layers, n_qkv, width), BF),
        vmem((layers, n_head, width), BF),
        vmem((layers, width, ff), BF),
        vmem((layers, ff, width), BF),
        vmem((layers, tokens, width), BF),
        vmem((layers, tokens, width), BF),
        vmem((layers, tokens, ff), BF),
        vmem((layers, tokens, ff), BF),
        vmem((tokens, width), BF),
        vmem((tokens, ff), BF),
        vmem((layers, rows, n_qkv, seq), BF),
        vmem((layers, rows, heads, seq, seq), BF),
        vmem((layers, rows, n_head, seq), BF),
        vmem((rows, n_qkv, seq), BF),
        vmem((seq, seq), BF),
        vmem((n_head, seq), BF),
        vmem((rows, seq, width), BF),
        vmem((rows, 3, block, width), BF),
        vmem((rows, block, width), F32),
        vmem((rows, block, width), F32),
        vmem((layers, 2, rows, block, width), BF),
        vmem((layers, 2, rows, block, 1), F32),
        vmem((layers * per_layer, width), BF),
        vmem((SLOTS, part // 2, width), BF),
        vmem((SLOTS, part // 2, width), BF),
        vmem((SLOTS, part // 2, width), BF),
        vmem((SLOTS, part, width), BF),
        vmem((SLOTS, part // 2, width), BF),
        vmem((SLOTS, part // 2, width), BF),
        vmem((max(outer, 1), SLOTS if outer else 1, part // 2, width), BF),
        vmem((max(outer, 1), SLOTS if outer else 1, part // 2, width), BF),
        vmem((SPACING, part // 2, width), BF),
        vmem((SPACING, part // 2, width), BF),
        vmem((SPACING, part, width), BF),
        vmem((SPACING, part // 2, width), BF),
        vmem((2, layers, 8, width), F32),
        vmem((n_vector, 2, layers, 8, width), F32),
        vmem((rows, seq, 1), jnp.int32),
        vmem((rows, 1, seq), jnp.int32),
        vmem((layers, n_qkv, 1), F32),
        vmem((layers, 8, ff), F32),
        vmem((layers, 8, width), F32),
        dma((4,)),
        dma((rows, 3)),
        dma((rows, 3)),
        dma((rows, 3)),
        dma((rows, 3)),
        dma((layers * per_layer // UNIT, depth)),
        dma((layers * per_layer // UNIT, depth)),
        dma((layers * per_layer // UNIT, depth)),
        dma((layers * per_layer // UNIT, depth)),
        dma((n_vector,)),
        dma((n_vector,)),
        dma((layers, 4)),
        pltpu.SemaphoreType.REGULAR,
        pltpu.SemaphoreType.REGULAR,
    ]
    whole, anywhere = pl.BlockSpec(memory_space=vmem), pl.BlockSpec(memory_space=pl.ANY)
    scalars = pl.BlockSpec(memory_space=pltpu.SMEM)
    (
        hidden_out,
        grad_hidden,
        grad_in,
        grad_in_bias,
        grad_out,
        grad_up,
        grad_up_bias,
        grad_down,
        grad_branch,
        grad_gain,
        grad_shift,
    ) = pl.pallas_call(
        functools.partial(kernel, n_dp, layers),
        out_shape=(
            jax.ShapeDtypeStruct(hidden_in.shape, BF),
            jax.ShapeDtypeStruct(hidden_in.shape, F32),
            jax.ShapeDtypeStruct((layers, n_qkv, width), BF),
            jax.ShapeDtypeStruct(input_bias.shape, F32),
            jax.ShapeDtypeStruct(output_weight.shape, BF),
            jax.ShapeDtypeStruct(up_weight.shape, BF),
            jax.ShapeDtypeStruct(up_bias.shape, F32),
            jax.ShapeDtypeStruct(down_weight.shape, BF),
            jax.ShapeDtypeStruct(branch_bias.shape, F32),
            jax.ShapeDtypeStruct(norm_gain.shape, F32),
            jax.ShapeDtypeStruct(norm_shift.shape, F32),
        ),
        in_specs=[whole, whole, scalars, scalars, anywhere, whole, anywhere, anywhere, whole, anywhere]
        + [whole] * 3,
        out_specs=(whole, whole, anywhere, whole, anywhere, anywhere, whole, anywhere, whole, whole, whole),
        scratch_shapes=scratch,
        compiler_params=pltpu.CompilerParams(
            collective_id=0, has_side_effects=True, vmem_limit_bytes=63 << 20
        ),
    )(
        hidden_in,
        cotangent,
        doc_lengths,
        pad_count,
        wt,
        input_bias,
        output_weight,
        up_weight,
        up_bias,
        down_weight,
        branch_bias,
        norm_gain,
        norm_shift,
    )
    grad_in = jnp.swapaxes(grad_in.reshape(layers, 3, n_head, width), 2, 3)
    return (
        hidden_out,
        grad_hidden,
        grad_in.astype(F32),
        grad_in_bias,
        grad_out.astype(F32),
        grad_up.astype(F32),
        grad_up_bias,
        grad_down.astype(F32),
        grad_branch,
        grad_gain,
        grad_shift,
    )


def solution(mesh):
    return jax.shard_map(
        local,
        mesh=mesh,
        in_specs=(
            P("tensor", "dp", None),
            P("tensor", "dp", None),
            P("dp", None),
            P("dp"),
            P(None, None, None, "tensor"),
            P(None, None, "tensor"),
            P(None, "tensor", None),
            P(None, None, "tensor"),
            P(None, "tensor"),
            P(None, "tensor", None),
            P(),
            P(),
            P(),
        ),
        out_specs=(
            P("tensor", "dp", None),
            P("tensor", "dp", None),
            P(None, None, None, "tensor"),
            P(None, None, "tensor"),
            P(None, "tensor", None),
            P(None, None, "tensor"),
            P(None, "tensor"),
            P(None, "tensor", None),
            P(),
            P(),
            P(),
        ),
        check_vma=False,
    )
```

```python
import functools

import jax
import jax.numpy as jnp
from jax import lax
from jax.experimental import pallas as pl
from jax.experimental.pallas import tpu as pltpu
from jax.sharding import PartitionSpec as P

HEAD_DIM = 64
EPSILON = 1e-05
MASKED = -1e30
MESH = pl.DeviceIdType.MESH
BF, F32 = jnp.bfloat16, jnp.float32
NN = (((1,), (0,)), ((), ()))
NT = (((1,), (1,)), ((), ()))
TN = (((0,), (0,)), ((), ()))
UNIT = 128
SPACING, SLOTS = 2, 6


def dot(a, b, dims):
    return lax.dot_general(a, b, dims, preferred_element_type=F32)


def aligned(value, by=16):
    return pl.multiple_of(value, by)


class Net:
    def __init__(self, n_dp):
        dp, t = lax.axis_index("dp"), lax.axis_index("tensor")
        self.dp, self.t = dp, t
        y, c = t // 2, t % 2
        self.t_core = t + 1 - 2 * c
        self.t_y = t + 2 - 4 * y
        self.t_far = 3 - t
        self.core, self.y = (dp, self.t_core), (dp, self.t_y)
        self.x = dp % 2
        z = (dp // 2) % 4
        self.half = z // 2
        self.inner = (z == 1) | (z == 2)
        self.inner_count = (z + 1) // 2 % 2
        self.edge = (z == 0) | (z == 3)
        self.x_dev = (dp + 1 - 2 * self.x, t)
        self.hop_dev = (dp + 2 * (1 - 2 * (z % 2)), t)
        self.mid_dev = (dp + 2 * (3 - 2 * z), t)
        self.outer_devs = []
        step = 8
        while step < n_dp:
            self.outer_devs.append((dp + step * (1 - 2 * ((dp // step) % 2)), t))
            step *= 2
        self.partners = [self.core, self.y, self.x_dev, self.hop_dev]
        self.inner_partners = [self.mid_dev] + self.outer_devs


def remote(src, dst, send, recv, device):
    return pltpu.make_async_remote_copy(
        src_ref=src, dst_ref=dst, send_sem=send, recv_sem=recv, device_id=device, device_id_type=MESH
    )


def kernel(n_dp, layers, *refs):
    (x_in, cot, lengths, padding, wt_h, in_bias, wo_h, wu_h, up_bias, wd_h, branch_bias, norm_gain, norm_shift,
     hidden_out, grad_hidden, grad_in, grad_out, grad_up, grad_down, small,
     WT, WO, WU, WD, XG, HG, G, DG, DF, DU, QKVT, PT, CT, DPT, DST, DCT, PART, RB, XRES, HRES, XH, RSTD, GR,
     RX0, RX1, RX2, RZ0, RZ1, RZ2, RXO, RZO, SX0, SX1, SZ0, SZ1, VB, RV, segc, segr, bcol, bup, vec,
     wsem, ag_s, ag_r, rs_s, rs_r, arx_s, arx_r, arz_s, arz_r, v_s, v_r, osem, credit_x, credit_z) = refs
    DY, DH = XRES, HRES
    net = Net(n_dp)
    block, rows, width = x_in.shape
    seq = PART.shape[1]
    n_qkv = WT.shape[1]
    n_head = n_qkv // 3
    heads = n_head // HEAD_DIM
    ff = WU.shape[2]

    weight_copies = [
        pltpu.make_async_copy(a, b, wsem.at[i])
        for i, (a, b) in enumerate(((wt_h, WT), (wo_h, WO), (wu_h, WU), (wd_h, WD)))
    ]
    for copy in weight_copies:
        copy.start()

    barrier = pltpu.get_barrier_semaphore()
    for device in net.partners:
        pl.semaphore_signal(barrier, inc=1, device_id=device, device_id_type=MESH)

    @pl.when(net.inner)
    def _():
        for device in net.inner_partners:
            pl.semaphore_signal(barrier, inc=1, device_id=device, device_id_type=MESH)

    pl.semaphore_wait(barrier, len(net.partners) + net.inner_count * len(net.inner_partners))

    def rows_at(r, t):
        return pl.ds(aligned(r * seq + t * block), block)

    def mine(r):
        return rows_at(r, net.t)

    ALONG, ACROSS, ONWARD = 0, 1, 2

    def gather_copy(buf, r, k):
        block = buf.at[rows_at(r, net.t_y if k == ONWARD else net.t)]
        return remote(block, block, ag_s.at[r, k], ag_r.at[r, k], net.y if k == ALONG else net.core)

    def gather_start(buf, r):
        gather_copy(buf, r, ALONG).start()
        gather_copy(buf, r, ACROSS).start()

    def gather_pass(buf, r):
        gather_copy(buf, r, ALONG).wait_recv()
        gather_copy(buf, r, ONWARD).start()

    def gather_end(buf, r):
        gather_copy(buf, r, ACROSS).wait_recv()
        gather_copy(buf, r, ONWARD).wait_recv()
        for k in (ALONG, ACROSS, ONWARD):
            gather_copy(buf, r, k).wait_send()

    FAR, NEAR, SUMMED = 0, 1, 2

    def sum_copy(r, k):
        block_of = (net.t_far, net.t_core, net.t_y)[k]
        src = PART.at[r, pl.ds(aligned(block_of * block), block)]
        return remote(src, RB.at[r, k], rs_s.at[r, k], rs_r.at[r, k], net.y if k == SUMMED else net.core)

    def sum_start(r):
        sum_copy(r, FAR).start()
        sum_copy(r, NEAR).start()

    def sum_pass(r):
        sum_copy(r, FAR).wait_recv()
        at = pl.ds(aligned(net.t_y * block), block)
        PART[r, at] = (PART[r, at].astype(F32) + RB[r, FAR].astype(F32)).astype(BF)
        sum_copy(r, SUMMED).start()

    def sum_end(r):
        sum_copy(r, NEAR).wait_recv()
        sum_copy(r, SUMMED).wait_recv()
        for k in (FAR, NEAR, SUMMED):
            sum_copy(r, k).wait_send()
        own = PART[r, pl.ds(aligned(net.t * block), block)]
        return own.astype(F32) + RB[r, NEAR].astype(F32) + RB[r, SUMMED].astype(F32)

    def attention_forward(l, r):
        xg = XG[l, r * seq : (r + 1) * seq]
        for c in range(3):
            at = slice(c * n_head, (c + 1) * n_head)
            QKVT[l, r, at] = (dot(WT[l, at], xg, NT) + bcol[l, at]).astype(BF)

        def head(h, carry):
            o = h * HEAD_DIM
            kt = QKVT[l, r, pl.ds(aligned(n_head + o), HEAD_DIM)] * jnp.asarray(HEAD_DIM**-0.5, BF)
            vt = QKVT[l, r, pl.ds(aligned(2 * n_head + o), HEAD_DIM)]
            qt = QKVT[l, r, pl.ds(aligned(o), HEAD_DIM)]
            scores = jnp.where(segc[r] == segr[r], dot(kt, qt, TN), MASKED)
            powers = jnp.exp(scores - jnp.max(scores, axis=0, keepdims=True))
            probs = (powers * (1.0 / jnp.sum(powers, axis=0, keepdims=True))).astype(BF)
            PT[l, r, h] = probs
            CT[l, r, pl.ds(aligned(o), HEAD_DIM)] = dot(vt, probs, NN).astype(BF)
            return carry

        lax.fori_loop(0, heads, head, 0)
        for q in range(2):
            at = slice(q * seq // 2, (q + 1) * seq // 2)
            PART[r, at] = dot(CT[l, r, :, at], WO[l], TN).astype(BF)

    def norm(l, k, r, value):
        centered = value - jnp.mean(value, axis=-1, keepdims=True)
        rstd = lax.rsqrt(jnp.mean(centered * centered, axis=-1, keepdims=True) + EPSILON)
        normal = centered * rstd
        XH[l, k, r] = normal.astype(BF)
        RSTD[l, k, r] = rstd
        return normal * vec[l, 2 + k : 3 + k] + vec[l, 4 + k : 5 + k]

    def first_norm(l, r):
        out = norm(l, 0, r, XRES[r] + sum_end(r) + vec[l, 0:1])
        HRES[r] = out
        HG[l, mine(r)] = out.astype(BF)
        gather_start(HG.at[l], r)

    def ff_forward(l, r):
        hg = HG[l, r * seq : (r + 1) * seq]
        wide = dot(hg, WU[l], NN) + bup[l, 0:1]
        cdf = 0.5 * (1.0 + lax.erf(wide * 0.7071067811865476))
        active = (wide * cdf).astype(BF)
        G[l, r * seq : (r + 1) * seq] = active
        DG[l, r * seq : (r + 1) * seq] = (cdf + wide * 0.3989422804014327 * jnp.exp(-0.5 * wide * wide)).astype(BF)
        PART[r] = dot(G[l, r * seq : (r + 1) * seq], WD[l], NN).astype(BF)

    def second_norm(l, r):
        out = norm(l, 1, r, HRES[r] + sum_end(r) + vec[l, 1:2])
        XRES[r] = out

        @pl.when(l < layers - 1)
        def _():
            XG[l + 1, mine(r)] = out.astype(BF)
            gather_start(XG.at[l + 1], r)

        @pl.when(l == layers - 1)
        def _():
            hidden_out[:, r, :] = out.astype(BF)

    def norm_backward(l, k, r, upstream):
        normal, rstd = XH[l, k, r].astype(F32), RSTD[l, k, r]
        VB[0, l, 2 + k : 3 + k] += jnp.sum(upstream * normal, axis=0, keepdims=True)
        VB[0, l, 4 + k : 5 + k] += jnp.sum(upstream, axis=0, keepdims=True)
        scaled = upstream * vec[l, 2 + k : 3 + k]
        grad = rstd * (
            scaled
            - jnp.mean(scaled, axis=-1, keepdims=True)
            - normal * jnp.mean(scaled * normal, axis=-1, keepdims=True)
        )
        VB[0, l, k : k + 1] += jnp.sum(grad, axis=0, keepdims=True)
        return grad

    def second_norm_backward(l, r, upstream):
        grad = norm_backward(l, 1, r, upstream)
        DH[r] = grad
        DF[mine(r)] = grad.astype(BF)
        gather_start(DF, r)

    def ff_backward(l, r):
        at = slice(r * seq, (r + 1) * seq)
        grad = (dot(DF[at], WD[l], NT) * DG[l, at].astype(F32)).astype(BF)
        DU[at] = grad
        VB[1, l, 0:1, :ff] += jnp.sum(grad.astype(F32), axis=0, keepdims=True)
        PART[r] = dot(DU[at], WU[l], NT).astype(BF)

    def first_norm_backward(l, r):
        grad = norm_backward(l, 0, r, DH[r] + sum_end(r))
        DY[r] = grad
        DG[l, mine(r)] = grad.astype(BF)
        gather_start(DG.at[l], r)

    def attention_backward(l, r):
        DCT[...] = dot(WO[l], DG[l, r * seq : (r + 1) * seq], NT).astype(BF)

        def head(h, carry):
            o = h * HEAD_DIM
            q_at, k_at, v_at = (pl.ds(aligned(c * n_head + o), HEAD_DIM) for c in range(3))
            dct = DCT[q_at]
            probs = PT[l, r, h].astype(F32)
            weighted = probs * dot(QKVT[l, r, v_at], dct, TN)
            inner = jnp.sum(weighted, axis=0, keepdims=True)
            DST[...] = (weighted - probs * inner).astype(BF)
            scale = HEAD_DIM**-0.5
            DPT[r, q_at] = (dot(QKVT[l, r, k_at], DST[...], NN) * scale).astype(BF)
            DPT[r, k_at] = (dot(QKVT[l, r, q_at], DST[...], NT) * scale).astype(BF)
            DPT[r, v_at] = dot(dct, PT[l, r, h], NT).astype(BF)
            return carry

        lax.fori_loop(0, heads, head, 0)
        ones = jnp.ones((8, seq), BF)
        VB[1, l, 1:2, :n_qkv] += dot(ones, DPT[r], NT)[0:1]
        for q in range(2):
            at = slice(q * seq // 2, (q + 1) * seq // 2)
            PART[r, at] = dot(DPT[r, :, at], WT[l], TN).astype(BF)

    per_layer = 2 * ff + n_qkv + n_head

    def tokens_product(left, right, base):
        def strip(i, carry):
            at = pl.ds(aligned(i * 256, 256), 256)
            GR[pl.ds(aligned(base + i * 256), 256)] = dot(left[:, at], right[...], TN).astype(BF)
            return carry

        lax.fori_loop(0, left.shape[1] // 256, strip, 0)

    def attention_gradients(l, base):
        at = pl.ds(aligned(base), n_qkv)
        GR[at] = sum(dot(DPT[r], XG[l, r * seq : (r + 1) * seq], NN) for r in range(rows)).astype(BF)
        at = pl.ds(aligned(base + n_qkv), n_head)
        GR[at] = sum(dot(CT[l, r], DG[l, r * seq : (r + 1) * seq], NN) for r in range(rows)).astype(BF)

    units = layers * per_layer // UNIT
    part = UNIT // 2
    half = part // 2
    stages_x, stages_z = [], []
    always = None

    def stage(who_send, who_recv, device, offset, length, landing=None, add=None, staging=None):
        return (who_send, who_recv, device, offset, length, landing, add, staging)

    inner, edge = net.inner, net.edge
    keep, give = net.x * half, (1 - net.x) * half
    stages_x.append(stage(always, always, net.x_dev, give, half, RX0, keep, SX0))
    stages_x.append(stage(edge, inner, net.hop_dev, keep, half, RX1, keep, SX1))
    stages_x.append(stage(inner, inner, net.mid_dev, keep, half, RX2, keep))
    for i, device in enumerate(net.outer_devs):
        stages_x.append(stage(inner, inner, device, keep, half, RXO.at[i], keep))
    stages_x.append(stage(inner, edge, net.hop_dev, keep, half))
    stages_x.append(stage(always, always, net.x_dev, keep, half))
    keep, give = part + net.half * half, part + (1 - net.half) * half
    stages_z.append(stage(edge, inner, net.hop_dev, part, part, RZ0, part, SZ0))
    stages_z.append(stage(inner, inner, net.mid_dev, give, half, RZ1, keep, SZ1))
    stages_z.append(stage(inner, inner, net.x_dev, keep, half, RZ2, keep))
    for i, device in enumerate(net.outer_devs):
        stages_z.append(stage(inner, inner, device, keep, half, RZO.at[i], keep))
    stages_z.append(stage(inner, inner, net.mid_dev, keep, half))
    stages_z.append(stage(inner, edge, net.hop_dev, part, part))
    depth = len(stages_x)
    hops = {0: (stages_z, credit_z), 1: (stages_x, credit_x)}

    def when(condition, body):
        if condition is None:
            body()
        else:
            pl.when(condition)(body)

    def stage_copy(which, s, u):
        _, _, device, offset, length, landing, _, staging = which[0][s]
        src = GR.at[pl.ds(aligned(u * UNIT + offset), length)]
        dst = src if landing is None else landing.at[u % SLOTS]
        src = src if staging is None else staging.at[u % SPACING]
        return remote(src, dst, which[1].at[u, s], which[2].at[u, s], device)

    def last_of(which):
        return units if which[0] is stages_x else units - 1

    def live(which, u):
        return (u >= 0) & (u <= last_of(which))

    def credit_of(which, s):
        return hops[s][1] if s in hops and hops[s][0] is which[0] else None

    def stage_send(which, s, u):
        who_send, _, _, offset, length, _, _, staging = which[0][s]

        def send():
            if credit_of(which, s) is not None:

                @pl.when(u >= SLOTS)
                def _():
                    pl.semaphore_wait(credit_of(which, s), 1)

            if staging is not None:
                staging[u % SPACING] = GR[pl.ds(aligned(u * UNIT + offset), length)]
            stage_copy(which, s, u).start()

        when(who_send, send)

    def stage_sent(which, s, u):
        when(which[0][s][0], lambda: stage_copy(which, s, u).wait_send())

    def stage_recv(which, s, u):
        _, who_recv, device, _, length, landing, add, _ = which[0][s]

        def take():
            stage_copy(which, s, u).wait_recv()
            if landing is not None:
                at = pl.ds(aligned(u * UNIT + add), length)
                GR[at] = (GR[at].astype(F32) + landing[u % SLOTS].astype(F32)).astype(BF)
            if credit_of(which, s) is not None:

                @pl.when(u < last_of(which) + 1 - SLOTS)
                def _():
                    pl.semaphore_signal(credit_of(which, s), inc=1, device_id=device, device_id_type=MESH)

        when(who_recv, take)

    both = ((stages_x, arx_s, arx_r), (stages_z, arz_s, arz_r))
    per_units = per_layer // UNIT
    sections = (
        (ff // UNIT, grad_down, 0),
        (2 * ff // UNIT, grad_up, ff),
        (per_units, grad_in, 2 * ff),
        (per_units, grad_out, 2 * ff + n_qkv),
    )
    at_place = (2, 1, 1, 1, 1, 1, 1, 1, 2, 1, 1, 1, 1, 2, 1)
    before = [sum(at_place[:e]) * per_units // sum(at_place) for e in range(len(at_place) + 1)]
    down_done, up_done, all_done = 4, 6, 13
    lag = before[down_done]
    assert before[up_done] <= lag + ff // UNIT and before[all_done] <= lag + 2 * ff // UNIT

    def out_copy(i, k):
        _, out, base = sections[k]
        out = out.at[layers - 1 - i]
        src = GR.at[pl.ds(aligned(i * per_layer + base), out.shape[0])]
        return pltpu.make_async_copy(src, out, osem.at[i, k])

    def unit_done(u):
        i, own = u // per_units, u % per_units
        for k, (end, _, _) in enumerate(sections):

            @pl.when((own == end - 1) & (u < units))
            def _(k=k):
                out_copy(i, k).start()

    def tick(now, carry=0):
        t = now - lag
        for s in range(depth):
            u = t - SPACING * (s + 1)
            for which in both:
                pl.when(live(which, u))(functools.partial(stage_sent, which, s, u))
        for which in both:
            pl.when(live(which, t))(functools.partial(stage_send, which, 0, t))
        for s in range(depth):
            u = t - SPACING * (s + 1)
            for which in both:

                @pl.when(live(which, u))
                def _(which=which, s=s, u=u):
                    stage_recv(which, s, u)
                    if s + 1 < depth:
                        stage_send(which, s + 1, u)

        u = t - SPACING * depth
        pl.when((u >= 0) & (u < units))(functools.partial(unit_done, u))
        return carry

    for r in range(rows):
        XG[0, mine(r)] = x_in[:, r, :]
        gather_start(XG.at[0], r)

    VB[...] = jnp.zeros(VB.shape, F32)
    diagonal = lax.broadcasted_iota(jnp.int32, (n_head, n_head), 0) == lax.broadcasted_iota(
        jnp.int32, (n_head, n_head), 1
    )
    for l in range(layers):
        vec[l, 0:2] = branch_bias[l].astype(F32)
        vec[l, 2:4] = norm_gain[l].astype(F32)
        vec[l, 4:6] = norm_shift[l].astype(F32)
        bup[l, 0:1] = up_bias[l : l + 1].astype(F32)
        for c, at in ((0, 0), (1, 2 * n_head)):
            spread = jnp.where(diagonal, in_bias[l, c : c + 1].astype(F32), 0.0)
            bcol[l, at : at + n_head] = jnp.sum(spread, axis=1, keepdims=True)
        bcol[l, n_head : 2 * n_head] = jnp.zeros((n_head, 1), F32)
    for r in range(rows):
        for ref, shape, axis in ((segc, (seq, 1), 0), (segr, (1, seq), 1)):
            position = lax.broadcasted_iota(jnp.int32, shape, axis)
            index, end = jnp.zeros(shape, jnp.int32), 0
            for j in range(lengths.shape[1]):
                end = end + lengths[r, j]
                index = index + jnp.where(position >= end, 1, 0)
            ref[r] = jnp.where(position >= seq - padding[r], lengths.shape[1], index)
    for r in range(rows):
        XRES[r] = XG[0, mine(r)].astype(F32)
    for copy in weight_copies:
        copy.wait()

    def half_layer(buf, compute):
        gather_pass(buf, 0)
        gather_end(buf, 0)
        compute(0)
        sum_start(0)
        gather_pass(buf, 1)
        sum_pass(0)
        gather_end(buf, 1)
        compute(1)
        sum_start(1)
        sum_pass(1)

    def forward(l, carry):
        half_layer(XG.at[l], lambda r: attention_forward(l, r))
        for r in range(rows):
            first_norm(l, r)
        half_layer(HG.at[l], lambda r: ff_forward(l, r))
        for r in range(rows):
            second_norm(l, r)
        return carry

    lax.fori_loop(0, layers, forward, 0)

    for r in range(rows):
        second_norm_backward(layers - 1, r, cot[:, r, :].astype(F32))

    def backward(i, carry):
        l = layers - 1 - i
        base = i * per_layer

        def place(e):
            for k in range(before[e], before[e + 1]):
                tick(i * per_units + k)

        place(0)
        gather_pass(DF, 0)
        place(1)
        gather_end(DF, 0)
        ff_backward(l, 0)
        sum_start(0)
        place(2)
        gather_pass(DF, 1)
        sum_pass(0)
        place(3)
        gather_end(DF, 1)
        tokens_product(G.at[l], DF, base)
        place(4)
        ff_backward(l, 1)
        sum_start(1)
        place(5)
        sum_pass(1)
        tokens_product(HG.at[l], DU, base + ff)
        place(6)
        first_norm_backward(l, 0)
        place(7)
        first_norm_backward(l, 1)
        place(8)
        buf = DG.at[l]
        gather_pass(buf, 0)
        place(9)
        gather_end(buf, 0)
        attention_backward(l, 0)
        sum_start(0)
        place(10)
        gather_pass(buf, 1)
        sum_pass(0)
        place(11)
        gather_end(buf, 1)
        attention_backward(l, 1)
        sum_start(1)
        place(12)
        sum_pass(1)
        attention_gradients(l, base + 2 * ff)
        place(13)
        for r in range(rows):
            DY[r] = DY[r] + sum_end(r)

            @pl.when(l > 0)
            def _(r=r):
                second_norm_backward(l - 1, r, DY[r])

            @pl.when(l == 0)
            def _(r=r):
                grad_hidden[:, r, :] = DY[r]

            if r == 0:
                place(14)

        return carry

    lax.fori_loop(0, layers, backward, 0)

    def vector_copy(k):
        return remote(VB.at[0], RV.at[k], v_s.at[k], v_r.at[k], (net.core, net.y)[k])

    now = layers * per_units
    for k in range(2):
        vector_copy(k).start()
        lax.fori_loop(now, now + min(1, lag // 2), tick, 0)
        now += min(1, lag // 2)
        vector_copy(k).wait()
        VB[0] += RV[k]
    base = layers * per_layer
    GR[base : base + UNIT] = jnp.zeros((UNIT, width), BF)
    GR[base : base + 16 * layers] = VB[...].reshape(16 * layers, width).astype(BF)
    lax.fori_loop(now, lag + units + 1 + SPACING * depth, tick, 0)
    small[...] = GR[base : base + 16 * layers].astype(F32)
    for i in range(layers):
        for k in range(len(sections)):
            out_copy(i, k).wait()


def local(
    hidden_in,
    cotangent,
    doc_lengths,
    pad_count,
    input_weight,
    input_bias,
    output_weight,
    up_weight,
    up_bias,
    down_weight,
    branch_bias,
    norm_gain,
    norm_shift,
):
    n_dp = lax.axis_size("dp")
    block, rows, width = hidden_in.shape
    seq = block * lax.axis_size("tensor")
    layers, _, _, n_head = input_weight.shape
    n_qkv, heads, ff = 3 * n_head, n_head // HEAD_DIM, up_weight.shape[2]
    tokens = rows * seq
    wt = jnp.swapaxes(input_weight, 2, 3).reshape(layers, n_qkv, width)
    per_layer = 2 * ff + n_qkv + n_head
    part = UNIT // 2
    outer = 0
    while 8 << outer < n_dp:
        outer += 1
    depth = 5 + outer
    vmem = pltpu.VMEM
    dma = pltpu.SemaphoreType.DMA
    scratch = [
        vmem((layers, n_qkv, width), BF),
        vmem((layers, n_head, width), BF),
        vmem((layers, width, ff), BF),
        vmem((layers, ff, width), BF),
        vmem((layers, tokens, width), BF),
        vmem((layers, tokens, width), BF),
        vmem((layers, tokens, ff), BF),
        vmem((layers, tokens, ff), BF),
        vmem((tokens, width), BF),
        vmem((tokens, ff), BF),
        vmem((layers, rows, n_qkv, seq), BF),
        vmem((layers, rows, heads, seq, seq), BF),
        vmem((layers, rows, n_head, seq), BF),
        vmem((rows, n_qkv, seq), BF),
        vmem((seq, seq), BF),
        vmem((n_head, seq), BF),
        vmem((rows, seq, width), BF),
        vmem((rows, 3, block, width), BF),
        vmem((rows, block, width), F32),
        vmem((rows, block, width), F32),
        vmem((layers, 2, rows, block, width), BF),
        vmem((layers, 2, rows, block, 1), F32),
        vmem((layers * per_layer + UNIT, width), BF),
        vmem((SLOTS, part // 2, width), BF),
        vmem((SLOTS, part // 2, width), BF),
        vmem((SLOTS, part // 2, width), BF),
        vmem((SLOTS, part, width), BF),
        vmem((SLOTS, part // 2, width), BF),
        vmem((SLOTS, part // 2, width), BF),
        vmem((max(outer, 1), SLOTS if outer else 1, part // 2, width), BF),
        vmem((max(outer, 1), SLOTS if outer else 1, part // 2, width), BF),
        vmem((SPACING, part // 2, width), BF),
        vmem((SPACING, part // 2, width), BF),
        vmem((SPACING, part, width), BF),
        vmem((SPACING, part // 2, width), BF),
        vmem((2, layers, 8, width), F32),
        vmem((2, layers, 8, width), F32),
        vmem((rows, seq, 1), jnp.int32),
        vmem((rows, 1, seq), jnp.int32),
        vmem((layers, n_qkv, 1), F32),
        vmem((layers, 8, ff), F32),
        vmem((layers, 8, width), F32),
        dma((4,)),
        dma((rows, 3)),
        dma((rows, 3)),
        dma((rows, 3)),
        dma((rows, 3)),
        dma((layers * per_layer // UNIT + 1, depth)),
        dma((layers * per_layer // UNIT + 1, depth)),
        dma((layers * per_layer // UNIT + 1, depth)),
        dma((layers * per_layer // UNIT + 1, depth)),
        dma((2,)),
        dma((2,)),
        dma((layers, 4)),
        pltpu.SemaphoreType.REGULAR,
        pltpu.SemaphoreType.REGULAR,
    ]
    whole, anywhere = pl.BlockSpec(memory_space=vmem), pl.BlockSpec(memory_space=pl.ANY)
    scalars = pl.BlockSpec(memory_space=pltpu.SMEM)
    results = pl.pallas_call(
        functools.partial(kernel, n_dp, layers),
        out_shape=(
            jax.ShapeDtypeStruct(hidden_in.shape, BF),
            jax.ShapeDtypeStruct(hidden_in.shape, F32),
            jax.ShapeDtypeStruct((layers, n_qkv, width), BF),
            jax.ShapeDtypeStruct(output_weight.shape, BF),
            jax.ShapeDtypeStruct(up_weight.shape, BF),
            jax.ShapeDtypeStruct(down_weight.shape, BF),
            jax.ShapeDtypeStruct((16 * layers, width), F32),
        ),
        in_specs=[whole, whole, scalars, scalars, anywhere, whole, anywhere, anywhere, whole, anywhere]
        + [whole] * 3,
        out_specs=(whole, whole, anywhere, anywhere, anywhere, anywhere, whole),
        scratch_shapes=scratch,
        compiler_params=pltpu.CompilerParams(
            collective_id=0, has_side_effects=True, vmem_limit_bytes=63 << 20
        ),
    )(
        hidden_in,
        cotangent,
        doc_lengths,
        pad_count,
        wt,
        input_bias,
        output_weight,
        up_weight,
        up_bias,
        down_weight,
        branch_bias,
        norm_gain,
        norm_shift,
    )
    pieces = 4

    def strip(array):
        return pl.BlockSpec((1, array.shape[1] // pieces, width), lambda l, c: (l, c, 0))

    strips = [strip(array) for array in results[2:6]]
    fixed = [
        jax.ShapeDtypeStruct(shape, F32)
        for shape in (input_bias.shape, up_bias.shape, branch_bias.shape, norm_gain.shape, norm_shift.shape)
    ]
    hidden_out, grad_hidden, grad_in, grad_out, grad_up, grad_down, *vectors = pl.pallas_call(
        functools.partial(finish, layers, pieces),
        grid=(layers, pieces),
        out_shape=[jax.ShapeDtypeStruct(array.shape, array.dtype) for array in results[:2]]
        + [jax.ShapeDtypeStruct(array.shape, F32) for array in results[2:6]]
        + fixed,
        in_specs=[whole] * 2 + strips + [whole],
        out_specs=[whole] * 2 + strips + [whole] * 5,
    )(*results)
    grad_in_bias, grad_up_bias, grad_branch, grad_gain, grad_shift = vectors
    grad_in = jnp.swapaxes(grad_in.reshape(layers, 3, n_head, width), 2, 3)
    return (
        hidden_out,
        grad_hidden,
        grad_in,
        grad_in_bias,
        grad_out,
        grad_up,
        grad_up_bias,
        grad_down,
        grad_branch,
        grad_gain,
        grad_shift,
    )


def finish(layers, pieces, *refs):
    hidden, grad_hidden, *grads = refs[:6]
    small = refs[6]
    hidden_out, grad_hidden_out, *outs = refs[7:13]
    grad_in_bias, grad_up_bias, grad_branch, grad_gain, grad_shift = refs[13:18]
    step = pl.program_id(0) * pieces + pl.program_id(1)

    @pl.when(step == 0)
    def _():
        hidden_out[...] = hidden[...]
        grad_hidden_out[...] = grad_hidden[...]
        n_head, ff = grad_in_bias.shape[2], grad_up_bias.shape[1]
        for l in range(layers):
            shared, split = 8 * l, 8 * (layers + l)
            grad_branch[l] = small[shared : shared + 2]
            grad_gain[l] = small[shared + 2 : shared + 4]
            grad_shift[l] = small[shared + 4 : shared + 6]
            grad_up_bias[l : l + 1] = small[split : split + 1, :ff]
            for c in range(2):
                grad_in_bias[l, c : c + 1] = small[split + 1 : split + 2, 2 * c * n_head : (2 * c + 1) * n_head]

    for grad, out in zip(grads, outs, strict=True):
        out[...] = grad[...].astype(F32)


def solution(mesh):
    return jax.shard_map(
        local,
        mesh=mesh,
        in_specs=(
            P("tensor", "dp", None),
            P("tensor", "dp", None),
            P("dp", None),
            P("dp"),
            P(None, None, None, "tensor"),
            P(None, None, "tensor"),
            P(None, "tensor", None),
            P(None, None, "tensor"),
            P(None, "tensor"),
            P(None, "tensor", None),
            P(),
            P(),
            P(),
        ),
        out_specs=(
            P("tensor", "dp", None),
            P("tensor", "dp", None),
            P(None, None, None, "tensor"),
            P(None, None, "tensor"),
            P(None, "tensor", None),
            P(None, None, "tensor"),
            P(None, "tensor"),
            P(None, "tensor", None),
            P(),
            P(),
            P(),
        ),
        check_vma=False,
    )
```

```python
import functools

import jax
import jax.numpy as jnp
from jax import lax
from jax.experimental import pallas as pl
from jax.experimental.pallas import tpu as pltpu
from jax.sharding import PartitionSpec as P

HEAD_DIM = 64
EPSILON = 1e-05
MASKED = -1e30
MESH = pl.DeviceIdType.MESH
BF, F32 = jnp.bfloat16, jnp.float32
NN = (((1,), (0,)), ((), ()))
NT = (((1,), (1,)), ((), ()))
TN = (((0,), (0,)), ((), ()))
UNIT = 128
SPACING, SLOTS = 2, 6


def dot(a, b, dims):
    return lax.dot_general(a, b, dims, preferred_element_type=F32)


def aligned(value, by=16):
    return pl.multiple_of(value, by)


class Net:
    def __init__(self, n_dp):
        dp, t = lax.axis_index("dp"), lax.axis_index("tensor")
        self.dp, self.t = dp, t
        self.own, self.c = t // 2, t % 2
        self.other = 1 - self.own
        self.core, self.y = (dp, t + 1 - 2 * self.c), (dp, t + 2 - 4 * self.own)
        self.x = dp % 2
        self.z = z = (dp // 2) % 4
        self.half = z // 2
        self.inner = (z == 1) | (z == 2)
        self.inner_count = (z + 1) // 2 % 2
        self.edge = (z == 0) | (z == 3)
        self.x_dev = (dp + 1 - 2 * self.x, t)
        self.hop_dev = (dp + 2 * (1 - 2 * (z % 2)), t)
        self.mid_dev = (dp + 2 * (3 - 2 * z), t)
        self.outer_devs = []
        step = 8
        while step < n_dp:
            self.outer_devs.append((dp + step * (1 - 2 * ((dp // step) % 2)), t))
            step *= 2
        self.partners = [self.core, self.y, self.x_dev, self.hop_dev]
        self.inner_partners = [self.mid_dev] + self.outer_devs


def remote(src, dst, send, recv, device):
    return pltpu.make_async_remote_copy(
        src_ref=src, dst_ref=dst, send_sem=send, recv_sem=recv, device_id=device, device_id_type=MESH
    )


def kernel(n_dp, layers, *refs):
    (x_in, cot, lengths, padding, wt_h, in_bias, wo_h, wu_h, up_bias, wd_h, branch_bias, norm_gain, norm_shift,
     hidden_out, grad_hidden, grad_in, grad_out, grad_up, grad_down, small,
     WT, WO, WU, WD, XG, HG, G, DG, DF, DU, QKVT, PT, CT, DPT, DST, DCT, PART, RB, XRES, HRES, XH, RSTD, GR,
     RX0, RX1, RX2, RZ0, RZ1, RZ2, RXO, RZO, SX0, SX1, SZ0, SZ1, VB, RV, segc, segr, bcol, bcol_y, bup, vec,
     BS, BY, CB, YB,
     wsem, ag_s, ag_r, rs_s, rs_r, arx_s, arx_r, arz_s, arz_r, v_s, v_r, osem, credit_x, credit_z,
     wg_s, wg_r, ex_s, ex_r) = refs
    DY, DH = XRES, HRES
    net = Net(n_dp)
    block, rows, width = x_in.shape
    seq = PART.shape[1]
    half_seq = seq // 2
    own, other, core = net.own, net.other, net.c
    last = layers - 1
    n_qkv = WT.shape[1]
    n_head = n_qkv // 3
    heads = n_head // HEAD_DIM
    ff = WU.shape[2]

    weight_copies = [
        pltpu.make_async_copy(a, b, wsem.at[i])
        for i, (a, b) in enumerate(((wt_h, WT), (wo_h, WO), (wu_h, WU), (wd_h, WD)))
    ]
    for copy in weight_copies:
        copy.start()

    barrier = pltpu.get_barrier_semaphore()
    for device in net.partners:
        pl.semaphore_signal(barrier, inc=1, device_id=device, device_id_type=MESH)

    @pl.when(net.inner)
    def _():
        for device in net.inner_partners:
            pl.semaphore_signal(barrier, inc=1, device_id=device, device_id_type=MESH)

    pl.semaphore_wait(barrier, len(net.partners) + net.inner_count * len(net.inner_partners))

    def rows_of(r, start, size):
        return pl.ds(aligned(r * seq + start), size)

    def piece(r, c, k):
        return rows_of(r, c * half_seq + k * block, block)

    ALONG, ACROSS, ONWARD = 0, 1, 2
    INPUT, USUAL, LAYER_IN, FF_IN = range(4)

    def gather_copy(group, buf, k, kind):
        if group == INPUT:
            first, second = (other, own) if kind == ONWARD else (own, other)
            at = piece((first, second)[k], core, other if kind == ONWARD else own)
        else:
            at = piece(other if kind == ONWARD else own, core, k)
        at = buf.at[at]
        return remote(at, at, ag_s.at[group, k, kind], ag_r.at[group, k, kind], net.y if kind == ALONG else net.core)

    def gather_start(group, buf, k):
        gather_copy(group, buf, k, ALONG).start()
        gather_copy(group, buf, k, ACROSS).start()

    def gather_pass(group, buf, k):
        gather_copy(group, buf, k, ALONG).wait_recv()
        gather_copy(group, buf, k, ONWARD).start()

    def own_ready(group, buf):
        for k in range(2):
            gather_copy(group, buf, k, ACROSS).wait_recv()

    def other_ready(group, buf, k):
        gather_copy(group, buf, k, ONWARD).wait_recv()

    def gather_sent(group, buf):
        for k in range(2):
            for kind in (ALONG, ACROSS, ONWARD):
                gather_copy(group, buf, k, kind).wait_send()

    FAR, NEAR, SUMMED = 0, 1, 2

    def sum_copy(k, kind):
        at = pl.ds(aligned((core if kind == SUMMED else 1 - core) * half_seq + k * block), block)
        src = PART.at[1 if kind == NEAR else 0, at]
        return remote(src, RB.at[k, kind], rs_s.at[k, kind], rs_r.at[k, kind], net.y if kind == SUMMED else net.core)

    def far_start(k):
        sum_copy(k, FAR).start()

    def near_start(k):
        sum_copy(k, NEAR).start()

    def sum_pass(k):
        sum_copy(k, FAR).wait_recv()
        at = pl.ds(aligned(core * half_seq + k * block), block)
        PART[0, at] = (PART[0, at].astype(F32) + RB[k, FAR].astype(F32)).astype(BF)
        sum_copy(k, SUMMED).start()

    def pair_end(k):
        sum_copy(k, NEAR).wait_recv()
        sum_copy(k, NEAR).wait_send()
        at = pl.ds(aligned(core * half_seq + k * block), block)
        return PART[1, at].astype(F32) + RB[k, NEAR].astype(F32)

    def sum_end(k):
        total = pair_end(k)
        sum_copy(k, SUMMED).wait_recv()
        for kind in (FAR, SUMMED):
            sum_copy(k, kind).wait_send()
        return total + RB[k, SUMMED].astype(F32)

    eighth, z, x = net.dp % 8, net.z, net.x
    hop_z, mid_z = z + 1 - 2 * (z % 2), 3 - z
    parts = (
        (0, (n_qkv + n_head) // 8, 6, WT, WO),
        (n_qkv + n_head, 2 * ff // 8, 4, WU, WD),
    )
    inner, edge = net.inner, net.edge
    FROM_Y, HOP_OWN, MID_OWN, MID_ON, HOP_ON, HOP_LAST, ALONG_X = range(7)

    def weight_copy(g, kind, zz, device, src=None):
        base, n = parts[g][:2]
        at = GR.at[pl.ds(aligned(base + (2 * zz + x) * n), n)]
        slot = ALONG_X + zz if kind == ALONG_X else kind
        return remote(at if src is None else src, at, wg_s.at[g, slot], wg_r.at[g, slot], device)

    def weight_on(g, zz):
        weight_copy(g, ALONG_X, zz, net.x_dev).start()

    def weights_0(g):
        _, n, split, first, second = parts[g]

        @pl.when(eighth < split)
        def _():
            weight_copy(g, FROM_Y, z, net.y, first.at[last, pl.ds(aligned(eighth * n), n)]).start()

        @pl.when(eighth >= split)
        def _():
            weight_copy(g, FROM_Y, z, net.y, second.at[last, pl.ds(aligned((eighth - split) * n), n)]).start()

    def weights_1(g):
        weight_copy(g, FROM_Y, z, net.y).wait_recv()
        weight_copy(g, HOP_OWN, z, net.hop_dev).start()

        @pl.when(inner)
        def _():
            weight_copy(g, MID_OWN, z, net.mid_dev).start()

        weight_on(g, z)

    def weights_2(g):
        weight_copy(g, HOP_OWN, hop_z, net.hop_dev).wait_recv()

        @pl.when(inner)
        def _():
            weight_copy(g, MID_ON, hop_z, net.mid_dev).start()
            weight_copy(g, MID_OWN, mid_z, net.mid_dev).wait_recv()
            weight_copy(g, HOP_ON, mid_z, net.hop_dev).start()
            weight_on(g, mid_z)

        weight_on(g, hop_z)

    def weights_3(g):
        @pl.when(inner)
        def _():
            weight_copy(g, MID_ON, 3 - hop_z, net.mid_dev).wait_recv()
            weight_copy(g, HOP_LAST, 3 - hop_z, net.hop_dev).start()

        @pl.when(edge)
        def _():
            weight_copy(g, HOP_ON, 3 - hop_z, net.hop_dev).wait_recv()

        weight_on(g, 3 - hop_z)

    def weights_4(g):
        @pl.when(edge)
        def _():
            weight_copy(g, HOP_LAST, mid_z, net.hop_dev).wait_recv()
            weight_on(g, mid_z)

    def weights_5(g):
        for zz in range(4):
            weight_copy(g, ALONG_X, zz, net.x_dev).wait_recv()
            weight_copy(g, ALONG_X, zz, net.x_dev).wait_send()
        weight_copy(g, FROM_Y, z, net.y).wait_send()
        weight_copy(g, HOP_OWN, z, net.hop_dev).wait_send()

        @pl.when(inner)
        def _():
            weight_copy(g, MID_OWN, z, net.mid_dev).wait_send()
            weight_copy(g, MID_ON, hop_z, net.mid_dev).wait_send()
            weight_copy(g, HOP_ON, mid_z, net.hop_dev).wait_send()
            weight_copy(g, HOP_LAST, 3 - hop_z, net.hop_dev).wait_send()

    BIASES, UPSTREAM, HIDDEN, GRADIENT = range(4)

    def swap(which, src, dst):
        return remote(src, dst, ex_s.at[which], ex_r.at[which], net.y)

    def attend(r, xg, wt, bias, qkvt, probs_of, ct):
        for c in range(3):
            at = slice(c * n_head, (c + 1) * n_head)
            qkvt[at] = (dot(wt[at], xg, NT) + bias[at]).astype(BF)

        def head(h, carry):
            o = h * HEAD_DIM
            kt = qkvt[pl.ds(aligned(n_head + o), HEAD_DIM)] * jnp.asarray(HEAD_DIM**-0.5, BF)
            vt = qkvt[pl.ds(aligned(2 * n_head + o), HEAD_DIM)]
            qt = qkvt[pl.ds(aligned(o), HEAD_DIM)]
            scores = jnp.where(segc[r] == segr[r], dot(kt, qt, TN), MASKED)
            powers = jnp.exp(scores - jnp.max(scores, axis=0, keepdims=True))
            probs = (powers * (1.0 / jnp.sum(powers, axis=0, keepdims=True))).astype(BF)
            probs_of(h)[...] = probs
            ct[pl.ds(aligned(o), HEAD_DIM)] = dot(vt, probs, NN).astype(BF)
            return carry

        lax.fori_loop(0, heads, head, 0)

    def attention_forward(l, r):
        xg = XG[l, rows_of(r, 0, seq)]
        attend(r, xg, WT.at[l], bcol.at[l], QKVT.at[l, r], lambda h: PT.at[l, r, h], CT.at[l, r])

    def neighbour_attention_forward():
        xg = XG[last, rows_of(own, 0, seq)]
        attend(own, xg, GR.at[:n_qkv], bcol_y, DPT.at[0], lambda h: DST, DCT)

    def partial(slot, products, start):
        for k in range(2):
            for c in range(2):
                at = slice(c * half_seq + k * block, c * half_seq + (k + 1) * block)
                PART[slot, at] = sum(dot(left[:, at], right[...], TN) for left, right in products).astype(BF)
            start(k)

    def norm(l, which, k, value):
        centered = value - jnp.mean(value, axis=-1, keepdims=True)
        rstd = lax.rsqrt(jnp.mean(centered * centered, axis=-1, keepdims=True) + EPSILON)
        normal = centered * rstd
        XH[l, which, k] = normal.astype(BF)
        RSTD[l, which, k] = rstd
        return normal * vec[l, 2 + which : 3 + which] + vec[l, 4 + which : 5 + which]

    def first_norm(l, k, branch, group):
        out = norm(l, 0, k, XRES[k] + branch + vec[l, 0:1])
        HRES[k] = out
        HG[l, piece(own, core, k)] = out.astype(BF)
        gather_start(group, HG.at[l], k)

    def second_norm(l, k, branch):
        out = norm(l, 1, k, HRES[k] + branch + vec[l, 1:2])
        XRES[k] = out
        return out.astype(BF)

    def ff_active(hidden, weight, bias):
        wide = dot(hidden, weight, NN) + bias
        cdf = 0.5 * (1.0 + lax.erf(wide * 0.7071067811865476))
        slope = cdf + wide * 0.3989422804014327 * jnp.exp(-0.5 * wide * wide)
        return (wide * cdf).astype(BF), slope.astype(BF)

    def ff_forward_own(l):
        at = rows_of(own, 0, seq)
        G[l, at], DG[l, at] = ff_active(HG[l, at], WU[l], bup[l, 0:1])

    def pieces_of(r, k):
        return piece(r, 0, k), piece(r, 1, k)

    def load(ref, ats):
        return jnp.concatenate([ref[at] for at in ats], axis=0)

    def store(ref, ats, value):
        for i, at in enumerate(ats):
            ref[at] = value[i * block : (i + 1) * block]

    def part_pieces(k):
        return [slice(c * half_seq + k * block, c * half_seq + (k + 1) * block) for c in range(2)]

    def ff_forward_other(l, k, product=True):
        ats = pieces_of(other, k)
        active, slope = ff_active(load(HG.at[l], ats), WU[l], bup[l, 0:1])
        store(G.at[l], ats, active)
        store(DG.at[l], ats, slope)
        if product:
            store(PART.at[0], part_pieces(k), dot(active, WD[l], NN).astype(BF))

    def norm_backward(l, which, k, upstream):
        normal, rstd = XH[l, which, k].astype(F32), RSTD[l, which, k]
        VB[0, l, 2 + which : 3 + which] += jnp.sum(upstream * normal, axis=0, keepdims=True)
        VB[0, l, 4 + which : 5 + which] += jnp.sum(upstream, axis=0, keepdims=True)
        scaled = upstream * vec[l, 2 + which : 3 + which]
        grad = rstd * (
            scaled
            - jnp.mean(scaled, axis=-1, keepdims=True)
            - normal * jnp.mean(scaled * normal, axis=-1, keepdims=True)
        )
        VB[0, l, which : which + 1] += jnp.sum(grad, axis=0, keepdims=True)
        return grad

    def second_norm_backward(l, k, upstream):
        grad = norm_backward(l, 1, k, upstream)
        DH[k] = grad
        DF[piece(own, core, k)] = grad.astype(BF)
        gather_start(USUAL, DF, k)

    def ff_backward(l, ats, slot, part_ats):
        grad = (dot(load(DF, ats), WD[l], NT) * load(DG.at[l], ats).astype(F32)).astype(BF)
        store(DU, ats, grad)
        VB[1, l, 0:1, :ff] += jnp.sum(grad.astype(F32), axis=0, keepdims=True)
        store(PART.at[slot], part_ats, dot(grad, WU[l], NT).astype(BF))

    def ff_backward_own(l):
        ats = [piece(own, c, k) for c in range(2) for k in range(2)]
        part_ats = [slice(i * block, (i + 1) * block) for i in range(4)]
        ff_backward(l, ats, 1, part_ats)

    def first_norm_backward(l, k):
        grad = norm_backward(l, 0, k, DH[k] + sum_end(k))
        DY[k] = grad
        DG[l, piece(own, core, k)] = grad.astype(BF)
        gather_start(USUAL, DG.at[l], k)

    def attention_backward(l, r, slot, start):
        DCT[...] = dot(WO[l], DG[l, rows_of(r, 0, seq)], NT).astype(BF)

        def head(h, carry):
            o = h * HEAD_DIM
            q_at, k_at, v_at = (pl.ds(aligned(c * n_head + o), HEAD_DIM) for c in range(3))
            dct = DCT[q_at]
            probs = PT[l, r, h].astype(F32)
            weighted = probs * dot(QKVT[l, r, v_at], dct, TN)
            mean = jnp.sum(weighted, axis=0, keepdims=True)
            DST[...] = (weighted - probs * mean).astype(BF)
            scale = HEAD_DIM**-0.5
            DPT[slot, q_at] = (dot(QKVT[l, r, k_at], DST[...], NN) * scale).astype(BF)
            DPT[slot, k_at] = (dot(QKVT[l, r, q_at], DST[...], NT) * scale).astype(BF)
            DPT[slot, v_at] = dot(dct, PT[l, r, h], NT).astype(BF)
            return carry

        lax.fori_loop(0, heads, head, 0)
        partial(slot, ((DPT.at[slot], WT.at[l]),), start)
        ones = jnp.ones((8, seq), BF)
        VB[1, l, 1:2, :n_qkv] += dot(ones, DPT[slot], NT)[0:1]

    per_layer = 2 * ff + n_qkv + n_head

    def tokens_product(left, right, base):
        def strip(i, carry):
            at = pl.ds(aligned(i * 256, 256), 256)
            GR[pl.ds(aligned(base + i * 256), 256)] = dot(left[:, at], right[...], TN).astype(BF)
            return carry

        lax.fori_loop(0, left.shape[1] // 256, strip, 0)

    def attention_gradients(l, base):
        at = pl.ds(aligned(base), n_qkv)
        both_rows = ((0, other), (1, own))
        GR[at] = sum(dot(DPT[slot], XG[l, rows_of(r, 0, seq)], NN) for slot, r in both_rows).astype(BF)
        at = pl.ds(aligned(base + n_qkv), n_head)
        GR[at] = sum(dot(CT[l, r], DG[l, rows_of(r, 0, seq)], NN) for _, r in both_rows).astype(BF)

    units = layers * per_layer // UNIT
    part = UNIT // 2
    half = part // 2
    stages_x, stages_z = [], []
    always = None

    def stage(who_send, who_recv, device, offset, length, landing=None, add=None, staging=None):
        return (who_send, who_recv, device, offset, length, landing, add, staging)

    keep, give = net.x * half, (1 - net.x) * half
    stages_x.append(stage(always, always, net.x_dev, give, half, RX0, keep, SX0))
    stages_x.append(stage(edge, inner, net.hop_dev, keep, half, RX1, keep, SX1))
    stages_x.append(stage(inner, inner, net.mid_dev, keep, half, RX2, keep))
    for i, device in enumerate(net.outer_devs):
        stages_x.append(stage(inner, inner, device, keep, half, RXO.at[i], keep))
    stages_x.append(stage(inner, edge, net.hop_dev, keep, half))
    stages_x.append(stage(always, always, net.x_dev, keep, half))
    keep, give = part + net.half * half, part + (1 - net.half) * half
    stages_z.append(stage(edge, inner, net.hop_dev, part, part, RZ0, part, SZ0))
    stages_z.append(stage(inner, inner, net.mid_dev, give, half, RZ1, keep, SZ1))
    stages_z.append(stage(inner, inner, net.x_dev, keep, half, RZ2, keep))
    for i, device in enumerate(net.outer_devs):
        stages_z.append(stage(inner, inner, device, keep, half, RZO.at[i], keep))
    stages_z.append(stage(inner, inner, net.mid_dev, keep, half))
    stages_z.append(stage(inner, edge, net.hop_dev, part, part))
    depth = len(stages_x)
    hops = {0: (stages_z, credit_z), 1: (stages_x, credit_x)}

    def when(condition, body):
        if condition is None:
            body()
        else:
            pl.when(condition)(body)

    def stage_copy(which, s, u):
        _, _, device, offset, length, landing, _, staging = which[0][s]
        src = GR.at[pl.ds(aligned(u * UNIT + offset), length)]
        dst = src if landing is None else landing.at[u % SLOTS]
        src = src if staging is None else staging.at[u % SPACING]
        return remote(src, dst, which[1].at[u, s], which[2].at[u, s], device)

    def last_of(which):
        return units if which[0] is stages_x else units - 1

    def live(which, u):
        return (u >= 0) & (u <= last_of(which))

    def credit_of(which, s):
        return hops[s][1] if s in hops and hops[s][0] is which[0] else None

    def stage_send(which, s, u):
        who_send, _, _, offset, length, _, _, staging = which[0][s]

        def send():
            if credit_of(which, s) is not None:

                @pl.when(u >= SLOTS)
                def _():
                    pl.semaphore_wait(credit_of(which, s), 1)

            if staging is not None:
                staging[u % SPACING] = GR[pl.ds(aligned(u * UNIT + offset), length)]
            stage_copy(which, s, u).start()

        when(who_send, send)

    def stage_sent(which, s, u):
        when(which[0][s][0], lambda: stage_copy(which, s, u).wait_send())

    def stage_recv(which, s, u):
        _, who_recv, device, _, length, landing, add, _ = which[0][s]

        def take():
            stage_copy(which, s, u).wait_recv()
            if landing is not None:
                at = pl.ds(aligned(u * UNIT + add), length)
                GR[at] = (GR[at].astype(F32) + landing[u % SLOTS].astype(F32)).astype(BF)
            if credit_of(which, s) is not None:

                @pl.when(u < last_of(which) + 1 - SLOTS)
                def _():
                    pl.semaphore_signal(credit_of(which, s), inc=1, device_id=device, device_id_type=MESH)

        when(who_recv, take)

    both = ((stages_x, arx_s, arx_r), (stages_z, arz_s, arz_r))
    per_units = per_layer // UNIT
    sections = (
        (ff // UNIT, grad_down, 0),
        (2 * ff // UNIT, grad_up, ff),
        (per_units, grad_in, 2 * ff),
        (per_units, grad_out, 2 * ff + n_qkv),
    )
    at_place = (1, 1, 1, 1, 1, 1, 1, 1, 2, 1, 1, 1, 2, 2, 1)
    before = [sum(at_place[:e]) * per_units // sum(at_place) for e in range(len(at_place) + 1)]
    down_done, up_done, all_done = 4, 6, 13
    lag = before[down_done]
    assert before[up_done] <= lag + ff // UNIT and before[all_done] <= lag + 2 * ff // UNIT

    def out_copy(i, k):
        _, out, base = sections[k]
        out = out.at[layers - 1 - i]
        src = GR.at[pl.ds(aligned(i * per_layer + base), out.shape[0])]
        return pltpu.make_async_copy(src, out, osem.at[i, k])

    def unit_done(u):
        i, own = u // per_units, u % per_units
        for k, (end, _, _) in enumerate(sections):

            @pl.when((own == end - 1) & (u < units))
            def _(k=k):
                out_copy(i, k).start()

    def tick(now, carry=0):
        t = now - lag
        for s in range(depth):
            u = t - SPACING * (s + 1)
            for which in both:
                pl.when(live(which, u))(functools.partial(stage_sent, which, s, u))
        for which in both:
            pl.when(live(which, t))(functools.partial(stage_send, which, 0, t))
        for s in range(depth):
            u = t - SPACING * (s + 1)
            for which in both:

                @pl.when(live(which, u))
                def _(which=which, s=s, u=u):
                    stage_recv(which, s, u)
                    if s + 1 < depth:
                        stage_send(which, s + 1, u)

        u = t - SPACING * depth
        pl.when((u >= 0) & (u < units))(functools.partial(unit_done, u))
        return carry

    for r in range(rows):
        XG[0, piece(r, core, own)] = x_in[:, r, :]
    for k in range(2):
        gather_start(INPUT, XG.at[0], k)

    VB[...] = jnp.zeros(VB.shape, F32)
    BS[...] = jnp.zeros(BS.shape, F32)
    BS[0:1, :ff] = up_bias[last : last + 1].astype(F32)
    BS[8:10, :n_head] = in_bias[last].astype(F32)
    swap(BIASES, BS, BY).start()
    diagonal = lax.broadcasted_iota(jnp.int32, (n_head, n_head), 0) == lax.broadcasted_iota(
        jnp.int32, (n_head, n_head), 1
    )

    def columns(out, two_rows):
        for c, at in ((0, 0), (1, 2 * n_head)):
            spread = jnp.where(diagonal, two_rows[c : c + 1], 0.0)
            out[at : at + n_head] = jnp.sum(spread, axis=1, keepdims=True)
        out[n_head : 2 * n_head] = jnp.zeros((n_head, 1), F32)

    for l in range(layers):
        vec[l, 0:2] = branch_bias[l].astype(F32)
        vec[l, 2:4] = norm_gain[l].astype(F32)
        vec[l, 4:6] = norm_shift[l].astype(F32)
        bup[l, 0:1] = up_bias[l : l + 1].astype(F32)
        columns(bcol.at[l], in_bias[l].astype(F32))
    for r in range(rows):
        for ref, shape, axis in ((segc, (seq, 1), 0), (segr, (1, seq), 1)):
            index = lax.broadcasted_iota(jnp.int32, shape, axis)
            position = (index // block % 2 * 2 + index // half_seq) * block + index % block
            text, end = jnp.zeros(shape, jnp.int32), 0
            for j in range(lengths.shape[1]):
                end = end + lengths[r, j]
                text = text + jnp.where(position >= end, 1, 0)
            ref[r] = jnp.where(position >= seq - padding[r], lengths.shape[1], text)
    first, second = cot[:, 0, :].astype(F32), cot[:, 1, :].astype(F32)
    CB[0] = jnp.where(own == 0, second, first).astype(BF)
    CB[2] = jnp.where(own == 0, first, second).astype(BF)
    for copy in weight_copies:
        copy.wait()

    def attention_product(l, r, slot, start):
        partial(slot, ((CT.at[l, r], WO.at[l]),), start)

    def forward_layer(l):
        group, buf = (INPUT if l == 0 else LAYER_IN), XG.at[l]
        if l == 0:
            weights_0(0)
            gather_pass(group, buf, 0)
            gather_copy(group, buf, 1, ACROSS).wait_recv()
            other_ready(group, buf, 0)
        else:
            for k in range(2):
                gather_pass(group, buf, k)
            own_ready(group, buf)
            for k in range(2):
                other_ready(group, buf, k)
        attention_forward(l, other)
        attention_product(l, other, 0, far_start)
        if l == 0:
            gather_pass(group, buf, 1)
        for k in range(2):
            sum_pass(k)
        if l == 0:
            weights_1(0)
            weights_0(1)
            gather_copy(group, buf, 0, ACROSS).wait_recv()
            other_ready(group, buf, 1)
            for k in range(2):
                XRES[k] = XG[0, piece(own, core, k)].astype(F32)
        attention_forward(l, own)
        attention_product(l, own, 1, near_start)
        if l == 0:
            weights_2(0)
        gather_sent(group, buf)
        for k in range(2):
            first_norm(l, k, sum_end(k), USUAL)
        if l == 0:
            weights_3(0)
        buf = HG.at[l]
        own_ready(USUAL, buf)
        ff_forward_own(l)
        PART[1] = dot(G[l, rows_of(own, 0, seq)], WD[l], NN).astype(BF)
        for k in range(2):
            near_start(k)
        if l == 0:
            weights_1(1)
            weights_4(0)
        gather_pass(USUAL, buf, 0)
        other_ready(USUAL, buf, 0)
        ff_forward_other(l, 0)
        far_start(0)
        gather_pass(USUAL, buf, 1)
        sum_pass(0)
        other_ready(USUAL, buf, 1)
        ff_forward_other(l, 1)
        far_start(1)
        if l == 0:
            weights_2(1)
        sum_pass(1)
        gather_sent(USUAL, buf)
        for k in range(2):
            XG[l + 1, piece(own, core, k)] = second_norm(l, k, sum_end(k))
            gather_start(LAYER_IN, XG.at[l + 1], k)

    def forward_last():
        l = last
        swap(UPSTREAM, CB.at[0], CB.at[1]).start()
        weights_3(1)
        own_ready(LAYER_IN, XG.at[l])
        attention_forward(l, own)
        weights_5(0)
        swap(BIASES, BS, BY).wait()
        columns(bcol_y, BY[8:10, :n_head])
        neighbour_attention_forward()
        both = ((CT.at[l, own], WO.at[l]), (DCT, GR.at[n_qkv : n_qkv + n_head]))
        partial(1, both, near_start)
        weights_4(1)
        for k in range(2):
            gather_pass(LAYER_IN, XG.at[l], k)
        for k in range(2):
            first_norm(l, k, pair_end(k), FF_IN)
        own_ready(FF_IN, HG.at[l])
        ff_forward_own(l)
        at, base = rows_of(own, 0, seq), n_qkv + n_head
        product = dot(G[l, at], WD[l], NN)
        weights_5(1)
        active, _ = ff_active(HG[l, at], GR[base : base + width], BY[0:1, :ff])
        PART[1] = (product + dot(active, GR[base + width : base + width + ff], NN)).astype(BF)
        for k in range(2):
            near_start(k)
        swap(UPSTREAM, CB.at[0], CB.at[1]).wait()
        for k in range(2):
            YB[k] = second_norm(l, k, pair_end(k))
            block_of = jnp.where(own == k, CB[2].astype(F32), CB[1].astype(F32))
            second_norm_backward(l, k, block_of)
        swap(HIDDEN, YB.at[other], YB.at[2]).start()

    for l in range(last):
        forward_layer(l)
    forward_last()

    def backward(i, carry):
        l = last - i
        base = i * per_layer

        def place(e):
            for k in range(before[e], before[e + 1]):
                tick(i * per_units + k)

        place(0)
        own_ready(USUAL, DF)
        ff_backward_own(l)
        for k in range(2):
            near_start(k)
        place(1)

        @pl.when(l == last)
        def _():
            for k in range(2):
                other_ready(LAYER_IN, XG.at[last], k)
            gather_sent(LAYER_IN, XG.at[last])
            attention_forward(last, other)
            for k in range(2):
                gather_pass(FF_IN, HG.at[last], k)
            for k in range(2):
                other_ready(FF_IN, HG.at[last], k)
                ff_forward_other(last, k, product=False)
            gather_sent(FF_IN, HG.at[last])

        gather_pass(USUAL, DF, 0)
        place(2)
        other_ready(USUAL, DF, 0)
        ff_backward(l, pieces_of(other, 0), 0, part_pieces(0))
        far_start(0)
        gather_pass(USUAL, DF, 1)
        sum_pass(0)
        place(3)
        other_ready(USUAL, DF, 1)
        tokens_product(G.at[l], DF, base)
        place(4)
        ff_backward(l, pieces_of(other, 1), 0, part_pieces(1))
        far_start(1)
        place(5)
        sum_pass(1)
        tokens_product(HG.at[l], DU, base + ff)
        place(6)
        gather_sent(USUAL, DF)
        first_norm_backward(l, 0)
        place(7)
        first_norm_backward(l, 1)
        place(8)
        buf = DG.at[l]
        own_ready(USUAL, buf)
        attention_backward(l, own, 1, near_start)
        place(9)
        gather_pass(USUAL, buf, 0)
        place(10)
        gather_pass(USUAL, buf, 1)
        place(11)
        for k in range(2):
            other_ready(USUAL, buf, k)
        attention_backward(l, other, 0, far_start)
        place(12)
        for k in range(2):
            sum_pass(k)
        attention_gradients(l, base + 2 * ff)
        place(13)
        gather_sent(USUAL, buf)
        for k in range(2):
            DY[k] = DY[k] + sum_end(k)

            @pl.when(l > 0)
            def _(k=k):
                second_norm_backward(l - 1, k, DY[k])

            if k == 0:
                place(14)

        return carry

    lax.fori_loop(0, layers, backward, 0)
    swap(GRADIENT, DY.at[other], DH.at[0]).start()
    swap(HIDDEN, YB.at[other], YB.at[2]).wait()
    mine, theirs = YB[own].astype(F32), YB[2].astype(F32)
    for r in range(rows):
        hidden_out[:, r, :] = jnp.where(own == r, mine, theirs).astype(BF)

    def vector_copy(k):
        return remote(VB.at[0], RV.at[k], v_s.at[k], v_r.at[k], (net.core, net.y)[k])

    now = layers * per_units
    for k in range(2):
        vector_copy(k).start()
        lax.fori_loop(now, now + min(1, lag // 2), tick, 0)
        now += min(1, lag // 2)
        vector_copy(k).wait()
        VB[0] += RV[k]
    base = layers * per_layer
    GR[base : base + UNIT] = jnp.zeros((UNIT, width), BF)
    GR[base : base + 16 * layers] = VB[...].reshape(16 * layers, width).astype(BF)
    lax.fori_loop(now, lag + units + 1 + SPACING * depth, tick, 0)
    small[...] = GR[base : base + 16 * layers].astype(F32)
    swap(GRADIENT, DY.at[other], DH.at[0]).wait()
    for r in range(rows):
        grad_hidden[:, r, :] = jnp.where(own == r, DY[own], DH[0])
    for i in range(layers):
        for k in range(len(sections)):
            out_copy(i, k).wait()


def local(
    hidden_in,
    cotangent,
    doc_lengths,
    pad_count,
    input_weight,
    input_bias,
    output_weight,
    up_weight,
    up_bias,
    down_weight,
    branch_bias,
    norm_gain,
    norm_shift,
):
    n_dp = lax.axis_size("dp")
    block, rows, width = hidden_in.shape
    seq = block * lax.axis_size("tensor")
    layers, _, _, n_head = input_weight.shape
    n_qkv, heads, ff = 3 * n_head, n_head // HEAD_DIM, up_weight.shape[2]
    tokens = rows * seq
    wt = jnp.swapaxes(input_weight, 2, 3).reshape(layers, n_qkv, width)
    per_layer = 2 * ff + n_qkv + n_head
    part = UNIT // 2
    outer = 0
    while 8 << outer < n_dp:
        outer += 1
    depth = 5 + outer
    vmem = pltpu.VMEM
    dma = pltpu.SemaphoreType.DMA
    scratch = [
        vmem((layers, n_qkv, width), BF),
        vmem((layers, n_head, width), BF),
        vmem((layers, width, ff), BF),
        vmem((layers, ff, width), BF),
        vmem((layers, tokens, width), BF),
        vmem((layers, tokens, width), BF),
        vmem((layers, tokens, ff), BF),
        vmem((layers, tokens, ff), BF),
        vmem((tokens, width), BF),
        vmem((tokens, ff), BF),
        vmem((layers, rows, n_qkv, seq), BF),
        vmem((layers, rows, heads, seq, seq), BF),
        vmem((layers, rows, n_head, seq), BF),
        vmem((rows, n_qkv, seq), BF),
        vmem((seq, seq), BF),
        vmem((n_head, seq), BF),
        vmem((rows, seq, width), BF),
        vmem((rows, 3, block, width), BF),
        vmem((rows, block, width), F32),
        vmem((rows, block, width), F32),
        vmem((layers, 2, rows, block, width), BF),
        vmem((layers, 2, rows, block, 1), F32),
        vmem((layers * per_layer + UNIT, width), BF),
        vmem((SLOTS, part // 2, width), BF),
        vmem((SLOTS, part // 2, width), BF),
        vmem((SLOTS, part // 2, width), BF),
        vmem((SLOTS, part, width), BF),
        vmem((SLOTS, part // 2, width), BF),
        vmem((SLOTS, part // 2, width), BF),
        vmem((max(outer, 1), SLOTS if outer else 1, part // 2, width), BF),
        vmem((max(outer, 1), SLOTS if outer else 1, part // 2, width), BF),
        vmem((SPACING, part // 2, width), BF),
        vmem((SPACING, part // 2, width), BF),
        vmem((SPACING, part, width), BF),
        vmem((SPACING, part // 2, width), BF),
        vmem((2, layers, 8, width), F32),
        vmem((2, layers, 8, width), F32),
        vmem((rows, seq, 1), jnp.int32),
        vmem((rows, 1, seq), jnp.int32),
        vmem((layers, n_qkv, 1), F32),
        vmem((n_qkv, 1), F32),
        vmem((layers, 8, ff), F32),
        vmem((layers, 8, width), F32),
        vmem((16, max(ff, n_head)), F32),
        vmem((16, max(ff, n_head)), F32),
        vmem((3, block, width), BF),
        vmem((3, block, width), BF),
        dma((4,)),
        dma((4, 2, 3)),
        dma((4, 2, 3)),
        dma((2, 3)),
        dma((2, 3)),
        dma((layers * per_layer // UNIT + 1, depth)),
        dma((layers * per_layer // UNIT + 1, depth)),
        dma((layers * per_layer // UNIT + 1, depth)),
        dma((layers * per_layer // UNIT + 1, depth)),
        dma((2,)),
        dma((2,)),
        dma((layers, 4)),
        pltpu.SemaphoreType.REGULAR,
        pltpu.SemaphoreType.REGULAR,
        dma((2, 10)),
        dma((2, 10)),
        dma((4,)),
        dma((4,)),
    ]
    whole, anywhere = pl.BlockSpec(memory_space=vmem), pl.BlockSpec(memory_space=pl.ANY)
    scalars = pl.BlockSpec(memory_space=pltpu.SMEM)
    results = pl.pallas_call(
        functools.partial(kernel, n_dp, layers),
        out_shape=(
            jax.ShapeDtypeStruct(hidden_in.shape, BF),
            jax.ShapeDtypeStruct(hidden_in.shape, F32),
            jax.ShapeDtypeStruct((layers, n_qkv, width), BF),
            jax.ShapeDtypeStruct(output_weight.shape, BF),
            jax.ShapeDtypeStruct(up_weight.shape, BF),
            jax.ShapeDtypeStruct(down_weight.shape, BF),
            jax.ShapeDtypeStruct((16 * layers, width), F32),
        ),
        in_specs=[whole, whole, scalars, scalars, anywhere, whole, anywhere, anywhere, whole, anywhere]
        + [whole] * 3,
        out_specs=(whole, whole, anywhere, anywhere, anywhere, anywhere, whole),
        scratch_shapes=scratch,
        compiler_params=pltpu.CompilerParams(
            collective_id=0, has_side_effects=True, vmem_limit_bytes=63 << 20
        ),
    )(
        hidden_in,
        cotangent,
        doc_lengths,
        pad_count,
        wt,
        input_bias,
        output_weight,
        up_weight,
        up_bias,
        down_weight,
        branch_bias,
        norm_gain,
        norm_shift,
    )
    pieces = 4

    def strip(array):
        return pl.BlockSpec((1, array.shape[1] // pieces, width), lambda l, c: (l, c, 0))

    strips = [strip(array) for array in results[2:6]]
    fixed = [
        jax.ShapeDtypeStruct(shape, F32)
        for shape in (input_bias.shape, up_bias.shape, branch_bias.shape, norm_gain.shape, norm_shift.shape)
    ]
    hidden_out, grad_hidden, grad_in, grad_out, grad_up, grad_down, *vectors = pl.pallas_call(
        functools.partial(finish, layers, pieces),
        grid=(layers, pieces),
        out_shape=[jax.ShapeDtypeStruct(array.shape, array.dtype) for array in results[:2]]
        + [jax.ShapeDtypeStruct(array.shape, F32) for array in results[2:6]]
        + fixed,
        in_specs=[whole] * 2 + strips + [whole],
        out_specs=[whole] * 2 + strips + [whole] * 5,
    )(*results)
    grad_in_bias, grad_up_bias, grad_branch, grad_gain, grad_shift = vectors
    grad_in = jnp.swapaxes(grad_in.reshape(layers, 3, n_head, width), 2, 3)
    return (
        hidden_out,
        grad_hidden,
        grad_in,
        grad_in_bias,
        grad_out,
        grad_up,
        grad_up_bias,
        grad_down,
        grad_branch,
        grad_gain,
        grad_shift,
    )


def finish(layers, pieces, *refs):
    hidden, grad_hidden, *grads = refs[:6]
    small = refs[6]
    hidden_out, grad_hidden_out, *outs = refs[7:13]
    grad_in_bias, grad_up_bias, grad_branch, grad_gain, grad_shift = refs[13:18]
    step = pl.program_id(0) * pieces + pl.program_id(1)

    @pl.when(step == 0)
    def _():
        hidden_out[...] = hidden[...]
        grad_hidden_out[...] = grad_hidden[...]
        n_head, ff = grad_in_bias.shape[2], grad_up_bias.shape[1]
        for l in range(layers):
            shared, split = 8 * l, 8 * (layers + l)
            grad_branch[l] = small[shared : shared + 2]
            grad_gain[l] = small[shared + 2 : shared + 4]
            grad_shift[l] = small[shared + 4 : shared + 6]
            grad_up_bias[l : l + 1] = small[split : split + 1, :ff]
            for c in range(2):
                grad_in_bias[l, c : c + 1] = small[split + 1 : split + 2, 2 * c * n_head : (2 * c + 1) * n_head]

    for grad, out in zip(grads, outs, strict=True):
        out[...] = grad[...].astype(F32)


def solution(mesh):
    return jax.shard_map(
        local,
        mesh=mesh,
        in_specs=(
            P("tensor", "dp", None),
            P("tensor", "dp", None),
            P("dp", None),
            P("dp"),
            P(None, None, None, "tensor"),
            P(None, None, "tensor"),
            P(None, "tensor", None),
            P(None, None, "tensor"),
            P(None, "tensor"),
            P(None, "tensor", None),
            P(),
            P(),
            P(),
        ),
        out_specs=(
            P("tensor", "dp", None),
            P("tensor", "dp", None),
            P(None, None, None, "tensor"),
            P(None, None, "tensor"),
            P(None, "tensor", None),
            P(None, None, "tensor"),
            P(None, "tensor"),
            P(None, "tensor", None),
            P(),
            P(),
            P(),
        ),
        check_vma=False,
    )
```

```python
import functools

import jax
import jax.numpy as jnp
from jax import lax
from jax.experimental import pallas as pl
from jax.experimental.pallas import tpu as pltpu
from jax.sharding import PartitionSpec as P

HEAD_DIM = 64
EPSILON = 1e-05
MASKED = -1e30
MESH = pl.DeviceIdType.MESH
BF, F32 = jnp.bfloat16, jnp.float32
NN = (((1,), (0,)), ((), ()))
NT = (((1,), (1,)), ((), ()))
TN = (((0,), (0,)), ((), ()))
UNIT = 128
SPACING, SLOTS = 2, 6


def dot(a, b, dims):
    return lax.dot_general(a, b, dims, preferred_element_type=F32)


def aligned(value, by=16):
    return pl.multiple_of(value, by)


class Net:
    def __init__(self, n_dp):
        dp, t = lax.axis_index("dp"), lax.axis_index("tensor")
        self.dp, self.t = dp, t
        self.own, self.c = t // 2, t % 2
        self.other = 1 - self.own
        self.core, self.y = (dp, t + 1 - 2 * self.c), (dp, t + 2 - 4 * self.own)
        self.x = dp % 2
        self.z = z = (dp // 2) % 4
        self.half = z // 2
        self.inner = (z == 1) | (z == 2)
        self.inner_count = (z + 1) // 2 % 2
        self.edge = (z == 0) | (z == 3)
        self.x_dev = (dp + 1 - 2 * self.x, t)
        self.hop_dev = (dp + 2 * (1 - 2 * (z % 2)), t)
        self.mid_dev = (dp + 2 * (3 - 2 * z), t)
        self.outer_devs = []
        step = 8
        while step < n_dp:
            self.outer_devs.append((dp + step * (1 - 2 * ((dp // step) % 2)), t))
            step *= 2
        self.partners = [self.core, self.y, self.x_dev, self.hop_dev]
        self.inner_partners = [self.mid_dev] + self.outer_devs


def remote(src, dst, send, recv, device):
    return pltpu.make_async_remote_copy(
        src_ref=src, dst_ref=dst, send_sem=send, recv_sem=recv, device_id=device, device_id_type=MESH
    )


def kernel(n_dp, layers, *refs):
    (x_in, cot, lengths, padding, wt_h, in_bias, wo_h, wu_h, up_bias, wd_h, branch_bias, norm_gain, norm_shift,
     hidden_out, grad_hidden, grad_in, grad_out, grad_up, grad_down, small,
     WT, WO, WU, WD, XG, HG, G, DG, DF, DU, QKVT, PT, CT, DPT, DST, DCT, PART, RB, XRES, HRES, XH, RSTD, GR,
     RX0, RX1, RX2, RZ0, RZ1, RZ2, RXO, RZO, SX0, SX1, SZ0, SZ1, VB, RV, segc, segr, bcol, bcol_y, bup, vec,
     BS, BY, CB, YB,
     wsem, ag_s, ag_r, rs_s, rs_r, arx_s, arx_r, arz_s, arz_r, v_s, v_r, osem, credit_x, credit_z,
     wg_s, wg_r, ex_s, ex_r) = refs
    DY, DH = XRES, HRES
    net = Net(n_dp)
    block, rows, width = x_in.shape
    seq = PART.shape[1]
    half_seq = seq // 2
    own, other, core = net.own, net.other, net.c
    last = layers - 1
    n_qkv = WT.shape[1]
    n_head = n_qkv // 3
    heads = n_head // HEAD_DIM
    ff = WU.shape[2]

    weight_copies = [
        pltpu.make_async_copy(a, b, wsem.at[i])
        for i, (a, b) in enumerate(((wt_h, WT), (wo_h, WO), (wu_h, WU), (wd_h, WD)))
    ]
    for copy in weight_copies:
        copy.start()

    barrier = pltpu.get_barrier_semaphore()
    for device in net.partners:
        pl.semaphore_signal(barrier, inc=1, device_id=device, device_id_type=MESH)

    @pl.when(net.inner)
    def _():
        for device in net.inner_partners:
            pl.semaphore_signal(barrier, inc=1, device_id=device, device_id_type=MESH)

    pl.semaphore_wait(barrier, len(net.partners) + net.inner_count * len(net.inner_partners))

    def rows_of(r, start, size):
        return pl.ds(aligned(r * seq + start), size)

    def piece(r, c, k):
        return rows_of(r, c * half_seq + k * block, block)

    ALONG, ACROSS, ONWARD = 0, 1, 2
    INPUT, USUAL, LAYER_IN, FF_IN = range(4)

    def gather_copy(group, buf, k, kind):
        if group == INPUT:
            first, second = (other, own) if kind == ONWARD else (own, other)
            at = piece((first, second)[k], core, other if kind == ONWARD else own)
        else:
            at = piece(other if kind == ONWARD else own, core, k)
        at = buf.at[at]
        return remote(at, at, ag_s.at[group, k, kind], ag_r.at[group, k, kind], net.y if kind == ALONG else net.core)

    def gather_start(group, buf, k):
        gather_copy(group, buf, k, ALONG).start()
        gather_copy(group, buf, k, ACROSS).start()

    def gather_pass(group, buf, k):
        gather_copy(group, buf, k, ALONG).wait_recv()
        gather_copy(group, buf, k, ONWARD).start()

    def own_ready(group, buf):
        for k in range(2):
            gather_copy(group, buf, k, ACROSS).wait_recv()

    def other_ready(group, buf, k):
        gather_copy(group, buf, k, ONWARD).wait_recv()

    def gather_sent(group, buf):
        for k in range(2):
            for kind in (ALONG, ACROSS, ONWARD):
                gather_copy(group, buf, k, kind).wait_send()

    FAR, NEAR, SUMMED = 0, 1, 2

    def sum_copy(k, kind):
        at = pl.ds(aligned((core if kind == SUMMED else 1 - core) * half_seq + k * block), block)
        src = PART.at[1 if kind == NEAR else 0, at]
        return remote(src, RB.at[k, kind], rs_s.at[k, kind], rs_r.at[k, kind], net.y if kind == SUMMED else net.core)

    def far_start(k):
        sum_copy(k, FAR).start()

    def near_start(k):
        sum_copy(k, NEAR).start()

    def sum_pass(k):
        sum_copy(k, FAR).wait_recv()
        at = pl.ds(aligned(core * half_seq + k * block), block)
        PART[0, at] = (PART[0, at].astype(F32) + RB[k, FAR].astype(F32)).astype(BF)
        sum_copy(k, SUMMED).start()

    def pair_end(k):
        sum_copy(k, NEAR).wait_recv()
        sum_copy(k, NEAR).wait_send()
        at = pl.ds(aligned(core * half_seq + k * block), block)
        return PART[1, at].astype(F32) + RB[k, NEAR].astype(F32)

    def sum_end(k):
        total = pair_end(k)
        sum_copy(k, SUMMED).wait_recv()
        for kind in (FAR, SUMMED):
            sum_copy(k, kind).wait_send()
        return total + RB[k, SUMMED].astype(F32)

    eighth, z, x = net.dp % 8, net.z, net.x
    hop_z, mid_z = z + 1 - 2 * (z % 2), 3 - z
    parts = (
        (0, (n_qkv + n_head) // 8, 6, WT, WO),
        (n_qkv + n_head, 2 * ff // 8, 4, WU, WD),
    )
    inner, edge = net.inner, net.edge
    FROM_Y, HOP_OWN, MID_OWN, MID_ON, HOP_ON, HOP_LAST, ALONG_X = range(7)

    def weight_copy(g, kind, zz, device, src=None):
        base, n = parts[g][:2]
        at = GR.at[pl.ds(aligned(base + (2 * zz + x) * n), n)]
        slot = ALONG_X + zz if kind == ALONG_X else kind
        return remote(at if src is None else src, at, wg_s.at[g, slot], wg_r.at[g, slot], device)

    def weight_on(g, zz):
        weight_copy(g, ALONG_X, zz, net.x_dev).start()

    def weights_0(g):
        _, n, split, first, second = parts[g]

        @pl.when(eighth < split)
        def _():
            weight_copy(g, FROM_Y, z, net.y, first.at[last, pl.ds(aligned(eighth * n), n)]).start()

        @pl.when(eighth >= split)
        def _():
            weight_copy(g, FROM_Y, z, net.y, second.at[last, pl.ds(aligned((eighth - split) * n), n)]).start()

    def weights_1(g):
        weight_copy(g, FROM_Y, z, net.y).wait_recv()
        weight_copy(g, HOP_OWN, z, net.hop_dev).start()

        @pl.when(inner)
        def _():
            weight_copy(g, MID_OWN, z, net.mid_dev).start()

        weight_on(g, z)

    def weights_2(g):
        weight_copy(g, HOP_OWN, hop_z, net.hop_dev).wait_recv()

        @pl.when(inner)
        def _():
            weight_copy(g, MID_ON, hop_z, net.mid_dev).start()
            weight_copy(g, MID_OWN, mid_z, net.mid_dev).wait_recv()
            weight_copy(g, HOP_ON, mid_z, net.hop_dev).start()
            weight_on(g, mid_z)

        weight_on(g, hop_z)

    def weights_3(g):
        @pl.when(inner)
        def _():
            weight_copy(g, MID_ON, 3 - hop_z, net.mid_dev).wait_recv()
            weight_copy(g, HOP_LAST, 3 - hop_z, net.hop_dev).start()

        @pl.when(edge)
        def _():
            weight_copy(g, HOP_ON, 3 - hop_z, net.hop_dev).wait_recv()

        weight_on(g, 3 - hop_z)

    def weights_4(g):
        @pl.when(edge)
        def _():
            weight_copy(g, HOP_LAST, mid_z, net.hop_dev).wait_recv()
            weight_on(g, mid_z)

    def weights_5(g):
        for zz in range(4):
            weight_copy(g, ALONG_X, zz, net.x_dev).wait_recv()
            weight_copy(g, ALONG_X, zz, net.x_dev).wait_send()
        weight_copy(g, FROM_Y, z, net.y).wait_send()
        weight_copy(g, HOP_OWN, z, net.hop_dev).wait_send()

        @pl.when(inner)
        def _():
            weight_copy(g, MID_OWN, z, net.mid_dev).wait_send()
            weight_copy(g, MID_ON, hop_z, net.mid_dev).wait_send()
            weight_copy(g, HOP_ON, mid_z, net.hop_dev).wait_send()
            weight_copy(g, HOP_LAST, 3 - hop_z, net.hop_dev).wait_send()

    BIASES, UPSTREAM, HIDDEN, GRADIENT = range(4)

    def swap(which, src, dst):
        return remote(src, dst, ex_s.at[which], ex_r.at[which], net.y)

    def attend(r, xg, wt, bias, qkvt, probs_of, ct):
        for c in range(3):
            at = slice(c * n_head, (c + 1) * n_head)
            qkvt[at] = (dot(wt[at], xg, NT) + bias[at]).astype(BF)

        def head(h, carry):
            o = h * HEAD_DIM
            kt = qkvt[pl.ds(aligned(n_head + o), HEAD_DIM)] * jnp.asarray(HEAD_DIM**-0.5, BF)
            vt = qkvt[pl.ds(aligned(2 * n_head + o), HEAD_DIM)]
            qt = qkvt[pl.ds(aligned(o), HEAD_DIM)]
            scores = jnp.where(segc[r] == segr[r], dot(kt, qt, TN), MASKED)
            powers = jnp.exp(scores - jnp.max(scores, axis=0, keepdims=True))
            probs = (powers * (1.0 / jnp.sum(powers, axis=0, keepdims=True))).astype(BF)
            probs_of(h)[...] = probs
            ct[pl.ds(aligned(o), HEAD_DIM)] = dot(vt, probs, NN).astype(BF)
            return carry

        lax.fori_loop(0, heads, head, 0)

    def attention_forward(l, r):
        xg = XG[l, rows_of(r, 0, seq)]
        attend(r, xg, WT.at[l], bcol.at[l], QKVT.at[l, r], lambda h: PT.at[l, r, h], CT.at[l, r])

    def neighbour_attention_forward():
        xg = XG[last, rows_of(own, 0, seq)]
        attend(own, xg, GR.at[:n_qkv], bcol_y, DPT.at[0], lambda h: DST, DCT)

    def partial(slot, products, start):
        for k in range(2):
            for c in range(2):
                at = slice(c * half_seq + k * block, c * half_seq + (k + 1) * block)
                PART[slot, at] = sum(dot(left[:, at], right[...], TN) for left, right in products).astype(BF)
            start(k)

    def norm(l, which, k, value):
        centered = value - jnp.mean(value, axis=-1, keepdims=True)
        rstd = lax.rsqrt(jnp.mean(centered * centered, axis=-1, keepdims=True) + EPSILON)
        normal = centered * rstd
        XH[l, which, k] = normal.astype(BF)
        RSTD[l, which, k] = rstd
        return normal * vec[l, 2 + which : 3 + which] + vec[l, 4 + which : 5 + which]

    def first_norm(l, k, branch, group):
        out = norm(l, 0, k, XRES[k] + branch + vec[l, 0:1])
        HRES[k] = out
        HG[l, piece(own, core, k)] = out.astype(BF)
        gather_start(group, HG.at[l], k)

    def second_norm(l, k, branch):
        out = norm(l, 1, k, HRES[k] + branch + vec[l, 1:2])
        XRES[k] = out
        return out.astype(BF)

    def ff_active(hidden, weight, bias):
        wide = dot(hidden, weight, NN) + bias
        cdf = 0.5 * (1.0 + lax.erf(wide * 0.7071067811865476))
        slope = cdf + wide * 0.3989422804014327 * jnp.exp(-0.5 * wide * wide)
        return (wide * cdf).astype(BF), slope.astype(BF)

    def ff_forward_own(l):
        at = rows_of(own, 0, seq)
        G[l, at], DG[l, at] = ff_active(HG[l, at], WU[l], bup[l, 0:1])

    def pieces_of(r, k):
        return piece(r, 0, k), piece(r, 1, k)

    def load(ref, ats):
        return jnp.concatenate([ref[at] for at in ats], axis=0)

    def store(ref, ats, value):
        for i, at in enumerate(ats):
            ref[at] = value[i * block : (i + 1) * block]

    def part_pieces(k):
        return [slice(c * half_seq + k * block, c * half_seq + (k + 1) * block) for c in range(2)]

    def ff_forward_other(l, k, product=True):
        ats = pieces_of(other, k)
        active, slope = ff_active(load(HG.at[l], ats), WU[l], bup[l, 0:1])
        store(G.at[l], ats, active)
        store(DG.at[l], ats, slope)
        if product:
            store(PART.at[0], part_pieces(k), dot(active, WD[l], NN).astype(BF))

    def norm_backward(l, which, k, upstream):
        normal, rstd = XH[l, which, k].astype(F32), RSTD[l, which, k]
        VB[0, l, 2 + which : 3 + which] += jnp.sum(upstream * normal, axis=0, keepdims=True)
        VB[0, l, 4 + which : 5 + which] += jnp.sum(upstream, axis=0, keepdims=True)
        scaled = upstream * vec[l, 2 + which : 3 + which]
        grad = rstd * (
            scaled
            - jnp.mean(scaled, axis=-1, keepdims=True)
            - normal * jnp.mean(scaled * normal, axis=-1, keepdims=True)
        )
        VB[0, l, which : which + 1] += jnp.sum(grad, axis=0, keepdims=True)
        return grad

    def second_norm_backward(l, k, upstream):
        grad = norm_backward(l, 1, k, upstream)
        DH[k] = grad
        DF[piece(own, core, k)] = grad.astype(BF)
        gather_start(USUAL, DF, k)

    def ff_backward(l, ats, slot, part_ats):
        grad = (dot(load(DF, ats), WD[l], NT) * load(DG.at[l], ats).astype(F32)).astype(BF)
        store(DU, ats, grad)
        VB[1, l, 0:1, :ff] += jnp.sum(grad.astype(F32), axis=0, keepdims=True)
        store(PART.at[slot], part_ats, dot(grad, WU[l], NT).astype(BF))

    def ff_backward_own(l):
        ats = [piece(own, c, k) for c in range(2) for k in range(2)]
        part_ats = [slice(i * block, (i + 1) * block) for i in range(4)]
        ff_backward(l, ats, 1, part_ats)

    def first_norm_backward(l, k):
        grad = norm_backward(l, 0, k, DH[k] + sum_end(k))
        DY[k] = grad
        DG[l, piece(own, core, k)] = grad.astype(BF)
        gather_start(USUAL, DG.at[l], k)

    def attention_backward(l, r, slot, start):
        DCT[...] = dot(WO[l], DG[l, rows_of(r, 0, seq)], NT).astype(BF)

        def head(h, carry):
            o = h * HEAD_DIM
            q_at, k_at, v_at = (pl.ds(aligned(c * n_head + o), HEAD_DIM) for c in range(3))
            dct = DCT[q_at]
            probs = PT[l, r, h].astype(F32)
            weighted = probs * dot(QKVT[l, r, v_at], dct, TN)
            mean = jnp.sum(weighted, axis=0, keepdims=True)
            DST[...] = (weighted - probs * mean).astype(BF)
            scale = HEAD_DIM**-0.5
            DPT[slot, q_at] = (dot(QKVT[l, r, k_at], DST[...], NN) * scale).astype(BF)
            DPT[slot, k_at] = (dot(QKVT[l, r, q_at], DST[...], NT) * scale).astype(BF)
            DPT[slot, v_at] = dot(dct, PT[l, r, h], NT).astype(BF)
            return carry

        lax.fori_loop(0, heads, head, 0)
        partial(slot, ((DPT.at[slot], WT.at[l]),), start)
        ones = jnp.ones((8, seq), BF)
        VB[1, l, 1:2, :n_qkv] += dot(ones, DPT[slot], NT)[0:1]

    per_layer = 2 * ff + n_qkv + n_head

    def tokens_product(left, right, base, lo, hi):
        def strip(i, carry):
            at = pl.ds(aligned(i * 256, 256), 256)
            GR[pl.ds(aligned(base + i * 256), 256)] = dot(left[:, at], right[...], TN).astype(BF)
            return carry

        lax.fori_loop(lo, hi, strip, 0)

    def attention_gradients(l, base):
        at = pl.ds(aligned(base), n_qkv)
        both_rows = ((0, other), (1, own))
        GR[at] = sum(dot(DPT[slot], XG[l, rows_of(r, 0, seq)], NN) for slot, r in both_rows).astype(BF)
        at = pl.ds(aligned(base + n_qkv), n_head)
        GR[at] = sum(dot(CT[l, r], DG[l, rows_of(r, 0, seq)], NN) for _, r in both_rows).astype(BF)

    units = layers * per_layer // UNIT
    part = UNIT // 2
    half = part // 2
    stages_x, stages_z = [], []
    always = None

    def stage(who_send, who_recv, device, offset, length, landing=None, add=None, staging=None):
        return (who_send, who_recv, device, offset, length, landing, add, staging)

    keep, give = net.x * half, (1 - net.x) * half
    stages_x.append(stage(always, always, net.x_dev, give, half, RX0, keep, SX0))
    stages_x.append(stage(edge, inner, net.hop_dev, keep, half, RX1, keep, SX1))
    stages_x.append(stage(inner, inner, net.mid_dev, keep, half, RX2, keep))
    for i, device in enumerate(net.outer_devs):
        stages_x.append(stage(inner, inner, device, keep, half, RXO.at[i], keep))
    stages_x.append(stage(inner, edge, net.hop_dev, keep, half))
    stages_x.append(stage(always, always, net.x_dev, keep, half))
    keep, give = part + net.half * half, part + (1 - net.half) * half
    stages_z.append(stage(edge, inner, net.hop_dev, part, part, RZ0, part, SZ0))
    stages_z.append(stage(inner, inner, net.mid_dev, give, half, RZ1, keep, SZ1))
    stages_z.append(stage(inner, inner, net.x_dev, keep, half, RZ2, keep))
    for i, device in enumerate(net.outer_devs):
        stages_z.append(stage(inner, inner, device, keep, half, RZO.at[i], keep))
    stages_z.append(stage(inner, inner, net.mid_dev, keep, half))
    stages_z.append(stage(inner, edge, net.hop_dev, part, part))
    depth = len(stages_x)
    hops = {0: (stages_z, credit_z), 1: (stages_x, credit_x)}

    def when(condition, body):
        if condition is None:
            body()
        else:
            pl.when(condition)(body)

    def stage_copy(which, s, u):
        _, _, device, offset, length, landing, _, staging = which[0][s]
        src = GR.at[pl.ds(aligned(u * UNIT + offset), length)]
        dst = src if landing is None else landing.at[u % SLOTS]
        src = src if staging is None else staging.at[u % SPACING]
        return remote(src, dst, which[1].at[u, s], which[2].at[u, s], device)

    def last_of(which):
        return units if which[0] is stages_x else units - 1

    def live(which, u):
        return (u >= 0) & (u <= last_of(which))

    def credit_of(which, s):
        return hops[s][1] if s in hops and hops[s][0] is which[0] else None

    def stage_send(which, s, u):
        who_send, _, _, offset, length, _, _, staging = which[0][s]

        def send():
            if credit_of(which, s) is not None:

                @pl.when(u >= SLOTS)
                def _():
                    pl.semaphore_wait(credit_of(which, s), 1)

            if staging is not None:
                staging[u % SPACING] = GR[pl.ds(aligned(u * UNIT + offset), length)]
            stage_copy(which, s, u).start()

        when(who_send, send)

    def stage_sent(which, s, u):
        when(which[0][s][0], lambda: stage_copy(which, s, u).wait_send())

    def stage_recv(which, s, u):
        _, who_recv, device, _, length, landing, add, _ = which[0][s]

        def take():
            stage_copy(which, s, u).wait_recv()
            if landing is not None:
                at = pl.ds(aligned(u * UNIT + add), length)
                GR[at] = (GR[at].astype(F32) + landing[u % SLOTS].astype(F32)).astype(BF)
            if credit_of(which, s) is not None:

                @pl.when(u < last_of(which) + 1 - SLOTS)
                def _():
                    pl.semaphore_signal(credit_of(which, s), inc=1, device_id=device, device_id_type=MESH)

        when(who_recv, take)

    both = ((stages_x, arx_s, arx_r), (stages_z, arz_s, arz_r))
    per_units = per_layer // UNIT
    sections = (
        (ff // UNIT, grad_down, 0),
        (2 * ff // UNIT, grad_up, ff),
        (per_units, grad_in, 2 * ff),
        (per_units, grad_out, 2 * ff + n_qkv),
    )
    at_place = (1, 1, 1, 1, 1, 1, 1, 1, 2, 1, 1, 1, 2, 2, 1)
    before = [sum(at_place[:e]) * per_units // sum(at_place) for e in range(len(at_place) + 1)]
    down_done, up_done, all_done = 4, 6, 13
    lag = before[down_done]
    assert before[down_done + 1] <= lag + 256 // UNIT
    assert before[up_done] <= lag + ff // UNIT and before[all_done] <= lag + 2 * ff // UNIT

    def out_copy(i, k):
        _, out, base = sections[k]
        out = out.at[layers - 1 - i]
        src = GR.at[pl.ds(aligned(i * per_layer + base), out.shape[0])]
        return pltpu.make_async_copy(src, out, osem.at[i, k])

    def unit_done(u):
        i, own = u // per_units, u % per_units
        for k, (end, _, _) in enumerate(sections):

            @pl.when((own == end - 1) & (u < units))
            def _(k=k):
                out_copy(i, k).start()

    def tick(now, carry=0):
        t = now - lag
        for s in range(depth):
            u = t - SPACING * (s + 1)
            for which in both:
                pl.when(live(which, u))(functools.partial(stage_sent, which, s, u))
        for which in both:
            pl.when(live(which, t))(functools.partial(stage_send, which, 0, t))
        for s in range(depth):
            u = t - SPACING * (s + 1)
            for which in both:

                @pl.when(live(which, u))
                def _(which=which, s=s, u=u):
                    stage_recv(which, s, u)
                    if s + 1 < depth:
                        stage_send(which, s + 1, u)

        u = t - SPACING * depth
        pl.when((u >= 0) & (u < units))(functools.partial(unit_done, u))
        return carry

    for r in range(rows):
        XG[0, piece(r, core, own)] = x_in[:, r, :]
    for k in range(2):
        gather_start(INPUT, XG.at[0], k)

    VB[...] = jnp.zeros(VB.shape, F32)
    BS[...] = jnp.zeros(BS.shape, F32)
    BS[0:1, :ff] = up_bias[last : last + 1].astype(F32)
    BS[8:10, :n_head] = in_bias[last].astype(F32)
    swap(BIASES, BS, BY).start()
    diagonal = lax.broadcasted_iota(jnp.int32, (n_head, n_head), 0) == lax.broadcasted_iota(
        jnp.int32, (n_head, n_head), 1
    )

    def columns(out, two_rows):
        for c, at in ((0, 0), (1, 2 * n_head)):
            spread = jnp.where(diagonal, two_rows[c : c + 1], 0.0)
            out[at : at + n_head] = jnp.sum(spread, axis=1, keepdims=True)
        out[n_head : 2 * n_head] = jnp.zeros((n_head, 1), F32)

    for l in range(layers):
        vec[l, 0:2] = branch_bias[l].astype(F32)
        vec[l, 2:4] = norm_gain[l].astype(F32)
        vec[l, 4:6] = norm_shift[l].astype(F32)
        bup[l, 0:1] = up_bias[l : l + 1].astype(F32)
        columns(bcol.at[l], in_bias[l].astype(F32))
    for r in range(rows):
        for ref, shape, axis in ((segc, (seq, 1), 0), (segr, (1, seq), 1)):
            index = lax.broadcasted_iota(jnp.int32, shape, axis)
            position = (index // block % 2 * 2 + index // half_seq) * block + index % block
            text, end = jnp.zeros(shape, jnp.int32), 0
            for j in range(lengths.shape[1]):
                end = end + lengths[r, j]
                text = text + jnp.where(position >= end, 1, 0)
            ref[r] = jnp.where(position >= seq - padding[r], lengths.shape[1], text)
    first, second = cot[:, 0, :].astype(F32), cot[:, 1, :].astype(F32)
    CB[0] = jnp.where(own == 0, second, first).astype(BF)
    CB[2] = jnp.where(own == 0, first, second).astype(BF)
    for copy in weight_copies:
        copy.wait()

    def attention_product(l, r, slot, start):
        partial(slot, ((CT.at[l, r], WO.at[l]),), start)

    def forward_layer(l):
        group, buf = (INPUT if l == 0 else LAYER_IN), XG.at[l]
        if l == 0:
            weights_0(0)
            gather_pass(group, buf, 0)
            gather_copy(group, buf, 1, ACROSS).wait_recv()
            other_ready(group, buf, 0)
        else:
            for k in range(2):
                gather_pass(group, buf, k)
            own_ready(group, buf)
            for k in range(2):
                other_ready(group, buf, k)
        attention_forward(l, other)
        attention_product(l, other, 0, far_start)
        if l == 0:
            gather_pass(group, buf, 1)
        for k in range(2):
            sum_pass(k)
        if l == 0:
            weights_1(0)
            weights_0(1)
            gather_copy(group, buf, 0, ACROSS).wait_recv()
            other_ready(group, buf, 1)
            for k in range(2):
                XRES[k] = XG[0, piece(own, core, k)].astype(F32)
        attention_forward(l, own)
        attention_product(l, own, 1, near_start)
        if l == 0:
            weights_2(0)
        gather_sent(group, buf)
        for k in range(2):
            first_norm(l, k, sum_end(k), USUAL)
        if l == 0:
            weights_3(0)
        buf = HG.at[l]
        own_ready(USUAL, buf)
        ff_forward_own(l)
        PART[1] = dot(G[l, rows_of(own, 0, seq)], WD[l], NN).astype(BF)
        for k in range(2):
            near_start(k)
        if l == 0:
            weights_1(1)
            weights_4(0)
        gather_pass(USUAL, buf, 0)
        other_ready(USUAL, buf, 0)
        ff_forward_other(l, 0)
        far_start(0)
        gather_pass(USUAL, buf, 1)
        sum_pass(0)
        other_ready(USUAL, buf, 1)
        ff_forward_other(l, 1)
        far_start(1)
        if l == 0:
            weights_2(1)
        sum_pass(1)
        gather_sent(USUAL, buf)
        for k in range(2):
            XG[l + 1, piece(own, core, k)] = second_norm(l, k, sum_end(k))
            gather_start(LAYER_IN, XG.at[l + 1], k)

    def forward_last():
        l = last
        swap(UPSTREAM, CB.at[0], CB.at[1]).start()
        weights_3(1)
        own_ready(LAYER_IN, XG.at[l])
        attention_forward(l, own)
        weights_5(0)
        swap(BIASES, BS, BY).wait()
        columns(bcol_y, BY[8:10, :n_head])
        neighbour_attention_forward()
        both = ((CT.at[l, own], WO.at[l]), (DCT, GR.at[n_qkv : n_qkv + n_head]))
        partial(1, both, near_start)
        weights_4(1)
        for k in range(2):
            gather_pass(LAYER_IN, XG.at[l], k)
        for k in range(2):
            first_norm(l, k, pair_end(k), FF_IN)
        up_y = n_qkv + n_head
        down_y = up_y + width

        def ff_own_units(c):
            at = rows_of(own, c * half_seq, half_seq)
            G[l, at], DG[l, at] = ff_active(HG[l, at], WU[l], bup[l, 0:1])

        def ff_product(c):
            at = rows_of(own, c * half_seq, half_seq)
            active, _ = ff_active(HG[l, at], GR[up_y:down_y], BY[0:1, :ff])
            product = dot(G[l, at], WD[l], NN) + dot(active, GR[down_y : down_y + ff], NN)
            PART[1, pl.ds(aligned(c * half_seq), half_seq)] = product.astype(BF)

        ff_own_units(core)
        own_ready(FF_IN, HG.at[l])
        ff_own_units(1 - core)
        weights_5(1)
        ff_product(1 - core)
        for k in range(2):
            near_start(k)
        ff_product(core)
        swap(UPSTREAM, CB.at[0], CB.at[1]).wait()
        for k in range(2):
            YB[k] = second_norm(l, k, pair_end(k))
            block_of = jnp.where(own == k, CB[2].astype(F32), CB[1].astype(F32))
            second_norm_backward(l, k, block_of)
        swap(HIDDEN, YB.at[other], YB.at[2]).start()

    for l in range(last):
        forward_layer(l)
    forward_last()

    def backward(i, carry):
        l = last - i
        base = i * per_layer

        def place(e):
            for k in range(before[e], before[e + 1]):
                tick(i * per_units + k)

        place(0)
        own_ready(USUAL, DF)
        ff_backward_own(l)
        for k in range(2):
            near_start(k)
        place(1)

        @pl.when(l == last)
        def _():
            for k in range(2):
                other_ready(LAYER_IN, XG.at[last], k)
            gather_sent(LAYER_IN, XG.at[last])
            attention_forward(last, other)
            for k in range(2):
                gather_pass(FF_IN, HG.at[last], k)
            for k in range(2):
                other_ready(FF_IN, HG.at[last], k)
                ff_forward_other(last, k, product=False)
            gather_sent(FF_IN, HG.at[last])

        gather_pass(USUAL, DF, 0)
        place(2)
        other_ready(USUAL, DF, 0)
        ff_backward(l, pieces_of(other, 0), 0, part_pieces(0))
        far_start(0)
        gather_pass(USUAL, DF, 1)
        sum_pass(0)
        place(3)
        other_ready(USUAL, DF, 1)
        tokens_product(G.at[l], DF, base, 0, 1)
        place(4)
        tokens_product(G.at[l], DF, base, 1, ff // 256)
        ff_backward(l, pieces_of(other, 1), 0, part_pieces(1))
        far_start(1)
        place(5)
        sum_pass(1)
        tokens_product(HG.at[l], DU, base + ff, 0, width // 256)
        place(6)
        gather_sent(USUAL, DF)
        first_norm_backward(l, 0)
        place(7)
        first_norm_backward(l, 1)
        place(8)
        buf = DG.at[l]
        own_ready(USUAL, buf)
        attention_backward(l, own, 1, near_start)
        place(9)
        gather_pass(USUAL, buf, 0)
        place(10)
        gather_pass(USUAL, buf, 1)
        place(11)
        for k in range(2):
            other_ready(USUAL, buf, k)
        attention_backward(l, other, 0, far_start)
        place(12)
        for k in range(2):
            sum_pass(k)
        attention_gradients(l, base + 2 * ff)
        place(13)
        gather_sent(USUAL, buf)
        for k in range(2):
            DY[k] = DY[k] + sum_end(k)

            @pl.when(l > 0)
            def _(k=k):
                second_norm_backward(l - 1, k, DY[k])

            if k == 0:
                place(14)

        return carry

    lax.fori_loop(0, layers, backward, 0)
    swap(GRADIENT, DY.at[other], DH.at[0]).start()
    swap(HIDDEN, YB.at[other], YB.at[2]).wait()
    mine, theirs = YB[own].astype(F32), YB[2].astype(F32)
    for r in range(rows):
        hidden_out[:, r, :] = jnp.where(own == r, mine, theirs).astype(BF)

    def vector_copy(k):
        return remote(VB.at[0], RV.at[k], v_s.at[k], v_r.at[k], (net.core, net.y)[k])

    now = layers * per_units
    for k in range(2):
        vector_copy(k).start()
        lax.fori_loop(now, now + min(1, lag // 2), tick, 0)
        now += min(1, lag // 2)
        vector_copy(k).wait()
        VB[0] += RV[k]
    base = layers * per_layer
    GR[base : base + UNIT] = jnp.zeros((UNIT, width), BF)
    GR[base : base + 16 * layers] = VB[...].reshape(16 * layers, width).astype(BF)
    lax.fori_loop(now, lag + units + 1 + SPACING * depth, tick, 0)
    small[...] = GR[base : base + 16 * layers].astype(F32)
    swap(GRADIENT, DY.at[other], DH.at[0]).wait()
    for r in range(rows):
        grad_hidden[:, r, :] = jnp.where(own == r, DY[own], DH[0])
    for i in range(layers):
        for k in range(len(sections)):
            out_copy(i, k).wait()


def local(
    hidden_in,
    cotangent,
    doc_lengths,
    pad_count,
    input_weight,
    input_bias,
    output_weight,
    up_weight,
    up_bias,
    down_weight,
    branch_bias,
    norm_gain,
    norm_shift,
):
    n_dp = lax.axis_size("dp")
    block, rows, width = hidden_in.shape
    seq = block * lax.axis_size("tensor")
    layers, _, _, n_head = input_weight.shape
    n_qkv, heads, ff = 3 * n_head, n_head // HEAD_DIM, up_weight.shape[2]
    tokens = rows * seq
    wt = jnp.swapaxes(input_weight, 2, 3).reshape(layers, n_qkv, width)
    per_layer = 2 * ff + n_qkv + n_head
    part = UNIT // 2
    outer = 0
    while 8 << outer < n_dp:
        outer += 1
    depth = 5 + outer
    vmem = pltpu.VMEM
    dma = pltpu.SemaphoreType.DMA
    scratch = [
        vmem((layers, n_qkv, width), BF),
        vmem((layers, n_head, width), BF),
        vmem((layers, width, ff), BF),
        vmem((layers, ff, width), BF),
        vmem((layers, tokens, width), BF),
        vmem((layers, tokens, width), BF),
        vmem((layers, tokens, ff), BF),
        vmem((layers, tokens, ff), BF),
        vmem((tokens, width), BF),
        vmem((tokens, ff), BF),
        vmem((layers, rows, n_qkv, seq), BF),
        vmem((layers, rows, heads, seq, seq), BF),
        vmem((layers, rows, n_head, seq), BF),
        vmem((rows, n_qkv, seq), BF),
        vmem((seq, seq), BF),
        vmem((n_head, seq), BF),
        vmem((rows, seq, width), BF),
        vmem((rows, 3, block, width), BF),
        vmem((rows, block, width), F32),
        vmem((rows, block, width), F32),
        vmem((layers, 2, rows, block, width), BF),
        vmem((layers, 2, rows, block, 1), F32),
        vmem((layers * per_layer + UNIT, width), BF),
        vmem((SLOTS, part // 2, width), BF),
        vmem((SLOTS, part // 2, width), BF),
        vmem((SLOTS, part // 2, width), BF),
        vmem((SLOTS, part, width), BF),
        vmem((SLOTS, part // 2, width), BF),
        vmem((SLOTS, part // 2, width), BF),
        vmem((max(outer, 1), SLOTS if outer else 1, part // 2, width), BF),
        vmem((max(outer, 1), SLOTS if outer else 1, part // 2, width), BF),
        vmem((SPACING, part // 2, width), BF),
        vmem((SPACING, part // 2, width), BF),
        vmem((SPACING, part, width), BF),
        vmem((SPACING, part // 2, width), BF),
        vmem((2, layers, 8, width), F32),
        vmem((2, layers, 8, width), F32),
        vmem((rows, seq, 1), jnp.int32),
        vmem((rows, 1, seq), jnp.int32),
        vmem((layers, n_qkv, 1), F32),
        vmem((n_qkv, 1), F32),
        vmem((layers, 8, ff), F32),
        vmem((layers, 8, width), F32),
        vmem((16, max(ff, n_head)), F32),
        vmem((16, max(ff, n_head)), F32),
        vmem((3, block, width), BF),
        vmem((3, block, width), BF),
        dma((4,)),
        dma((4, 2, 3)),
        dma((4, 2, 3)),
        dma((2, 3)),
        dma((2, 3)),
        dma((layers * per_layer // UNIT + 1, depth)),
        dma((layers * per_layer // UNIT + 1, depth)),
        dma((layers * per_layer // UNIT + 1, depth)),
        dma((layers * per_layer // UNIT + 1, depth)),
        dma((2,)),
        dma((2,)),
        dma((layers, 4)),
        pltpu.SemaphoreType.REGULAR,
        pltpu.SemaphoreType.REGULAR,
        dma((2, 10)),
        dma((2, 10)),
        dma((4,)),
        dma((4,)),
    ]
    whole, anywhere = pl.BlockSpec(memory_space=vmem), pl.BlockSpec(memory_space=pl.ANY)
    scalars = pl.BlockSpec(memory_space=pltpu.SMEM)
    results = pl.pallas_call(
        functools.partial(kernel, n_dp, layers),
        out_shape=(
            jax.ShapeDtypeStruct(hidden_in.shape, BF),
            jax.ShapeDtypeStruct(hidden_in.shape, F32),
            jax.ShapeDtypeStruct((layers, n_qkv, width), BF),
            jax.ShapeDtypeStruct(output_weight.shape, BF),
            jax.ShapeDtypeStruct(up_weight.shape, BF),
            jax.ShapeDtypeStruct(down_weight.shape, BF),
            jax.ShapeDtypeStruct((16 * layers, width), F32),
        ),
        in_specs=[whole, whole, scalars, scalars, anywhere, whole, anywhere, anywhere, whole, anywhere]
        + [whole] * 3,
        out_specs=(whole, whole, anywhere, anywhere, anywhere, anywhere, whole),
        scratch_shapes=scratch,
        compiler_params=pltpu.CompilerParams(
            collective_id=0, has_side_effects=True, vmem_limit_bytes=63 << 20
        ),
    )(
        hidden_in,
        cotangent,
        doc_lengths,
        pad_count,
        wt,
        input_bias,
        output_weight,
        up_weight,
        up_bias,
        down_weight,
        branch_bias,
        norm_gain,
        norm_shift,
    )
    pieces = 2

    def strip(array):
        return pl.BlockSpec((1, array.shape[1] // pieces, width), lambda l, c: (l, c, 0))

    strips = [strip(array) for array in results[2:6]]
    fixed = [
        jax.ShapeDtypeStruct(shape, F32)
        for shape in (input_bias.shape, up_bias.shape, branch_bias.shape, norm_gain.shape, norm_shift.shape)
    ]
    hidden_out, grad_hidden, grad_in, grad_out, grad_up, grad_down, *vectors = pl.pallas_call(
        functools.partial(finish, layers, pieces),
        grid=(layers, pieces),
        out_shape=[jax.ShapeDtypeStruct(array.shape, array.dtype) for array in results[:2]]
        + [jax.ShapeDtypeStruct(array.shape, F32) for array in results[2:6]]
        + fixed,
        in_specs=[whole] * 2 + strips + [whole],
        out_specs=[whole] * 2 + strips + [whole] * 5,
    )(*results)
    grad_in_bias, grad_up_bias, grad_branch, grad_gain, grad_shift = vectors
    grad_in = jnp.swapaxes(grad_in.reshape(layers, 3, n_head, width), 2, 3)
    return (
        hidden_out,
        grad_hidden,
        grad_in,
        grad_in_bias,
        grad_out,
        grad_up,
        grad_up_bias,
        grad_down,
        grad_branch,
        grad_gain,
        grad_shift,
    )


def finish(layers, pieces, *refs):
    hidden, grad_hidden, *grads = refs[:6]
    small = refs[6]
    hidden_out, grad_hidden_out, *outs = refs[7:13]
    grad_in_bias, grad_up_bias, grad_branch, grad_gain, grad_shift = refs[13:18]
    step = pl.program_id(0) * pieces + pl.program_id(1)

    @pl.when(step == 0)
    def _():
        hidden_out[...] = hidden[...]
        grad_hidden_out[...] = grad_hidden[...]
        n_head, ff = grad_in_bias.shape[2], grad_up_bias.shape[1]
        for l in range(layers):
            shared, split = 8 * l, 8 * (layers + l)
            grad_branch[l] = small[shared : shared + 2]
            grad_gain[l] = small[shared + 2 : shared + 4]
            grad_shift[l] = small[shared + 4 : shared + 6]
            grad_up_bias[l : l + 1] = small[split : split + 1, :ff]
            for c in range(2):
                grad_in_bias[l, c : c + 1] = small[split + 1 : split + 2, 2 * c * n_head : (2 * c + 1) * n_head]

    for grad, out in zip(grads, outs, strict=True):
        out[...] = grad[...].astype(F32)


def solution(mesh):
    return jax.shard_map(
        local,
        mesh=mesh,
        in_specs=(
            P("tensor", "dp", None),
            P("tensor", "dp", None),
            P("dp", None),
            P("dp"),
            P(None, None, None, "tensor"),
            P(None, None, "tensor"),
            P(None, "tensor", None),
            P(None, None, "tensor"),
            P(None, "tensor"),
            P(None, "tensor", None),
            P(),
            P(),
            P(),
        ),
        out_specs=(
            P("tensor", "dp", None),
            P("tensor", "dp", None),
            P(None, None, None, "tensor"),
            P(None, None, "tensor"),
            P(None, "tensor", None),
            P(None, None, "tensor"),
            P(None, "tensor"),
            P(None, "tensor", None),
            P(),
            P(),
            P(),
        ),
        check_vma=False,
    )
```

```python
import functools

import jax
import jax.numpy as jnp
from jax import lax
from jax.experimental import pallas as pl
from jax.experimental.pallas import tpu as pltpu
from jax.sharding import PartitionSpec as P

HEAD_DIM = 64
EPSILON = 1e-05
MASKED = -1e30
MESH = pl.DeviceIdType.MESH
BF, F32 = jnp.bfloat16, jnp.float32
NN = (((1,), (0,)), ((), ()))
NT = (((1,), (1,)), ((), ()))
TN = (((0,), (0,)), ((), ()))
UNIT = 128
SPACING, SLOTS = 2, 6


def dot(a, b, dims):
    return lax.dot_general(a, b, dims, preferred_element_type=F32)


def aligned(value, by=16):
    return pl.multiple_of(value, by)


class Net:
    def __init__(self, n_dp):
        dp, t = lax.axis_index("dp"), lax.axis_index("tensor")
        self.dp, self.t = dp, t
        self.own, self.c = t // 2, t % 2
        self.other = 1 - self.own
        self.core, self.y = (dp, t + 1 - 2 * self.c), (dp, t + 2 - 4 * self.own)
        self.x = dp % 2
        self.z = z = (dp // 2) % 4
        self.half = z // 2
        self.inner = (z == 1) | (z == 2)
        self.inner_count = (z + 1) // 2 % 2
        self.edge = (z == 0) | (z == 3)
        self.x_dev = (dp + 1 - 2 * self.x, t)
        self.hop_dev = (dp + 2 * (1 - 2 * (z % 2)), t)
        self.mid_dev = (dp + 2 * (3 - 2 * z), t)
        self.outer_devs = []
        step = 8
        while step < n_dp:
            self.outer_devs.append((dp + step * (1 - 2 * ((dp // step) % 2)), t))
            step *= 2
        self.partners = [self.core, self.y, self.x_dev, self.hop_dev]
        self.inner_partners = [self.mid_dev] + self.outer_devs


def remote(src, dst, send, recv, device):
    return pltpu.make_async_remote_copy(
        src_ref=src, dst_ref=dst, send_sem=send, recv_sem=recv, device_id=device, device_id_type=MESH
    )


def kernel(n_dp, layers, *refs):
    (x_in, cot, lengths, padding, wt_h, in_bias, wo_h, wu_h, up_bias, wd_h, branch_bias, norm_gain, norm_shift,
     hidden_out, grad_hidden, grad_in, grad_out, grad_up, grad_down, small,
     WT, WO, WU, WD, XG, HG, G, DG, DF, DU, QKVT, PT, CT, DPT, DST, DCT, PART, RB, XRES, HRES, XH, RSTD, GR,
     RX0, RX1, RX2, RZ0, RZ1, RZ2, RXO, RZO, SX0, SX1, SZ0, SZ1, VB, RV, segc, segr, bcol, bcol_y, bup, vec,
     BS, BY, CB, YB,
     wsem, ag_s, ag_r, rs_s, rs_r, arx_s, arx_r, arz_s, arz_r, v_s, v_r, osem, credit_x, credit_z,
     wg_s, wg_r, ex_s, ex_r) = refs
    DY, DH = XRES, HRES
    net = Net(n_dp)
    block, rows, width = x_in.shape
    seq = PART.shape[1]
    half_seq = seq // 2
    own, other, core = net.own, net.other, net.c
    last = layers - 1
    n_qkv = WT.shape[1]
    n_head = n_qkv // 3
    heads = n_head // HEAD_DIM
    ff = WU.shape[2]

    weight_copies = [
        pltpu.make_async_copy(a, b, wsem.at[i])
        for i, (a, b) in enumerate(((wt_h, WT), (wo_h, WO), (wu_h, WU), (wd_h, WD)))
    ]
    for copy in weight_copies:
        copy.start()

    barrier = pltpu.get_barrier_semaphore()
    for device in net.partners:
        pl.semaphore_signal(barrier, inc=1, device_id=device, device_id_type=MESH)

    @pl.when(net.inner)
    def _():
        for device in net.inner_partners:
            pl.semaphore_signal(barrier, inc=1, device_id=device, device_id_type=MESH)

    pl.semaphore_wait(barrier, len(net.partners) + net.inner_count * len(net.inner_partners))

    def rows_of(r, start, size):
        return pl.ds(aligned(r * seq + start), size)

    def piece(r, c, k):
        return rows_of(r, c * half_seq + k * block, block)

    ALONG, ACROSS, ONWARD = 0, 1, 2
    INPUT, USUAL, LAYER_IN, FF_IN = range(4)

    def gather_copy(group, buf, k, kind):
        if group == INPUT:
            first, second = (other, own) if kind == ONWARD else (own, other)
            at = piece((first, second)[k], core, other if kind == ONWARD else own)
        else:
            at = piece(other if kind == ONWARD else own, core, k)
        at = buf.at[at]
        return remote(at, at, ag_s.at[group, k, kind], ag_r.at[group, k, kind], net.y if kind == ALONG else net.core)

    def gather_start(group, buf, k):
        gather_copy(group, buf, k, ALONG).start()
        gather_copy(group, buf, k, ACROSS).start()

    def gather_pass(group, buf, k):
        gather_copy(group, buf, k, ALONG).wait_recv()
        gather_copy(group, buf, k, ONWARD).start()

    def own_ready(group, buf):
        for k in range(2):
            gather_copy(group, buf, k, ACROSS).wait_recv()

    def other_ready(group, buf, k):
        gather_copy(group, buf, k, ONWARD).wait_recv()

    def gather_sent(group, buf):
        for k in range(2):
            for kind in (ALONG, ACROSS, ONWARD):
                gather_copy(group, buf, k, kind).wait_send()

    FAR, NEAR, SUMMED = 0, 1, 2

    def sum_copy(k, kind):
        at = pl.ds(aligned((core if kind == SUMMED else 1 - core) * half_seq + k * block), block)
        src = PART.at[1 if kind == NEAR else 0, at]
        return remote(src, RB.at[k, kind], rs_s.at[k, kind], rs_r.at[k, kind], net.y if kind == SUMMED else net.core)

    def far_start(k):
        sum_copy(k, FAR).start()

    def near_start(k):
        sum_copy(k, NEAR).start()

    def sum_pass(k):
        sum_copy(k, FAR).wait_recv()
        at = pl.ds(aligned(core * half_seq + k * block), block)
        PART[0, at] = (PART[0, at].astype(F32) + RB[k, FAR].astype(F32)).astype(BF)
        sum_copy(k, SUMMED).start()

    def pair_end(k):
        sum_copy(k, NEAR).wait_recv()
        sum_copy(k, NEAR).wait_send()
        at = pl.ds(aligned(core * half_seq + k * block), block)
        return PART[1, at].astype(F32) + RB[k, NEAR].astype(F32)

    def sum_end(k):
        total = pair_end(k)
        sum_copy(k, SUMMED).wait_recv()
        for kind in (FAR, SUMMED):
            sum_copy(k, kind).wait_send()
        return total + RB[k, SUMMED].astype(F32)

    eighth, z, x = net.dp % 8, net.z, net.x
    hop_z, mid_z = z + 1 - 2 * (z % 2), 3 - z
    parts = (
        (0, (n_qkv + n_head) // 8, 6, WT, WO),
        (n_qkv + n_head, 2 * ff // 8, 4, WU, WD),
    )
    inner, edge = net.inner, net.edge
    FROM_Y, HOP_OWN, MID_OWN, MID_ON, HOP_ON, HOP_LAST, ALONG_X = range(7)

    def weight_copy(g, kind, zz, device, src=None):
        base, n = parts[g][:2]
        at = GR.at[pl.ds(aligned(base + (2 * zz + x) * n), n)]
        slot = ALONG_X + zz if kind == ALONG_X else kind
        return remote(at if src is None else src, at, wg_s.at[g, slot], wg_r.at[g, slot], device)

    def weight_on(g, zz):
        weight_copy(g, ALONG_X, zz, net.x_dev).start()

    def weights_0(g):
        _, n, split, first, second = parts[g]

        @pl.when(eighth < split)
        def _():
            weight_copy(g, FROM_Y, z, net.y, first.at[last, pl.ds(aligned(eighth * n), n)]).start()

        @pl.when(eighth >= split)
        def _():
            weight_copy(g, FROM_Y, z, net.y, second.at[last, pl.ds(aligned((eighth - split) * n), n)]).start()

    def weights_1(g):
        weight_copy(g, FROM_Y, z, net.y).wait_recv()
        weight_copy(g, HOP_OWN, z, net.hop_dev).start()

        @pl.when(inner)
        def _():
            weight_copy(g, MID_OWN, z, net.mid_dev).start()

        weight_on(g, z)

    def weights_2(g):
        weight_copy(g, HOP_OWN, hop_z, net.hop_dev).wait_recv()

        @pl.when(inner)
        def _():
            weight_copy(g, MID_ON, hop_z, net.mid_dev).start()
            weight_copy(g, MID_OWN, mid_z, net.mid_dev).wait_recv()
            weight_copy(g, HOP_ON, mid_z, net.hop_dev).start()
            weight_on(g, mid_z)

        weight_on(g, hop_z)

    def weights_3(g):
        @pl.when(inner)
        def _():
            weight_copy(g, MID_ON, 3 - hop_z, net.mid_dev).wait_recv()
            weight_copy(g, HOP_LAST, 3 - hop_z, net.hop_dev).start()

        @pl.when(edge)
        def _():
            weight_copy(g, HOP_ON, 3 - hop_z, net.hop_dev).wait_recv()

        weight_on(g, 3 - hop_z)

    def weights_4(g):
        @pl.when(edge)
        def _():
            weight_copy(g, HOP_LAST, mid_z, net.hop_dev).wait_recv()
            weight_on(g, mid_z)

    def weights_5(g):
        for zz in range(4):
            weight_copy(g, ALONG_X, zz, net.x_dev).wait_recv()
            weight_copy(g, ALONG_X, zz, net.x_dev).wait_send()
        weight_copy(g, FROM_Y, z, net.y).wait_send()
        weight_copy(g, HOP_OWN, z, net.hop_dev).wait_send()

        @pl.when(inner)
        def _():
            weight_copy(g, MID_OWN, z, net.mid_dev).wait_send()
            weight_copy(g, MID_ON, hop_z, net.mid_dev).wait_send()
            weight_copy(g, HOP_ON, mid_z, net.hop_dev).wait_send()
            weight_copy(g, HOP_LAST, 3 - hop_z, net.hop_dev).wait_send()

    BIASES, UPSTREAM, HIDDEN, GRADIENT = range(4)

    def swap(which, src, dst):
        return remote(src, dst, ex_s.at[which], ex_r.at[which], net.y)

    def attend(r, xg, wt, bias, qkvt, probs_of, ct):
        for c in range(3):
            at = slice(c * n_head, (c + 1) * n_head)
            qkvt[at] = (dot(wt[at], xg, NT) + bias[at]).astype(BF)

        def head(h, carry):
            o = h * HEAD_DIM
            kt = qkvt[pl.ds(aligned(n_head + o), HEAD_DIM)] * jnp.asarray(HEAD_DIM**-0.5, BF)
            vt = qkvt[pl.ds(aligned(2 * n_head + o), HEAD_DIM)]
            qt = qkvt[pl.ds(aligned(o), HEAD_DIM)]
            scores = jnp.where(segc[r] == segr[r], dot(kt, qt, TN), MASKED)
            powers = jnp.exp(scores - jnp.max(scores, axis=0, keepdims=True))
            probs = (powers * (1.0 / jnp.sum(powers, axis=0, keepdims=True))).astype(BF)
            probs_of(h)[...] = probs
            ct[pl.ds(aligned(o), HEAD_DIM)] = dot(vt, probs, NN).astype(BF)
            return carry

        lax.fori_loop(0, heads, head, 0)

    def attention_forward(l, r):
        xg = XG[l, rows_of(r, 0, seq)]
        attend(r, xg, WT.at[l], bcol.at[l], QKVT.at[l, r], lambda h: PT.at[l, r, h], CT.at[l, r])

    def neighbour_attention_forward():
        xg = XG[last, rows_of(own, 0, seq)]
        attend(own, xg, GR.at[:n_qkv], bcol_y, DPT.at[0], lambda h: DST, DCT)

    def partial(slot, products, start):
        for k in range(2):
            for c in range(2):
                at = slice(c * half_seq + k * block, c * half_seq + (k + 1) * block)
                PART[slot, at] = sum(dot(left[:, at], right[...], TN) for left, right in products).astype(BF)
            start(k)

    def norm(l, which, k, value):
        centered = value - jnp.mean(value, axis=-1, keepdims=True)
        rstd = lax.rsqrt(jnp.mean(centered * centered, axis=-1, keepdims=True) + EPSILON)
        normal = centered * rstd
        XH[l, which, k] = normal.astype(BF)
        RSTD[l, which, k] = rstd
        return normal * vec[l, 2 + which : 3 + which] + vec[l, 4 + which : 5 + which]

    def first_norm(l, k, branch, group):
        out = norm(l, 0, k, XRES[k] + branch + vec[l, 0:1])
        HRES[k] = out
        HG[l, piece(own, core, k)] = out.astype(BF)
        gather_start(group, HG.at[l], k)

    def second_norm(l, k, branch):
        out = norm(l, 1, k, HRES[k] + branch + vec[l, 1:2])
        XRES[k] = out
        return out.astype(BF)

    def ff_active(hidden, weight, bias):
        wide = dot(hidden, weight, NN) + bias
        cdf = 0.5 * (1.0 + lax.erf(wide * 0.7071067811865476))
        slope = cdf + wide * 0.3989422804014327 * jnp.exp(-0.5 * wide * wide)
        return (wide * cdf).astype(BF), slope.astype(BF)

    def ff_forward_own(l):
        at = rows_of(own, 0, seq)
        G[l, at], DG[l, at] = ff_active(HG[l, at], WU[l], bup[l, 0:1])

    def pieces_of(r, k):
        return piece(r, 0, k), piece(r, 1, k)

    def load(ref, ats):
        return jnp.concatenate([ref[at] for at in ats], axis=0)

    def store(ref, ats, value):
        for i, at in enumerate(ats):
            ref[at] = value[i * block : (i + 1) * block]

    def part_pieces(k):
        return [slice(c * half_seq + k * block, c * half_seq + (k + 1) * block) for c in range(2)]

    def ff_forward_other(l, k, product=True):
        ats = pieces_of(other, k)
        active, slope = ff_active(load(HG.at[l], ats), WU[l], bup[l, 0:1])
        store(G.at[l], ats, active)
        store(DG.at[l], ats, slope)
        if product:
            store(PART.at[0], part_pieces(k), dot(active, WD[l], NN).astype(BF))

    def norm_backward(l, which, k, upstream):
        normal, rstd = XH[l, which, k].astype(F32), RSTD[l, which, k]
        VB[0, l, 2 + which : 3 + which] += jnp.sum(upstream * normal, axis=0, keepdims=True)
        VB[0, l, 4 + which : 5 + which] += jnp.sum(upstream, axis=0, keepdims=True)
        scaled = upstream * vec[l, 2 + which : 3 + which]
        grad = rstd * (
            scaled
            - jnp.mean(scaled, axis=-1, keepdims=True)
            - normal * jnp.mean(scaled * normal, axis=-1, keepdims=True)
        )
        VB[0, l, which : which + 1] += jnp.sum(grad, axis=0, keepdims=True)
        return grad

    def second_norm_backward(l, k, upstream):
        grad = norm_backward(l, 1, k, upstream)
        DH[k] = grad
        DF[piece(own, core, k)] = grad.astype(BF)
        gather_start(USUAL, DF, k)

    def ff_backward(l, ats, slot, part_ats):
        grad = (dot(load(DF, ats), WD[l], NT) * load(DG.at[l], ats).astype(F32)).astype(BF)
        store(DU, ats, grad)
        VB[1, l, 0:1, :ff] += jnp.sum(grad.astype(F32), axis=0, keepdims=True)
        store(PART.at[slot], part_ats, dot(grad, WU[l], NT).astype(BF))

    def ff_backward_own(l):
        ats = [piece(own, c, k) for c in range(2) for k in range(2)]
        part_ats = [slice(i * block, (i + 1) * block) for i in range(4)]
        ff_backward(l, ats, 1, part_ats)

    def first_norm_backward(l, k):
        grad = norm_backward(l, 0, k, DH[k] + sum_end(k))
        DY[k] = grad
        DG[l, piece(own, core, k)] = grad.astype(BF)
        gather_start(USUAL, DG.at[l], k)

    def attention_backward(l, r, slot, start):
        DCT[...] = dot(WO[l], DG[l, rows_of(r, 0, seq)], NT).astype(BF)

        def head(h, carry):
            o = h * HEAD_DIM
            q_at, k_at, v_at = (pl.ds(aligned(c * n_head + o), HEAD_DIM) for c in range(3))
            dct = DCT[q_at]
            probs = PT[l, r, h].astype(F32)
            weighted = probs * dot(QKVT[l, r, v_at], dct, TN)
            mean = jnp.sum(weighted, axis=0, keepdims=True)
            DST[...] = (weighted - probs * mean).astype(BF)
            scale = HEAD_DIM**-0.5
            DPT[slot, q_at] = (dot(QKVT[l, r, k_at], DST[...], NN) * scale).astype(BF)
            DPT[slot, k_at] = (dot(QKVT[l, r, q_at], DST[...], NT) * scale).astype(BF)
            DPT[slot, v_at] = dot(dct, PT[l, r, h], NT).astype(BF)
            return carry

        lax.fori_loop(0, heads, head, 0)
        partial(slot, ((DPT.at[slot], WT.at[l]),), start)
        ones = jnp.ones((8, seq), BF)
        VB[1, l, 1:2, :n_qkv] += dot(ones, DPT[slot], NT)[0:1]

    per_layer = 2 * ff + n_qkv + n_head

    def tokens_product(left, right, base, lo, hi):
        def strip(i, carry):
            at = pl.ds(aligned(i * 256, 256), 256)
            GR[pl.ds(aligned(base + i * 256), 256)] = dot(left[:, at], right[...], TN).astype(BF)
            return carry

        lax.fori_loop(lo, hi, strip, 0)

    def attention_gradients(l, base):
        at = pl.ds(aligned(base), n_qkv)
        both_rows = ((0, other), (1, own))
        GR[at] = sum(dot(DPT[slot], XG[l, rows_of(r, 0, seq)], NN) for slot, r in both_rows).astype(BF)
        at = pl.ds(aligned(base + n_qkv), n_head)
        GR[at] = sum(dot(CT[l, r], DG[l, rows_of(r, 0, seq)], NN) for _, r in both_rows).astype(BF)

    units = layers * per_layer // UNIT
    part = UNIT // 2
    half = part // 2
    stages_x, stages_z = [], []
    always = None

    def stage(who_send, who_recv, device, offset, length, landing=None, add=None, staging=None):
        return (who_send, who_recv, device, offset, length, landing, add, staging)

    keep, give = net.x * half, (1 - net.x) * half
    stages_x.append(stage(always, always, net.x_dev, give, half, RX0, keep, SX0))
    stages_x.append(stage(edge, inner, net.hop_dev, keep, half, RX1, keep, SX1))
    stages_x.append(stage(inner, inner, net.mid_dev, keep, half, RX2, keep))
    for i, device in enumerate(net.outer_devs):
        stages_x.append(stage(inner, inner, device, keep, half, RXO.at[i], keep))
    stages_x.append(stage(inner, edge, net.hop_dev, keep, half))
    stages_x.append(stage(always, always, net.x_dev, keep, half))
    keep, give = part + net.half * half, part + (1 - net.half) * half
    stages_z.append(stage(edge, inner, net.hop_dev, part, part, RZ0, part, SZ0))
    stages_z.append(stage(inner, inner, net.mid_dev, give, half, RZ1, keep, SZ1))
    stages_z.append(stage(inner, inner, net.x_dev, keep, half, RZ2, keep))
    for i, device in enumerate(net.outer_devs):
        stages_z.append(stage(inner, inner, device, keep, half, RZO.at[i], keep))
    stages_z.append(stage(inner, inner, net.mid_dev, keep, half))
    stages_z.append(stage(inner, edge, net.hop_dev, part, part))
    depth = len(stages_x)
    hops = {0: (stages_z, credit_z), 1: (stages_x, credit_x)}

    def when(condition, body):
        if condition is None:
            body()
        else:
            pl.when(condition)(body)

    def stage_copy(which, s, u):
        _, _, device, offset, length, landing, _, staging = which[0][s]
        src = GR.at[pl.ds(aligned(u * UNIT + offset), length)]
        dst = src if landing is None else landing.at[u % SLOTS]
        src = src if staging is None else staging.at[u % SPACING]
        return remote(src, dst, which[1].at[u, s], which[2].at[u, s], device)

    def last_of(which):
        return units if which[0] is stages_x else units - 1

    def live(which, u):
        return (u >= 0) & (u <= last_of(which))

    def credit_of(which, s):
        return hops[s][1] if s in hops and hops[s][0] is which[0] else None

    def stage_send(which, s, u):
        who_send, _, _, offset, length, _, _, staging = which[0][s]

        def send():
            if credit_of(which, s) is not None:

                @pl.when(u >= SLOTS)
                def _():
                    pl.semaphore_wait(credit_of(which, s), 1)

            if staging is not None:
                staging[u % SPACING] = GR[pl.ds(aligned(u * UNIT + offset), length)]
            stage_copy(which, s, u).start()

        when(who_send, send)

    def stage_sent(which, s, u):
        when(which[0][s][0], lambda: stage_copy(which, s, u).wait_send())

    def stage_recv(which, s, u):
        _, who_recv, device, _, length, landing, add, _ = which[0][s]

        def take():
            stage_copy(which, s, u).wait_recv()
            if landing is not None:
                at = pl.ds(aligned(u * UNIT + add), length)
                GR[at] = (GR[at].astype(F32) + landing[u % SLOTS].astype(F32)).astype(BF)
            if credit_of(which, s) is not None:

                @pl.when(u < last_of(which) + 1 - SLOTS)
                def _():
                    pl.semaphore_signal(credit_of(which, s), inc=1, device_id=device, device_id_type=MESH)

        when(who_recv, take)

    both = ((stages_x, arx_s, arx_r), (stages_z, arz_s, arz_r))
    per_units = per_layer // UNIT
    sections = (
        (ff // UNIT, grad_down, 0),
        (2 * ff // UNIT, grad_up, ff),
        (per_units, grad_in, 2 * ff),
        (per_units, grad_out, 2 * ff + n_qkv),
    )
    at_place = (1, 1, 1, 1, 2, 1, 1, 1, 1, 1, 1, 1, 2, 2, 1)
    before = [sum(at_place[:e]) * per_units // sum(at_place) for e in range(len(at_place) + 1)]
    down_done, up_done, all_done = 4, 6, 13
    lag = before[down_done]
    assert before[down_done + 1] <= lag + 256 // UNIT
    assert before[up_done] <= lag + ff // UNIT and before[all_done] <= lag + 2 * ff // UNIT

    def out_copy(i, k):
        _, out, base = sections[k]
        out = out.at[layers - 1 - i]
        src = GR.at[pl.ds(aligned(i * per_layer + base), out.shape[0])]
        return pltpu.make_async_copy(src, out, osem.at[i, k])

    def unit_done(u):
        i, own = u // per_units, u % per_units
        for k, (end, _, _) in enumerate(sections):

            @pl.when((own == end - 1) & (u < units))
            def _(k=k):
                out_copy(i, k).start()

    def tick(now, carry=0):
        t = now - lag
        for s in range(depth):
            u = t - SPACING * (s + 1)
            for which in both:
                pl.when(live(which, u))(functools.partial(stage_sent, which, s, u))
        for which in both:
            pl.when(live(which, t))(functools.partial(stage_send, which, 0, t))
        for s in range(depth):
            u = t - SPACING * (s + 1)
            for which in both:

                @pl.when(live(which, u))
                def _(which=which, s=s, u=u):
                    stage_recv(which, s, u)
                    if s + 1 < depth:
                        stage_send(which, s + 1, u)

        u = t - SPACING * depth
        pl.when((u >= 0) & (u < units))(functools.partial(unit_done, u))
        return carry

    for r in range(rows):
        XG[0, piece(r, core, own)] = x_in[:, r, :]
    for k in range(2):
        gather_start(INPUT, XG.at[0], k)

    VB[...] = jnp.zeros(VB.shape, F32)
    BS[...] = jnp.zeros(BS.shape, F32)
    BS[0:1, :ff] = up_bias[last : last + 1].astype(F32)
    BS[8:10, :n_head] = in_bias[last].astype(F32)
    swap(BIASES, BS, BY).start()
    diagonal = lax.broadcasted_iota(jnp.int32, (n_head, n_head), 0) == lax.broadcasted_iota(
        jnp.int32, (n_head, n_head), 1
    )

    def columns(out, two_rows):
        for c, at in ((0, 0), (1, 2 * n_head)):
            spread = jnp.where(diagonal, two_rows[c : c + 1], 0.0)
            out[at : at + n_head] = jnp.sum(spread, axis=1, keepdims=True)
        out[n_head : 2 * n_head] = jnp.zeros((n_head, 1), F32)

    for l in range(layers):
        vec[l, 0:2] = branch_bias[l].astype(F32)
        vec[l, 2:4] = norm_gain[l].astype(F32)
        vec[l, 4:6] = norm_shift[l].astype(F32)
        bup[l, 0:1] = up_bias[l : l + 1].astype(F32)
        columns(bcol.at[l], in_bias[l].astype(F32))
    for r in range(rows):
        for ref, shape, axis in ((segc, (seq, 1), 0), (segr, (1, seq), 1)):
            index = lax.broadcasted_iota(jnp.int32, shape, axis)
            position = (index // block % 2 * 2 + index // half_seq) * block + index % block
            text, end = jnp.zeros(shape, jnp.int32), 0
            for j in range(lengths.shape[1]):
                end = end + lengths[r, j]
                text = text + jnp.where(position >= end, 1, 0)
            ref[r] = jnp.where(position >= seq - padding[r], lengths.shape[1], text)
    first, second = cot[:, 0, :].astype(F32), cot[:, 1, :].astype(F32)
    CB[0] = jnp.where(own == 0, second, first).astype(BF)
    CB[2] = jnp.where(own == 0, first, second).astype(BF)
    for copy in weight_copies:
        copy.wait()

    def attention_product(l, r, slot, start):
        partial(slot, ((CT.at[l, r], WO.at[l]),), start)

    def forward_layer(l):
        group, buf = (INPUT if l == 0 else LAYER_IN), XG.at[l]
        if l == 0:
            weights_0(0)
            gather_pass(group, buf, 0)
            gather_copy(group, buf, 1, ACROSS).wait_recv()
            other_ready(group, buf, 0)
        else:
            for k in range(2):
                gather_pass(group, buf, k)
            own_ready(group, buf)
            for k in range(2):
                other_ready(group, buf, k)
        attention_forward(l, other)
        attention_product(l, other, 0, far_start)
        if l == 0:
            gather_pass(group, buf, 1)
        for k in range(2):
            sum_pass(k)
        if l == 0:
            weights_1(0)
            weights_0(1)
            gather_copy(group, buf, 0, ACROSS).wait_recv()
            other_ready(group, buf, 1)
            for k in range(2):
                XRES[k] = XG[0, piece(own, core, k)].astype(F32)
        attention_forward(l, own)
        attention_product(l, own, 1, near_start)
        if l == 0:
            weights_2(0)
        gather_sent(group, buf)
        for k in range(2):
            first_norm(l, k, sum_end(k), USUAL)
        if l == 0:
            weights_3(0)
        buf = HG.at[l]
        own_ready(USUAL, buf)
        ff_forward_own(l)
        PART[1] = dot(G[l, rows_of(own, 0, seq)], WD[l], NN).astype(BF)
        for k in range(2):
            near_start(k)
        if l == 0:
            weights_1(1)
            weights_4(0)
        gather_pass(USUAL, buf, 0)
        other_ready(USUAL, buf, 0)
        ff_forward_other(l, 0)
        far_start(0)
        gather_pass(USUAL, buf, 1)
        sum_pass(0)
        other_ready(USUAL, buf, 1)
        ff_forward_other(l, 1)
        far_start(1)
        if l == 0:
            weights_2(1)
        sum_pass(1)
        gather_sent(USUAL, buf)
        for k in range(2):
            XG[l + 1, piece(own, core, k)] = second_norm(l, k, sum_end(k))
            gather_start(LAYER_IN, XG.at[l + 1], k)

    def forward_last():
        l = last
        swap(UPSTREAM, CB.at[0], CB.at[1]).start()
        weights_3(1)
        own_ready(LAYER_IN, XG.at[l])
        attention_forward(l, own)
        weights_5(0)
        swap(BIASES, BS, BY).wait()
        columns(bcol_y, BY[8:10, :n_head])
        neighbour_attention_forward()
        both = ((CT.at[l, own], WO.at[l]), (DCT, GR.at[n_qkv : n_qkv + n_head]))
        partial(1, both, near_start)
        weights_4(1)
        for k in range(2):
            gather_pass(LAYER_IN, XG.at[l], k)
        for k in range(2):
            first_norm(l, k, pair_end(k), FF_IN)
        up_y = n_qkv + n_head
        down_y = up_y + width

        def ff_own_units(c):
            at = rows_of(own, c * half_seq, half_seq)
            G[l, at], DG[l, at] = ff_active(HG[l, at], WU[l], bup[l, 0:1])

        def ff_product(c):
            at = rows_of(own, c * half_seq, half_seq)
            active, _ = ff_active(HG[l, at], GR[up_y:down_y], BY[0:1, :ff])
            product = dot(G[l, at], WD[l], NN) + dot(active, GR[down_y : down_y + ff], NN)
            PART[1, pl.ds(aligned(c * half_seq), half_seq)] = product.astype(BF)

        ff_own_units(core)
        own_ready(FF_IN, HG.at[l])
        ff_own_units(1 - core)
        weights_5(1)
        ff_product(1 - core)
        for k in range(2):
            near_start(k)
        ff_product(core)
        swap(UPSTREAM, CB.at[0], CB.at[1]).wait()
        for k in range(2):
            YB[k] = second_norm(l, k, pair_end(k))
            block_of = jnp.where(own == k, CB[2].astype(F32), CB[1].astype(F32))
            second_norm_backward(l, k, block_of)
        swap(HIDDEN, YB.at[other], YB.at[2]).start()

    for l in range(last):
        forward_layer(l)
    forward_last()

    def backward(i, carry):
        l = last - i
        base = i * per_layer

        def place(e):
            for k in range(before[e], before[e + 1]):
                tick(i * per_units + k)

        place(0)
        own_ready(USUAL, DF)
        ff_backward_own(l)
        for k in range(2):
            near_start(k)
        place(1)

        @pl.when(l == last)
        def _():
            for k in range(2):
                other_ready(LAYER_IN, XG.at[last], k)
            gather_sent(LAYER_IN, XG.at[last])
            attention_forward(last, other)
            for k in range(2):
                gather_pass(FF_IN, HG.at[last], k)
            for k in range(2):
                other_ready(FF_IN, HG.at[last], k)
                ff_forward_other(last, k, product=False)
            gather_sent(FF_IN, HG.at[last])

        gather_pass(USUAL, DF, 0)
        place(2)
        other_ready(USUAL, DF, 0)
        ff_backward(l, pieces_of(other, 0), 0, part_pieces(0))
        far_start(0)
        gather_pass(USUAL, DF, 1)
        sum_pass(0)
        place(3)
        other_ready(USUAL, DF, 1)
        tokens_product(G.at[l], DF, base, 0, 1)
        place(4)
        tokens_product(G.at[l], DF, base, 1, ff // 256)
        ff_backward(l, pieces_of(other, 1), 0, part_pieces(1))
        far_start(1)
        place(5)
        sum_pass(1)
        tokens_product(HG.at[l], DU, base + ff, 0, width // 256)
        place(6)
        gather_sent(USUAL, DF)
        first_norm_backward(l, 0)
        place(7)
        first_norm_backward(l, 1)
        place(8)
        buf = DG.at[l]
        own_ready(USUAL, buf)
        attention_backward(l, own, 1, near_start)
        place(9)
        gather_pass(USUAL, buf, 0)
        place(10)
        gather_pass(USUAL, buf, 1)
        place(11)
        for k in range(2):
            other_ready(USUAL, buf, k)
        attention_backward(l, other, 0, far_start)
        place(12)
        for k in range(2):
            sum_pass(k)
        attention_gradients(l, base + 2 * ff)
        place(13)
        gather_sent(USUAL, buf)
        for k in range(2):
            DY[k] = DY[k] + sum_end(k)

            @pl.when(l > 0)
            def _(k=k):
                second_norm_backward(l - 1, k, DY[k])

            if k == 0:
                place(14)

        return carry

    lax.fori_loop(0, layers, backward, 0)
    swap(GRADIENT, DY.at[other], DH.at[0]).start()
    swap(HIDDEN, YB.at[other], YB.at[2]).wait()
    mine, theirs = YB[own].astype(F32), YB[2].astype(F32)
    for r in range(rows):
        hidden_out[:, r, :] = jnp.where(own == r, mine, theirs).astype(BF)

    def vector_copy(k):
        return remote(VB.at[0], RV.at[k], v_s.at[k], v_r.at[k], (net.core, net.y)[k])

    now = layers * per_units
    for k in range(2):
        vector_copy(k).start()
        lax.fori_loop(now, now + lag // 2, tick, 0)
        now += lag // 2
        vector_copy(k).wait()
        VB[0] += RV[k]
    base = layers * per_layer
    GR[base : base + UNIT] = jnp.zeros((UNIT, width), BF)
    GR[base : base + 16 * layers] = VB[...].reshape(16 * layers, width).astype(BF)
    lax.fori_loop(now, lag + units + 1 + SPACING * depth, tick, 0)
    small[...] = GR[base : base + 16 * layers].astype(F32)
    swap(GRADIENT, DY.at[other], DH.at[0]).wait()
    for r in range(rows):
        grad_hidden[:, r, :] = jnp.where(own == r, DY[own], DH[0])
    for i in range(layers):
        for k in range(len(sections)):
            out_copy(i, k).wait()


def local(
    hidden_in,
    cotangent,
    doc_lengths,
    pad_count,
    input_weight,
    input_bias,
    output_weight,
    up_weight,
    up_bias,
    down_weight,
    branch_bias,
    norm_gain,
    norm_shift,
):
    n_dp = lax.axis_size("dp")
    block, rows, width = hidden_in.shape
    seq = block * lax.axis_size("tensor")
    layers, _, _, n_head = input_weight.shape
    n_qkv, heads, ff = 3 * n_head, n_head // HEAD_DIM, up_weight.shape[2]
    tokens = rows * seq
    wt = jnp.swapaxes(input_weight, 2, 3).reshape(layers, n_qkv, width)
    per_layer = 2 * ff + n_qkv + n_head
    part = UNIT // 2
    outer = 0
    while 8 << outer < n_dp:
        outer += 1
    depth = 5 + outer
    vmem = pltpu.VMEM
    dma = pltpu.SemaphoreType.DMA
    scratch = [
        vmem((layers, n_qkv, width), BF),
        vmem((layers, n_head, width), BF),
        vmem((layers, width, ff), BF),
        vmem((layers, ff, width), BF),
        vmem((layers, tokens, width), BF),
        vmem((layers, tokens, width), BF),
        vmem((layers, tokens, ff), BF),
        vmem((layers, tokens, ff), BF),
        vmem((tokens, width), BF),
        vmem((tokens, ff), BF),
        vmem((layers, rows, n_qkv, seq), BF),
        vmem((layers, rows, heads, seq, seq), BF),
        vmem((layers, rows, n_head, seq), BF),
        vmem((rows, n_qkv, seq), BF),
        vmem((seq, seq), BF),
        vmem((n_head, seq), BF),
        vmem((rows, seq, width), BF),
        vmem((rows, 3, block, width), BF),
        vmem((rows, block, width), F32),
        vmem((rows, block, width), F32),
        vmem((layers, 2, rows, block, width), BF),
        vmem((layers, 2, rows, block, 1), F32),
        vmem((layers * per_layer + UNIT, width), BF),
        vmem((SLOTS, part // 2, width), BF),
        vmem((SLOTS, part // 2, width), BF),
        vmem((SLOTS, part // 2, width), BF),
        vmem((SLOTS, part, width), BF),
        vmem((SLOTS, part // 2, width), BF),
        vmem((SLOTS, part // 2, width), BF),
        vmem((max(outer, 1), SLOTS if outer else 1, part // 2, width), BF),
        vmem((max(outer, 1), SLOTS if outer else 1, part // 2, width), BF),
        vmem((SPACING, part // 2, width), BF),
        vmem((SPACING, part // 2, width), BF),
        vmem((SPACING, part, width), BF),
        vmem((SPACING, part // 2, width), BF),
        vmem((2, layers, 8, width), F32),
        vmem((2, layers, 8, width), F32),
        vmem((rows, seq, 1), jnp.int32),
        vmem((rows, 1, seq), jnp.int32),
        vmem((layers, n_qkv, 1), F32),
        vmem((n_qkv, 1), F32),
        vmem((layers, 8, ff), F32),
        vmem((layers, 8, width), F32),
        vmem((16, max(ff, n_head)), F32),
        vmem((16, max(ff, n_head)), F32),
        vmem((3, block, width), BF),
        vmem((3, block, width), BF),
        dma((4,)),
        dma((4, 2, 3)),
        dma((4, 2, 3)),
        dma((2, 3)),
        dma((2, 3)),
        dma((layers * per_layer // UNIT + 1, depth)),
        dma((layers * per_layer // UNIT + 1, depth)),
        dma((layers * per_layer // UNIT + 1, depth)),
        dma((layers * per_layer // UNIT + 1, depth)),
        dma((2,)),
        dma((2,)),
        dma((layers, 4)),
        pltpu.SemaphoreType.REGULAR,
        pltpu.SemaphoreType.REGULAR,
        dma((2, 10)),
        dma((2, 10)),
        dma((4,)),
        dma((4,)),
    ]
    whole, anywhere = pl.BlockSpec(memory_space=vmem), pl.BlockSpec(memory_space=pl.ANY)
    scalars = pl.BlockSpec(memory_space=pltpu.SMEM)
    results = pl.pallas_call(
        functools.partial(kernel, n_dp, layers),
        out_shape=(
            jax.ShapeDtypeStruct(hidden_in.shape, BF),
            jax.ShapeDtypeStruct(hidden_in.shape, F32),
            jax.ShapeDtypeStruct((layers, n_qkv, width), BF),
            jax.ShapeDtypeStruct(output_weight.shape, BF),
            jax.ShapeDtypeStruct(up_weight.shape, BF),
            jax.ShapeDtypeStruct(down_weight.shape, BF),
            jax.ShapeDtypeStruct((16 * layers, width), F32),
        ),
        in_specs=[whole, whole, scalars, scalars, anywhere, whole, anywhere, anywhere, whole, anywhere]
        + [whole] * 3,
        out_specs=(whole, whole, anywhere, anywhere, anywhere, anywhere, whole),
        scratch_shapes=scratch,
        compiler_params=pltpu.CompilerParams(
            collective_id=0, has_side_effects=True, vmem_limit_bytes=63 << 20
        ),
    )(
        hidden_in,
        cotangent,
        doc_lengths,
        pad_count,
        wt,
        input_bias,
        output_weight,
        up_weight,
        up_bias,
        down_weight,
        branch_bias,
        norm_gain,
        norm_shift,
    )
    pieces = 1

    def strip(array):
        return pl.BlockSpec((1, array.shape[1] // pieces, width), lambda l, c: (l, c, 0))

    strips = [strip(array) for array in results[2:6]]
    fixed = [
        jax.ShapeDtypeStruct(shape, F32)
        for shape in (input_bias.shape, up_bias.shape, branch_bias.shape, norm_gain.shape, norm_shift.shape)
    ]
    hidden_out, grad_hidden, grad_in, grad_out, grad_up, grad_down, *vectors = pl.pallas_call(
        functools.partial(finish, layers, pieces),
        grid=(layers, pieces),
        out_shape=[jax.ShapeDtypeStruct(array.shape, array.dtype) for array in results[:2]]
        + [jax.ShapeDtypeStruct(array.shape, F32) for array in results[2:6]]
        + fixed,
        in_specs=[whole] * 2 + strips + [whole],
        out_specs=[whole] * 2 + strips + [whole] * 5,
    )(*results)
    grad_in_bias, grad_up_bias, grad_branch, grad_gain, grad_shift = vectors
    grad_in = jnp.swapaxes(grad_in.reshape(layers, 3, n_head, width), 2, 3)
    return (
        hidden_out,
        grad_hidden,
        grad_in,
        grad_in_bias,
        grad_out,
        grad_up,
        grad_up_bias,
        grad_down,
        grad_branch,
        grad_gain,
        grad_shift,
    )


def finish(layers, pieces, *refs):
    hidden, grad_hidden, *grads = refs[:6]
    small = refs[6]
    hidden_out, grad_hidden_out, *outs = refs[7:13]
    grad_in_bias, grad_up_bias, grad_branch, grad_gain, grad_shift = refs[13:18]
    step = pl.program_id(0) * pieces + pl.program_id(1)

    @pl.when(step == 0)
    def _():
        hidden_out[...] = hidden[...]
        grad_hidden_out[...] = grad_hidden[...]
        n_head, ff = grad_in_bias.shape[2], grad_up_bias.shape[1]
        for l in range(layers):
            shared, split = 8 * l, 8 * (layers + l)
            grad_branch[l] = small[shared : shared + 2]
            grad_gain[l] = small[shared + 2 : shared + 4]
            grad_shift[l] = small[shared + 4 : shared + 6]
            grad_up_bias[l : l + 1] = small[split : split + 1, :ff]
            for c in range(2):
                grad_in_bias[l, c : c + 1] = small[split + 1 : split + 2, 2 * c * n_head : (2 * c + 1) * n_head]

    for grad, out in zip(grads, outs, strict=True):
        out[...] = grad[...].astype(F32)


def solution(mesh):
    return jax.shard_map(
        local,
        mesh=mesh,
        in_specs=(
            P("tensor", "dp", None),
            P("tensor", "dp", None),
            P("dp", None),
            P("dp"),
            P(None, None, None, "tensor"),
            P(None, None, "tensor"),
            P(None, "tensor", None),
            P(None, None, "tensor"),
            P(None, "tensor"),
            P(None, "tensor", None),
            P(),
            P(),
            P(),
        ),
        out_specs=(
            P("tensor", "dp", None),
            P("tensor", "dp", None),
            P(None, None, None, "tensor"),
            P(None, None, "tensor"),
            P(None, "tensor", None),
            P(None, None, "tensor"),
            P(None, "tensor"),
            P(None, "tensor", None),
            P(),
            P(),
            P(),
        ),
        check_vma=False,
    )
```

```python
import functools

import jax
import jax.numpy as jnp
from jax import lax
from jax.experimental import pallas as pl
from jax.experimental.pallas import tpu as pltpu
from jax.sharding import PartitionSpec as P

HEAD_DIM = 64
EPSILON = 1e-05
MASKED = -1e30
MESH = pl.DeviceIdType.MESH
BF, F32 = jnp.bfloat16, jnp.float32
NN = (((1,), (0,)), ((), ()))
NT = (((1,), (1,)), ((), ()))
TN = (((0,), (0,)), ((), ()))
UNIT = 128
SPACING, SLOTS = 2, 6


def dot(a, b, dims):
    return lax.dot_general(a, b, dims, preferred_element_type=F32)


def aligned(value, by=16):
    return pl.multiple_of(value, by)


class Net:
    def __init__(self, n_dp):
        dp, t = lax.axis_index("dp"), lax.axis_index("tensor")
        self.dp, self.t = dp, t
        self.own, self.c = t // 2, t % 2
        self.other = 1 - self.own
        self.core, self.y = (dp, t + 1 - 2 * self.c), (dp, t + 2 - 4 * self.own)
        self.x = dp % 2
        self.z = z = (dp // 2) % 4
        self.half = z // 2
        self.inner = (z == 1) | (z == 2)
        self.inner_count = (z + 1) // 2 % 2
        self.edge = (z == 0) | (z == 3)
        self.x_dev = (dp + 1 - 2 * self.x, t)
        self.hop_dev = (dp + 2 * (1 - 2 * (z % 2)), t)
        self.mid_dev = (dp + 2 * (3 - 2 * z), t)
        self.outer_devs = []
        step = 8
        while step < n_dp:
            self.outer_devs.append((dp + step * (1 - 2 * ((dp // step) % 2)), t))
            step *= 2
        self.partners = [self.core, self.y, self.x_dev, self.hop_dev]
        self.inner_partners = [self.mid_dev] + self.outer_devs


def remote(src, dst, send, recv, device):
    return pltpu.make_async_remote_copy(
        src_ref=src, dst_ref=dst, send_sem=send, recv_sem=recv, device_id=device, device_id_type=MESH
    )


def kernel(n_dp, layers, *refs):
    (x_in, cot, lengths, padding, wt_h, in_bias, wo_h, wu_h, up_bias, wd_h, branch_bias, norm_gain, norm_shift,
     hidden_out, grad_hidden, grad_in, grad_out, grad_up, grad_down, small,
     WT, WO, WU, WD, XG, HG, G, DG, DF, DU, QKVT, PT, CT, DPT, DST, DCT, PART, RB, XRES, HRES, XH, RSTD, GR,
     RX0, RX1, RX2, RZ0, RZ1, RZ2, RXO, RZO, SX0, SX1, SZ0, SZ1, VB, RV, segc, segr, bcol, bcol_y, bup, vec,
     BS, BY, CB, YB,
     wsem, ag_s, ag_r, rs_s, rs_r, arx_s, arx_r, arz_s, arz_r, v_s, v_r, osem, credit_x, credit_z,
     wg_s, wg_r, ex_s, ex_r) = refs
    DY, DH = XRES, HRES
    net = Net(n_dp)
    block, rows, width = x_in.shape
    seq = PART.shape[1]
    half_seq = seq // 2
    own, other, core = net.own, net.other, net.c
    last = layers - 1
    n_qkv = WT.shape[1]
    n_head = n_qkv // 3
    heads = n_head // HEAD_DIM
    ff = WU.shape[2]

    weight_copies = [
        pltpu.make_async_copy(a, b, wsem.at[i])
        for i, (a, b) in enumerate(((wt_h, WT), (wo_h, WO), (wu_h, WU), (wd_h, WD)))
    ]
    for copy in weight_copies:
        copy.start()

    barrier = pltpu.get_barrier_semaphore()
    for device in net.partners:
        pl.semaphore_signal(barrier, inc=1, device_id=device, device_id_type=MESH)

    @pl.when(net.inner)
    def _():
        for device in net.inner_partners:
            pl.semaphore_signal(barrier, inc=1, device_id=device, device_id_type=MESH)

    pl.semaphore_wait(barrier, len(net.partners) + net.inner_count * len(net.inner_partners))

    def rows_of(r, start, size):
        return pl.ds(aligned(r * seq + start), size)

    def piece(r, c, k):
        return rows_of(r, c * half_seq + k * block, block)

    ALONG, ACROSS, ONWARD = 0, 1, 2
    INPUT, USUAL, LAYER_IN, FF_IN = range(4)

    def gather_copy(group, buf, k, kind):
        if group == INPUT:
            first, second = (other, own) if kind == ONWARD else (own, other)
            at = piece((first, second)[k], core, other if kind == ONWARD else own)
        else:
            at = piece(other if kind == ONWARD else own, core, k)
        at = buf.at[at]
        return remote(at, at, ag_s.at[group, k, kind], ag_r.at[group, k, kind], net.y if kind == ALONG else net.core)

    def gather_start(group, buf, k):
        gather_copy(group, buf, k, ALONG).start()
        gather_copy(group, buf, k, ACROSS).start()

    def gather_pass(group, buf, k):
        gather_copy(group, buf, k, ALONG).wait_recv()
        gather_copy(group, buf, k, ONWARD).start()

    def own_ready(group, buf):
        for k in range(2):
            gather_copy(group, buf, k, ACROSS).wait_recv()

    def other_ready(group, buf, k):
        gather_copy(group, buf, k, ONWARD).wait_recv()

    def gather_sent(group, buf):
        for k in range(2):
            for kind in (ALONG, ACROSS, ONWARD):
                gather_copy(group, buf, k, kind).wait_send()

    FAR, NEAR, SUMMED = 0, 1, 2

    def sum_copy(k, kind):
        at = pl.ds(aligned((core if kind == SUMMED else 1 - core) * half_seq + k * block), block)
        src = PART.at[1 if kind == NEAR else 0, at]
        return remote(src, RB.at[k, kind], rs_s.at[k, kind], rs_r.at[k, kind], net.y if kind == SUMMED else net.core)

    def far_start(k):
        sum_copy(k, FAR).start()

    def near_start(k):
        sum_copy(k, NEAR).start()

    def sum_pass(k):
        sum_copy(k, FAR).wait_recv()
        at = pl.ds(aligned(core * half_seq + k * block), block)
        PART[0, at] = (PART[0, at].astype(F32) + RB[k, FAR].astype(F32)).astype(BF)
        sum_copy(k, SUMMED).start()

    def pair_end(k):
        sum_copy(k, NEAR).wait_recv()
        sum_copy(k, NEAR).wait_send()
        at = pl.ds(aligned(core * half_seq + k * block), block)
        return PART[1, at].astype(F32) + RB[k, NEAR].astype(F32)

    def sum_end(k):
        total = pair_end(k)
        sum_copy(k, SUMMED).wait_recv()
        for kind in (FAR, SUMMED):
            sum_copy(k, kind).wait_send()
        return total + RB[k, SUMMED].astype(F32)

    eighth, z, x = net.dp % 8, net.z, net.x
    hop_z, mid_z = z + 1 - 2 * (z % 2), 3 - z
    parts = (
        (0, (n_qkv + n_head) // 8, 6, WT, WO),
        (n_qkv + n_head, 2 * ff // 8, 4, WU, WD),
    )
    inner, edge = net.inner, net.edge
    FROM_Y, HOP_OWN, MID_OWN, MID_ON, HOP_ON, HOP_LAST, ALONG_X = range(7)

    def weight_copy(g, kind, zz, device, src=None):
        base, n = parts[g][:2]
        at = GR.at[pl.ds(aligned(base + (2 * zz + x) * n), n)]
        slot = ALONG_X + zz if kind == ALONG_X else kind
        return remote(at if src is None else src, at, wg_s.at[g, slot], wg_r.at[g, slot], device)

    def weight_on(g, zz):
        weight_copy(g, ALONG_X, zz, net.x_dev).start()

    def weights_0(g):
        _, n, split, first, second = parts[g]

        @pl.when(eighth < split)
        def _():
            weight_copy(g, FROM_Y, z, net.y, first.at[last, pl.ds(aligned(eighth * n), n)]).start()

        @pl.when(eighth >= split)
        def _():
            weight_copy(g, FROM_Y, z, net.y, second.at[last, pl.ds(aligned((eighth - split) * n), n)]).start()

    def weights_1(g):
        weight_copy(g, FROM_Y, z, net.y).wait_recv()
        weight_copy(g, HOP_OWN, z, net.hop_dev).start()

        @pl.when(inner)
        def _():
            weight_copy(g, MID_OWN, z, net.mid_dev).start()

        weight_on(g, z)

    def weights_2(g):
        weight_copy(g, HOP_OWN, hop_z, net.hop_dev).wait_recv()

        @pl.when(inner)
        def _():
            weight_copy(g, MID_ON, hop_z, net.mid_dev).start()
            weight_copy(g, MID_OWN, mid_z, net.mid_dev).wait_recv()
            weight_copy(g, HOP_ON, mid_z, net.hop_dev).start()
            weight_on(g, mid_z)

        weight_on(g, hop_z)

    def weights_3(g):
        @pl.when(inner)
        def _():
            weight_copy(g, MID_ON, 3 - hop_z, net.mid_dev).wait_recv()
            weight_copy(g, HOP_LAST, 3 - hop_z, net.hop_dev).start()

        @pl.when(edge)
        def _():
            weight_copy(g, HOP_ON, 3 - hop_z, net.hop_dev).wait_recv()

        weight_on(g, 3 - hop_z)

    def weights_4(g):
        @pl.when(edge)
        def _():
            weight_copy(g, HOP_LAST, mid_z, net.hop_dev).wait_recv()
            weight_on(g, mid_z)

    def weights_5(g):
        for zz in range(4):
            weight_copy(g, ALONG_X, zz, net.x_dev).wait_recv()
            weight_copy(g, ALONG_X, zz, net.x_dev).wait_send()
        weight_copy(g, FROM_Y, z, net.y).wait_send()
        weight_copy(g, HOP_OWN, z, net.hop_dev).wait_send()

        @pl.when(inner)
        def _():
            weight_copy(g, MID_OWN, z, net.mid_dev).wait_send()
            weight_copy(g, MID_ON, hop_z, net.mid_dev).wait_send()
            weight_copy(g, HOP_ON, mid_z, net.hop_dev).wait_send()
            weight_copy(g, HOP_LAST, 3 - hop_z, net.hop_dev).wait_send()

    BIASES, UPSTREAM, HIDDEN, GRADIENT = range(4)

    def swap(which, src, dst):
        return remote(src, dst, ex_s.at[which], ex_r.at[which], net.y)

    def attend(r, xg, wt, bias, qkvt, probs_of, ct):
        for c in range(3):
            at = slice(c * n_head, (c + 1) * n_head)
            qkvt[at] = (dot(wt[at], xg, NT) + bias[at]).astype(BF)

        def head(h, carry):
            o = h * HEAD_DIM
            kt = qkvt[pl.ds(aligned(n_head + o), HEAD_DIM)] * jnp.asarray(HEAD_DIM**-0.5, BF)
            vt = qkvt[pl.ds(aligned(2 * n_head + o), HEAD_DIM)]
            qt = qkvt[pl.ds(aligned(o), HEAD_DIM)]
            scores = jnp.where(segc[r] == segr[r], dot(kt, qt, TN), MASKED)
            powers = jnp.exp(scores - jnp.max(scores, axis=0, keepdims=True))
            probs = (powers * (1.0 / jnp.sum(powers, axis=0, keepdims=True))).astype(BF)
            probs_of(h)[...] = probs
            ct[pl.ds(aligned(o), HEAD_DIM)] = dot(vt, probs, NN).astype(BF)
            return carry

        lax.fori_loop(0, heads, head, 0)

    def attention_forward(l, r):
        xg = XG[l, rows_of(r, 0, seq)]
        attend(r, xg, WT.at[l], bcol.at[l], QKVT.at[l, r], lambda h: PT.at[l, r, h], CT.at[l, r])

    def neighbour_attention_forward():
        xg = XG[last, rows_of(own, 0, seq)]
        attend(own, xg, GR.at[:n_qkv], bcol_y, DPT.at[0], lambda h: DST, DCT)

    def partial(slot, products, start):
        for k in range(2):
            for c in range(2):
                at = slice(c * half_seq + k * block, c * half_seq + (k + 1) * block)
                PART[slot, at] = sum(dot(left[:, at], right[...], TN) for left, right in products).astype(BF)
            start(k)

    def norm(l, which, k, value):
        centered = value - jnp.mean(value, axis=-1, keepdims=True)
        rstd = lax.rsqrt(jnp.mean(centered * centered, axis=-1, keepdims=True) + EPSILON)
        normal = centered * rstd
        XH[l, which, k] = normal.astype(BF)
        RSTD[l, which, k] = rstd
        return normal * vec[l, 2 + which : 3 + which] + vec[l, 4 + which : 5 + which]

    def first_norm(l, k, branch, group):
        out = norm(l, 0, k, XRES[k] + branch + vec[l, 0:1])
        HRES[k] = out
        HG[l, piece(own, core, k)] = out.astype(BF)
        gather_start(group, HG.at[l], k)

    def second_norm(l, k, branch):
        out = norm(l, 1, k, HRES[k] + branch + vec[l, 1:2])
        XRES[k] = out
        return out.astype(BF)

    def ff_active(hidden, weight, bias):
        wide = dot(hidden, weight, NN) + bias
        cdf = 0.5 * (1.0 + lax.erf(wide * 0.7071067811865476))
        slope = cdf + wide * 0.3989422804014327 * jnp.exp(-0.5 * wide * wide)
        return (wide * cdf).astype(BF), slope.astype(BF)

    def ff_forward_own(l):
        at = rows_of(own, 0, seq)
        G[l, at], DG[l, at] = ff_active(HG[l, at], WU[l], bup[l, 0:1])

    def pieces_of(r, k):
        return piece(r, 0, k), piece(r, 1, k)

    def load(ref, ats):
        return jnp.concatenate([ref[at] for at in ats], axis=0)

    def store(ref, ats, value):
        for i, at in enumerate(ats):
            ref[at] = value[i * block : (i + 1) * block]

    def part_pieces(k):
        return [slice(c * half_seq + k * block, c * half_seq + (k + 1) * block) for c in range(2)]

    def ff_forward_other(l, k, product=True):
        ats = pieces_of(other, k)
        active, slope = ff_active(load(HG.at[l], ats), WU[l], bup[l, 0:1])
        store(G.at[l], ats, active)
        store(DG.at[l], ats, slope)
        if product:
            store(PART.at[0], part_pieces(k), dot(active, WD[l], NN).astype(BF))

    def norm_backward(l, which, k, upstream):
        normal, rstd = XH[l, which, k].astype(F32), RSTD[l, which, k]
        VB[0, l, 2 + which : 3 + which] += jnp.sum(upstream * normal, axis=0, keepdims=True)
        VB[0, l, 4 + which : 5 + which] += jnp.sum(upstream, axis=0, keepdims=True)
        scaled = upstream * vec[l, 2 + which : 3 + which]
        grad = rstd * (
            scaled
            - jnp.mean(scaled, axis=-1, keepdims=True)
            - normal * jnp.mean(scaled * normal, axis=-1, keepdims=True)
        )
        VB[0, l, which : which + 1] += jnp.sum(grad, axis=0, keepdims=True)
        return grad

    def second_norm_backward(l, k, upstream):
        grad = norm_backward(l, 1, k, upstream)
        DH[k] = grad
        DF[piece(own, core, k)] = grad.astype(BF)
        gather_start(USUAL, DF, k)

    def ff_backward(l, ats, slot, part_ats):
        grad = (dot(load(DF, ats), WD[l], NT) * load(DG.at[l], ats).astype(F32)).astype(BF)
        store(DU, ats, grad)
        VB[1, l, 0:1, :ff] += jnp.sum(grad.astype(F32), axis=0, keepdims=True)
        store(PART.at[slot], part_ats, dot(grad, WU[l], NT).astype(BF))

    def ff_backward_own(l):
        ats = [piece(own, c, k) for c in range(2) for k in range(2)]
        part_ats = [slice(i * block, (i + 1) * block) for i in range(4)]
        ff_backward(l, ats, 1, part_ats)

    def first_norm_backward(l, k):
        grad = norm_backward(l, 0, k, DH[k] + sum_end(k))
        DY[k] = grad
        DG[l, piece(own, core, k)] = grad.astype(BF)
        gather_start(USUAL, DG.at[l], k)

    def attention_backward(l, r, slot, start):
        DCT[...] = dot(WO[l], DG[l, rows_of(r, 0, seq)], NT).astype(BF)

        def head(h, carry):
            o = h * HEAD_DIM
            q_at, k_at, v_at = (pl.ds(aligned(c * n_head + o), HEAD_DIM) for c in range(3))
            dct = DCT[q_at]
            probs = PT[l, r, h].astype(F32)
            weighted = probs * dot(QKVT[l, r, v_at], dct, TN)
            mean = jnp.sum(weighted, axis=0, keepdims=True)
            DST[...] = (weighted - probs * mean).astype(BF)
            scale = HEAD_DIM**-0.5
            DPT[slot, q_at] = (dot(QKVT[l, r, k_at], DST[...], NN) * scale).astype(BF)
            DPT[slot, k_at] = (dot(QKVT[l, r, q_at], DST[...], NT) * scale).astype(BF)
            DPT[slot, v_at] = dot(dct, PT[l, r, h], NT).astype(BF)
            return carry

        lax.fori_loop(0, heads, head, 0)
        partial(slot, ((DPT.at[slot], WT.at[l]),), start)
        ones = jnp.ones((8, seq), BF)
        VB[1, l, 1:2, :n_qkv] += dot(ones, DPT[slot], NT)[0:1]

    per_layer = 2 * ff + n_qkv + n_head

    def tokens_product(left, right, base, lo, hi):
        def strip(i, carry):
            at = pl.ds(aligned(i * 256, 256), 256)
            GR[pl.ds(aligned(base + i * 256), 256)] = dot(left[:, at], right[...], TN).astype(BF)
            return carry

        lax.fori_loop(lo, hi, strip, 0)

    def attention_gradients(l, base):
        at = pl.ds(aligned(base), n_qkv)
        both_rows = ((0, other), (1, own))
        GR[at] = sum(dot(DPT[slot], XG[l, rows_of(r, 0, seq)], NN) for slot, r in both_rows).astype(BF)
        at = pl.ds(aligned(base + n_qkv), n_head)
        GR[at] = sum(dot(CT[l, r], DG[l, rows_of(r, 0, seq)], NN) for _, r in both_rows).astype(BF)

    units = layers * per_layer // UNIT
    part = UNIT // 2
    half = part // 2
    stages_x, stages_z = [], []
    always = None

    def stage(who_send, who_recv, device, offset, length, landing=None, add=None, staging=None):
        return (who_send, who_recv, device, offset, length, landing, add, staging)

    keep, give = net.x * half, (1 - net.x) * half
    stages_x.append(stage(always, always, net.x_dev, give, half, RX0, keep, SX0))
    stages_x.append(stage(edge, inner, net.hop_dev, keep, half, RX1, keep, SX1))
    stages_x.append(stage(inner, inner, net.mid_dev, keep, half, RX2, keep))
    for i, device in enumerate(net.outer_devs):
        stages_x.append(stage(inner, inner, device, keep, half, RXO.at[i], keep))
    stages_x.append(stage(inner, edge, net.hop_dev, keep, half))
    stages_x.append(stage(always, always, net.x_dev, keep, half))
    keep, give = part + net.half * half, part + (1 - net.half) * half
    stages_z.append(stage(edge, inner, net.hop_dev, part, part, RZ0, part, SZ0))
    stages_z.append(stage(inner, inner, net.mid_dev, give, half, RZ1, keep, SZ1))
    stages_z.append(stage(inner, inner, net.x_dev, keep, half, RZ2, keep))
    for i, device in enumerate(net.outer_devs):
        stages_z.append(stage(inner, inner, device, keep, half, RZO.at[i], keep))
    stages_z.append(stage(inner, inner, net.mid_dev, keep, half))
    stages_z.append(stage(inner, edge, net.hop_dev, part, part))
    depth = len(stages_x)
    hops = {0: (stages_z, credit_z), 1: (stages_x, credit_x)}

    def when(condition, body):
        if condition is None:
            body()
        else:
            pl.when(condition)(body)

    def stage_copy(which, s, u):
        _, _, device, offset, length, landing, _, staging = which[0][s]
        src = GR.at[pl.ds(aligned(u * UNIT + offset), length)]
        dst = src if landing is None else landing.at[u % SLOTS]
        src = src if staging is None else staging.at[u % SPACING]
        return remote(src, dst, which[1].at[u, s], which[2].at[u, s], device)

    def last_of(which):
        return units if which[0] is stages_x else units - 1

    def live(which, u):
        return (u >= 0) & (u <= last_of(which))

    def credit_of(which, s):
        return hops[s][1] if s in hops and hops[s][0] is which[0] else None

    def stage_send(which, s, u):
        who_send, _, _, offset, length, _, _, staging = which[0][s]

        def send():
            if credit_of(which, s) is not None:

                @pl.when(u >= SLOTS)
                def _():
                    pl.semaphore_wait(credit_of(which, s), 1)

            if staging is not None:
                staging[u % SPACING] = GR[pl.ds(aligned(u * UNIT + offset), length)]
            stage_copy(which, s, u).start()

        when(who_send, send)

    def stage_sent(which, s, u):
        when(which[0][s][0], lambda: stage_copy(which, s, u).wait_send())

    def stage_recv(which, s, u):
        _, who_recv, device, _, length, landing, add, _ = which[0][s]

        def take():
            stage_copy(which, s, u).wait_recv()
            if landing is not None:
                at = pl.ds(aligned(u * UNIT + add), length)
                GR[at] = (GR[at].astype(F32) + landing[u % SLOTS].astype(F32)).astype(BF)
            if credit_of(which, s) is not None:

                @pl.when(u < last_of(which) + 1 - SLOTS)
                def _():
                    pl.semaphore_signal(credit_of(which, s), inc=1, device_id=device, device_id_type=MESH)

        when(who_recv, take)

    both = ((stages_x, arx_s, arx_r), (stages_z, arz_s, arz_r))
    per_units = per_layer // UNIT
    sections = (
        (ff // UNIT, grad_down, 0),
        (2 * ff // UNIT, grad_up, ff),
        (per_units, grad_in, 2 * ff),
        (per_units, grad_out, 2 * ff + n_qkv),
    )
    at_place = (1, 1, 1, 1, 2, 1, 1, 1, 1, 1, 1, 1, 2, 2, 1)
    before = [sum(at_place[:e]) * per_units // sum(at_place) for e in range(len(at_place) + 1)]
    down_done, up_done, all_done = 4, 6, 13
    lag = before[down_done]
    assert before[down_done + 1] <= lag + 256 // UNIT
    assert before[up_done] <= lag + ff // UNIT and before[all_done] <= lag + 2 * ff // UNIT

    def out_copy(i, k):
        _, out, base = sections[k]
        out = out.at[layers - 1 - i]
        src = GR.at[pl.ds(aligned(i * per_layer + base), out.shape[0])]
        return pltpu.make_async_copy(src, out, osem.at[i, k])

    def unit_done(u):
        i, own = u // per_units, u % per_units
        for k, (end, _, _) in enumerate(sections):

            @pl.when((own == end - 1) & (u < units))
            def _(k=k):
                out_copy(i, k).start()

    def tick(now, carry=0):
        t = now - lag
        for s in range(depth):
            u = t - SPACING * (s + 1)
            for which in both:
                pl.when(live(which, u))(functools.partial(stage_sent, which, s, u))
        for which in both:
            pl.when(live(which, t))(functools.partial(stage_send, which, 0, t))
        for s in range(depth):
            u = t - SPACING * (s + 1)
            for which in both:

                @pl.when(live(which, u))
                def _(which=which, s=s, u=u):
                    stage_recv(which, s, u)
                    if s + 1 < depth:
                        stage_send(which, s + 1, u)

        u = t - SPACING * depth
        pl.when((u >= 0) & (u < units))(functools.partial(unit_done, u))
        return carry

    for r in range(rows):
        XG[0, piece(r, core, own)] = x_in[:, r, :]
    for k in range(2):
        gather_start(INPUT, XG.at[0], k)

    VB[...] = jnp.zeros(VB.shape, F32)
    BS[...] = jnp.zeros(BS.shape, F32)
    BS[0:1, :ff] = up_bias[last : last + 1].astype(F32)
    BS[8:10, :n_head] = in_bias[last].astype(F32)
    swap(BIASES, BS, BY).start()
    diagonal = lax.broadcasted_iota(jnp.int32, (n_head, n_head), 0) == lax.broadcasted_iota(
        jnp.int32, (n_head, n_head), 1
    )

    def columns(out, two_rows):
        for c, at in ((0, 0), (1, 2 * n_head)):
            spread = jnp.where(diagonal, two_rows[c : c + 1], 0.0)
            out[at : at + n_head] = jnp.sum(spread, axis=1, keepdims=True)
        out[n_head : 2 * n_head] = jnp.zeros((n_head, 1), F32)

    for l in range(layers):
        vec[l, 0:2] = branch_bias[l].astype(F32)
        vec[l, 2:4] = norm_gain[l].astype(F32)
        vec[l, 4:6] = norm_shift[l].astype(F32)
        bup[l, 0:1] = up_bias[l : l + 1].astype(F32)
        columns(bcol.at[l], in_bias[l].astype(F32))
    for r in range(rows):
        for ref, shape, axis in ((segc, (seq, 1), 0), (segr, (1, seq), 1)):
            index = lax.broadcasted_iota(jnp.int32, shape, axis)
            position = (index // block % 2 * 2 + index // half_seq) * block + index % block
            text, end = jnp.zeros(shape, jnp.int32), 0
            for j in range(lengths.shape[1]):
                end = end + lengths[r, j]
                text = text + jnp.where(position >= end, 1, 0)
            ref[r] = jnp.where(position >= seq - padding[r], lengths.shape[1], text)
    first, second = cot[:, 0, :].astype(F32), cot[:, 1, :].astype(F32)
    CB[0] = jnp.where(own == 0, second, first).astype(BF)
    CB[2] = jnp.where(own == 0, first, second).astype(BF)
    for copy in weight_copies:
        copy.wait()

    def attention_product(l, r, slot, start):
        partial(slot, ((CT.at[l, r], WO.at[l]),), start)

    def forward_layer(l):
        group, buf = (INPUT if l == 0 else LAYER_IN), XG.at[l]
        if l == 0:
            weights_0(0)
            gather_pass(group, buf, 0)
            gather_copy(group, buf, 1, ACROSS).wait_recv()
            other_ready(group, buf, 0)
        else:
            for k in range(2):
                gather_pass(group, buf, k)
            own_ready(group, buf)
            for k in range(2):
                other_ready(group, buf, k)
        attention_forward(l, other)
        attention_product(l, other, 0, far_start)
        if l == 0:
            gather_pass(group, buf, 1)
        for k in range(2):
            sum_pass(k)
        if l == 0:
            weights_1(0)
            weights_0(1)
            gather_copy(group, buf, 0, ACROSS).wait_recv()
            other_ready(group, buf, 1)
            for k in range(2):
                XRES[k] = XG[0, piece(own, core, k)].astype(F32)
        attention_forward(l, own)
        attention_product(l, own, 1, near_start)
        if l == 0:
            weights_2(0)
        gather_sent(group, buf)
        for k in range(2):
            first_norm(l, k, sum_end(k), USUAL)
        if l == 0:
            weights_3(0)
        buf = HG.at[l]
        own_ready(USUAL, buf)
        ff_forward_own(l)
        PART[1] = dot(G[l, rows_of(own, 0, seq)], WD[l], NN).astype(BF)
        for k in range(2):
            near_start(k)
        if l == 0:
            weights_1(1)
            weights_4(0)
        gather_pass(USUAL, buf, 0)
        other_ready(USUAL, buf, 0)
        ff_forward_other(l, 0)
        far_start(0)
        gather_pass(USUAL, buf, 1)
        sum_pass(0)
        other_ready(USUAL, buf, 1)
        ff_forward_other(l, 1)
        far_start(1)
        if l == 0:
            weights_2(1)
        sum_pass(1)
        gather_sent(USUAL, buf)
        for k in range(2):
            XG[l + 1, piece(own, core, k)] = second_norm(l, k, sum_end(k))
            gather_start(LAYER_IN, XG.at[l + 1], k)

    def forward_last():
        l = last
        swap(UPSTREAM, CB.at[0], CB.at[1]).start()
        weights_3(1)
        own_ready(LAYER_IN, XG.at[l])
        attention_forward(l, own)
        weights_5(0)
        swap(BIASES, BS, BY).wait()
        columns(bcol_y, BY[8:10, :n_head])
        neighbour_attention_forward()
        both = ((CT.at[l, own], WO.at[l]), (DCT, GR.at[n_qkv : n_qkv + n_head]))
        partial(1, both, near_start)
        weights_4(1)
        for k in range(2):
            gather_pass(LAYER_IN, XG.at[l], k)
        for k in range(2):
            first_norm(l, k, pair_end(k), FF_IN)
        up_y = n_qkv + n_head
        down_y = up_y + width

        def ff_own_units(c):
            at = rows_of(own, c * half_seq, half_seq)
            G[l, at], DG[l, at] = ff_active(HG[l, at], WU[l], bup[l, 0:1])

        def ff_product(c):
            at = rows_of(own, c * half_seq, half_seq)
            active, _ = ff_active(HG[l, at], GR[up_y:down_y], BY[0:1, :ff])
            product = dot(G[l, at], WD[l], NN) + dot(active, GR[down_y : down_y + ff], NN)
            PART[1, pl.ds(aligned(c * half_seq), half_seq)] = product.astype(BF)

        ff_own_units(core)
        own_ready(FF_IN, HG.at[l])
        ff_own_units(1 - core)
        weights_5(1)
        ff_product(1 - core)
        for k in range(2):
            near_start(k)
        ff_product(core)
        swap(UPSTREAM, CB.at[0], CB.at[1]).wait()
        for k in range(2):
            YB[k] = second_norm(l, k, pair_end(k))
            block_of = jnp.where(own == k, CB[2].astype(F32), CB[1].astype(F32))
            second_norm_backward(l, k, block_of)
        swap(HIDDEN, YB.at[other], YB.at[2]).start()

    for l in range(last):
        forward_layer(l)
    forward_last()

    def backward(i, carry):
        l = last - i
        base = i * per_layer

        def place(e):
            for k in range(before[e], before[e + 1]):
                tick(i * per_units + k)

        place(0)
        own_ready(USUAL, DF)
        ff_backward_own(l)
        for k in range(2):
            near_start(k)
        place(1)

        @pl.when(l == last)
        def _():
            for k in range(2):
                other_ready(LAYER_IN, XG.at[last], k)
            gather_sent(LAYER_IN, XG.at[last])
            attention_forward(last, other)
            for k in range(2):
                gather_pass(FF_IN, HG.at[last], k)
            for k in range(2):
                other_ready(FF_IN, HG.at[last], k)
                ff_forward_other(last, k, product=False)
            gather_sent(FF_IN, HG.at[last])

        gather_pass(USUAL, DF, 0)
        place(2)
        other_ready(USUAL, DF, 0)
        ff_backward(l, pieces_of(other, 0), 0, part_pieces(0))
        far_start(0)
        gather_pass(USUAL, DF, 1)
        sum_pass(0)
        place(3)
        other_ready(USUAL, DF, 1)
        tokens_product(G.at[l], DF, base, 0, 1)
        place(4)
        tokens_product(G.at[l], DF, base, 1, ff // 256)
        ff_backward(l, pieces_of(other, 1), 0, part_pieces(1))
        far_start(1)
        place(5)
        sum_pass(1)
        tokens_product(HG.at[l], DU, base + ff, 0, width // 256)
        place(6)
        gather_sent(USUAL, DF)
        first_norm_backward(l, 0)
        place(7)
        first_norm_backward(l, 1)
        place(8)
        buf = DG.at[l]
        own_ready(USUAL, buf)
        attention_backward(l, own, 1, near_start)
        place(9)
        gather_pass(USUAL, buf, 0)
        place(10)
        gather_pass(USUAL, buf, 1)
        place(11)
        for k in range(2):
            other_ready(USUAL, buf, k)
        attention_backward(l, other, 0, far_start)
        place(12)
        for k in range(2):
            sum_pass(k)
        attention_gradients(l, base + 2 * ff)
        place(13)
        gather_sent(USUAL, buf)
        for k in range(2):
            DY[k] = DY[k] + sum_end(k)

            @pl.when(l > 0)
            def _(k=k):
                second_norm_backward(l - 1, k, DY[k])

            if k == 0:
                place(14)

        return carry

    lax.fori_loop(0, layers, backward, 0)
    swap(GRADIENT, DY.at[other], DH.at[0]).start()
    swap(HIDDEN, YB.at[other], YB.at[2]).wait()
    mine, theirs = YB[own].astype(F32), YB[2].astype(F32)
    for r in range(rows):
        hidden_out[:, r, :] = jnp.where(own == r, mine, theirs).astype(BF)

    def vector_copy(k):
        return remote(VB.at[0], RV.at[k], v_s.at[k], v_r.at[k], (net.core, net.y)[k])

    now = layers * per_units
    for k in range(2):
        vector_copy(k).start()
        lax.fori_loop(now, now + lag // 2, tick, 0)
        now += lag // 2
        vector_copy(k).wait()
        VB[0] += RV[k]
    base = layers * per_layer
    GR[base : base + UNIT] = jnp.zeros((UNIT, width), BF)
    GR[base : base + 16 * layers] = VB[...].reshape(16 * layers, width).astype(BF)
    lax.fori_loop(now, lag + units + 1 + SPACING * depth, tick, 0)
    small[...] = GR[base : base + 16 * layers].astype(F32)
    swap(GRADIENT, DY.at[other], DH.at[0]).wait()
    for r in range(rows):
        grad_hidden[:, r, :] = jnp.where(own == r, DY[own], DH[0])
    for i in range(layers):
        for k in range(len(sections)):
            out_copy(i, k).wait()


def local(
    hidden_in,
    cotangent,
    doc_lengths,
    pad_count,
    input_weight,
    input_bias,
    output_weight,
    up_weight,
    up_bias,
    down_weight,
    branch_bias,
    norm_gain,
    norm_shift,
):
    n_dp = lax.axis_size("dp")
    block, rows, width = hidden_in.shape
    seq = block * lax.axis_size("tensor")
    layers, _, _, n_head = input_weight.shape
    n_qkv, heads, ff = 3 * n_head, n_head // HEAD_DIM, up_weight.shape[2]
    tokens = rows * seq
    wt = jnp.swapaxes(input_weight, 2, 3).reshape(layers, n_qkv, width)
    per_layer = 2 * ff + n_qkv + n_head
    part = UNIT // 2
    outer = 0
    while 8 << outer < n_dp:
        outer += 1
    depth = 5 + outer
    vmem = pltpu.VMEM
    dma = pltpu.SemaphoreType.DMA
    scratch = [
        vmem((layers, n_qkv, width), BF),
        vmem((layers, n_head, width), BF),
        vmem((layers, width, ff), BF),
        vmem((layers, ff, width), BF),
        vmem((layers, tokens, width), BF),
        vmem((layers, tokens, width), BF),
        vmem((layers, tokens, ff), BF),
        vmem((layers, tokens, ff), BF),
        vmem((tokens, width), BF),
        vmem((tokens, ff), BF),
        vmem((layers, rows, n_qkv, seq), BF),
        vmem((layers, rows, heads, seq, seq), BF),
        vmem((layers, rows, n_head, seq), BF),
        vmem((rows, n_qkv, seq), BF),
        vmem((seq, seq), BF),
        vmem((n_head, seq), BF),
        vmem((rows, seq, width), BF),
        vmem((rows, 3, block, width), BF),
        vmem((rows, block, width), F32),
        vmem((rows, block, width), F32),
        vmem((layers, 2, rows, block, width), BF),
        vmem((layers, 2, rows, block, 1), F32),
        vmem((layers * per_layer + UNIT, width), BF),
        vmem((SLOTS, part // 2, width), BF),
        vmem((SLOTS, part // 2, width), BF),
        vmem((SLOTS, part // 2, width), BF),
        vmem((SLOTS, part, width), BF),
        vmem((SLOTS, part // 2, width), BF),
        vmem((SLOTS, part // 2, width), BF),
        vmem((max(outer, 1), SLOTS if outer else 1, part // 2, width), BF),
        vmem((max(outer, 1), SLOTS if outer else 1, part // 2, width), BF),
        vmem((SPACING, part // 2, width), BF),
        vmem((SPACING, part // 2, width), BF),
        vmem((SPACING, part, width), BF),
        vmem((SPACING, part // 2, width), BF),
        vmem((2, layers, 8, width), F32),
        vmem((2, layers, 8, width), F32),
        vmem((rows, seq, 1), jnp.int32),
        vmem((rows, 1, seq), jnp.int32),
        vmem((layers, n_qkv, 1), F32),
        vmem((n_qkv, 1), F32),
        vmem((layers, 8, ff), F32),
        vmem((layers, 8, width), F32),
        vmem((16, max(ff, n_head)), F32),
        vmem((16, max(ff, n_head)), F32),
        vmem((3, block, width), BF),
        vmem((3, block, width), BF),
        dma((4,)),
        dma((4, 2, 3)),
        dma((4, 2, 3)),
        dma((2, 3)),
        dma((2, 3)),
        dma((layers * per_layer // UNIT + 1, depth)),
        dma((layers * per_layer // UNIT + 1, depth)),
        dma((layers * per_layer // UNIT + 1, depth)),
        dma((layers * per_layer // UNIT + 1, depth)),
        dma((2,)),
        dma((2,)),
        dma((layers, 4)),
        pltpu.SemaphoreType.REGULAR,
        pltpu.SemaphoreType.REGULAR,
        dma((2, 10)),
        dma((2, 10)),
        dma((4,)),
        dma((4,)),
    ]
    whole, anywhere = pl.BlockSpec(memory_space=vmem), pl.BlockSpec(memory_space=pl.ANY)
    scalars = pl.BlockSpec(memory_space=pltpu.SMEM)
    results = pl.pallas_call(
        functools.partial(kernel, n_dp, layers),
        out_shape=(
            jax.ShapeDtypeStruct(hidden_in.shape, BF),
            jax.ShapeDtypeStruct(hidden_in.shape, F32),
            jax.ShapeDtypeStruct((layers, n_qkv, width), BF),
            jax.ShapeDtypeStruct(output_weight.shape, BF),
            jax.ShapeDtypeStruct(up_weight.shape, BF),
            jax.ShapeDtypeStruct(down_weight.shape, BF),
            jax.ShapeDtypeStruct((16 * layers, width), F32),
        ),
        in_specs=[whole, whole, scalars, scalars, anywhere, whole, anywhere, anywhere, whole, anywhere]
        + [whole] * 3,
        out_specs=(whole, whole, anywhere, anywhere, anywhere, anywhere, whole),
        scratch_shapes=scratch,
        compiler_params=pltpu.CompilerParams(
            collective_id=0, has_side_effects=True, vmem_limit_bytes=63 << 20
        ),
    )(
        hidden_in,
        cotangent,
        doc_lengths,
        pad_count,
        wt,
        input_bias,
        output_weight,
        up_weight,
        up_bias,
        down_weight,
        branch_bias,
        norm_gain,
        norm_shift,
    )
    pieces = 2

    def strip(array):
        return pl.BlockSpec((1, array.shape[1] // pieces, width), lambda l, c: (l, c, 0))

    strips = [strip(array) for array in results[2:6]]
    fixed = [
        jax.ShapeDtypeStruct(shape, F32)
        for shape in (input_bias.shape, up_bias.shape, branch_bias.shape, norm_gain.shape, norm_shift.shape)
    ]
    hidden_out, grad_hidden, grad_in, grad_out, grad_up, grad_down, *vectors = pl.pallas_call(
        functools.partial(finish, layers, pieces),
        grid=(layers, pieces),
        out_shape=[jax.ShapeDtypeStruct(array.shape, array.dtype) for array in results[:2]]
        + [jax.ShapeDtypeStruct(array.shape, F32) for array in results[2:6]]
        + fixed,
        in_specs=[whole] * 2 + strips + [whole],
        out_specs=[whole] * 2 + strips + [whole] * 5,
        compiler_params=pltpu.CompilerParams(vmem_limit_bytes=20 << 20),
    )(*results)
    grad_in_bias, grad_up_bias, grad_branch, grad_gain, grad_shift = vectors
    grad_in = jnp.swapaxes(grad_in.reshape(layers, 3, n_head, width), 2, 3)
    return (
        hidden_out,
        grad_hidden,
        grad_in,
        grad_in_bias,
        grad_out,
        grad_up,
        grad_up_bias,
        grad_down,
        grad_branch,
        grad_gain,
        grad_shift,
    )


def finish(layers, pieces, *refs):
    hidden, grad_hidden, *grads = refs[:6]
    small = refs[6]
    hidden_out, grad_hidden_out, *outs = refs[7:13]
    grad_in_bias, grad_up_bias, grad_branch, grad_gain, grad_shift = refs[13:18]
    step = pl.program_id(0) * pieces + pl.program_id(1)

    @pl.when(step == 0)
    def _():
        hidden_out[...] = hidden[...]
        grad_hidden_out[...] = grad_hidden[...]
        n_head, ff = grad_in_bias.shape[2], grad_up_bias.shape[1]
        for l in range(layers):
            shared, split = 8 * l, 8 * (layers + l)
            grad_branch[l] = small[shared : shared + 2]
            grad_gain[l] = small[shared + 2 : shared + 4]
            grad_shift[l] = small[shared + 4 : shared + 6]
            grad_up_bias[l : l + 1] = small[split : split + 1, :ff]
            for c in range(2):
                grad_in_bias[l, c : c + 1] = small[split + 1 : split + 2, 2 * c * n_head : (2 * c + 1) * n_head]

    for grad, out in zip(grads, outs, strict=True):
        out[...] = grad[...].astype(F32)


def solution(mesh):
    return jax.shard_map(
        local,
        mesh=mesh,
        in_specs=(
            P("tensor", "dp", None),
            P("tensor", "dp", None),
            P("dp", None),
            P("dp"),
            P(None, None, None, "tensor"),
            P(None, None, "tensor"),
            P(None, "tensor", None),
            P(None, None, "tensor"),
            P(None, "tensor"),
            P(None, "tensor", None),
            P(),
            P(),
            P(),
        ),
        out_specs=(
            P("tensor", "dp", None),
            P("tensor", "dp", None),
            P(None, None, None, "tensor"),
            P(None, None, "tensor"),
            P(None, "tensor", None),
            P(None, None, "tensor"),
            P(None, "tensor"),
            P(None, "tensor", None),
            P(),
            P(),
            P(),
        ),
        check_vma=False,
    )
```
